128 devices in a mesh: gx: 8 (over y, core), gy: 16 (over x, z).
Axes of the slice: x: 4, y: 4, z: 4, core: 2. Of those that a mesh axis runs over, the one named last changes fastest.
Arguments:
- pressure: float32 [10, 256, 2048], P(None, 'gx', 'gy'), may hold values from -2 to -0.1
- soil: int32 [10, 256, 2048], P(None, 'gx', 'gy'), may hold values from 0 to 22
- vg_alpha: float32 [23], replicated, may hold values from 0.5 to 2.5
- vg_n: float32 [23], replicated, may hold values from 1.4 to 2.6
- sat_cond: float32 [23], replicated, may hold values from 0.2 to 5
- storage: float32 [10, 256, 2048], P(None, 'gx', 'gy'), may hold values from 0.02 to 0.2
- right_side: float32 [10, 256, 2048], P(None, 'gx', 'gy'), may hold values from -30 to 30
Outputs:
- solution: float32 [10, 256, 2048], P(None, 'gx', 'gy')
- new_residual: float32 [10, 256, 2048], P(None, 'gx', 'gy')
- residual_norm: float32 [1], replicated
The draws below stay inside these ranges and needn't reach their ends.
All inputs are finite; a program needn't handle non-finite values.
Results may differ from the reference program's by a relative error of at most 0.009.
Values sent between devices are 32-bit elements; how exact they have to be, the bound alone decides.
No kernel may reach another device: no remote copies, remote signals or barrier semaphores. Data moves between devices by JAX's collectives and lax.ppermute only.
A program may use at most 192 MiB of HBM per device.

```python
import math
import jax
import jax.numpy as jnp
from jax import lax

NZ = 10
NSOIL = 23
LEVELS = 4
COARSE_PAIRS = 3
NX = 256
NY = 2048


def draw_right_side(key, part):
    key = jax.random.fold_in(key, 11)
    along_x = jnp.arange(NX, dtype=jnp.float32) / NX
    along_y = jnp.arange(NY, dtype=jnp.float32) / NY
    rising = jnp.exp(math.log(3.0) * along_x)[None, :, None] * jnp.exp(math.log(2.0) * along_y)[None, None, :]
    rough = jnp.clip(jax.random.normal(key, (NZ, NX, NY), jnp.float32), -5.0, 5.0)
    return (rising * rough).astype(jnp.float32)


def place_ends(array, rng, least, largest):
    shape = array.shape
    spot = [jax.random.randint(jax.random.fold_in(rng, axis), (), 0, shape[axis]) for axis in range(len(shape))]
    array = array.at[tuple(spot)].set(least)
    longest = shape.index(max(shape))
    spot[longest] = (spot[longest] + 1) % shape[longest]
    return array.at[tuple(spot)].set(largest)


def block_scale(stream_key, dims, shards, smallest, top_value):
    gain = 1.0
    for dim, shards_of in shards:
        steps = jax.random.uniform(jax.random.fold_in(jax.random.fold_in(stream_key, 6), dim), (shards_of,), jnp.float32, smallest / len(shards), top_value / len(shards))
        gain = gain * jnp.repeat(jnp.exp(steps), dims[dim] // shards_of).reshape((-1,) + (1,) * (len(dims) - 1 - dim))
    return gain


def setup_inputs(seed: int = 0) -> dict:
    seeds = jax.random.split(jax.random.key(seed), 8)
    pressure = jnp.clip(-2.0 + 1.9 * jax.random.uniform(seeds[0], (NZ, NX, NY), jnp.float32) ** block_scale(seeds[0], (NZ, NX, NY), ((1, 8), (2, 16)), -0.2, 0.2), -2.0, -0.1)
    soil = place_ends(jax.random.randint(seeds[1], (NZ, NX, NY), 0, NSOIL), jax.random.fold_in(seeds[1], 1), 0, NSOIL - 1).astype(jnp.int32)
    vg_alpha = jnp.clip(jnp.exp(jax.random.uniform(seeds[2], (NSOIL,), jnp.float32, math.log(0.5), math.log(2.5))), 0.5, 2.5)
    vg_n = jnp.clip(jax.random.uniform(seeds[3], (NSOIL,), jnp.float32, 1.4, 2.6), 1.4, 2.6)
    sat_cond = jnp.clip(jnp.exp(jax.random.uniform(seeds[4], (NSOIL,), jnp.float32, math.log(0.2), math.log(5.0))), 0.2, 5.0)
    storage = jnp.clip(jnp.exp(math.log(0.2) - 2.3025851 * jax.random.uniform(seeds[5], (NZ, NX, NY), jnp.float32) ** block_scale(seeds[5], (NZ, NX, NY), ((1, 8), (2, 16)), -0.2, 0.2)), 0.02, 0.2)
    right_side = draw_right_side(jax.random.fold_in(seeds[7], 71), 0)
    return {"pressure": pressure, "soil": soil, "vg_alpha": vg_alpha, "vg_n": vg_n, "sat_cond": sat_cond, "storage": storage, "right_side": right_side}


WEIGHT_Z = 2.0

def soil_values(soil, vg_alpha, vg_n, sat_cond):
    entry_scale = jnp.zeros(soil.shape, jnp.float32)
    pore_index = jnp.zeros(soil.shape, jnp.float32)
    saturated = jnp.zeros(soil.shape, jnp.float32)
    for soil_kind in range(NSOIL):
        matched = soil == soil_kind
        entry_scale = jnp.where(matched, vg_alpha[soil_kind], entry_scale)
        pore_index = jnp.where(matched, vg_n[soil_kind], pore_index)
        saturated = jnp.where(matched, sat_cond[soil_kind], saturated)
    return (entry_scale, pore_index, saturated)

def conductivity(pressure, soil, vg_alpha, vg_n, sat_cond):
    entry_scale, pore_index, saturated = soil_values(soil, vg_alpha, vg_n, sat_cond)
    exponent = 1.0 - 1.0 / pore_index
    scaled_head = jnp.power(entry_scale * jnp.abs(pressure), pore_index)
    rooted = jnp.exp(-0.5 * exponent * jnp.log1p(scaled_head))
    outer_term = -jnp.expm1(-exponent * jnp.log1p(1.0 / scaled_head))
    return saturated * rooted * outer_term * outer_term

def fine_coeffs(cond, storage):
    layers, rows_x, rows_y = cond.shape
    face_x = 0.5 * (cond[:, :-1, :] + cond[:, 1:, :])
    edge_x = jnp.zeros((layers, 1, rows_y), jnp.float32)
    face_y = 0.5 * (cond[:, :, :-1] + cond[:, :, 1:])
    edge_y = jnp.zeros((layers, rows_x, 1), jnp.float32)
    face_z = WEIGHT_Z * (0.5 * (cond[:-1] + cond[1:]))
    edge_z = jnp.zeros((1, rows_x, rows_y), jnp.float32)
    return (storage, jnp.concatenate([face_x, edge_x], axis=1), jnp.concatenate([edge_x, face_x], axis=1), jnp.concatenate([face_y, edge_y], axis=2), jnp.concatenate([edge_y, face_y], axis=2), jnp.concatenate([face_z, edge_z], axis=0), jnp.concatenate([edge_z, face_z], axis=0))

def pad_zero(field):
    return jnp.pad(field, ((0, 0), (1, 1), (1, 1)))

def beside_sum(padded, coeffs):
    centre = padded[:, 1:-1, 1:-1]
    vertical = jnp.pad(centre, ((1, 1), (0, 0), (0, 0)))
    return coeffs[1] * padded[:, 2:, 1:-1] + coeffs[2] * padded[:, :-2, 1:-1] + coeffs[3] * padded[:, 1:-1, 2:] + coeffs[4] * padded[:, 1:-1, :-2] + coeffs[5] * vertical[2:] + coeffs[6] * vertical[:-2]

def diagonal_of(coeffs):
    return coeffs[0] + coeffs[1] + coeffs[2] + coeffs[3] + coeffs[4] + coeffs[5] + coeffs[6]

def colours(shape, start_x, start_y):
    layer_ids = lax.broadcasted_iota(jnp.int32, shape, 0)
    row_ids = lax.broadcasted_iota(jnp.int32, shape, 1) + start_x
    column_ids = lax.broadcasted_iota(jnp.int32, shape, 2) + start_y
    return (layer_ids + row_ids + column_ids) % 2

def half_sweep(field, source, coeffs, diagonal, colour, wanted, pad_fn):
    beside = beside_sum(pad_fn(field), coeffs)
    return jnp.where(colour == wanted, (source + beside) / diagonal, field)

def apply_operator(field, coeffs, diagonal, pad_fn):
    return diagonal * field - beside_sum(pad_fn(field), coeffs)

def block_sum(field):
    layers, rows_x, rows_y = field.shape
    return field.reshape(layers, rows_x // 2, 2, rows_y // 2, 2).sum(axis=(2, 4))

def prolong(field):
    return jnp.repeat(jnp.repeat(field, 2, axis=1), 2, axis=2)

def coarsen(coeffs):
    storage, east, west, north, south, upward, downward = coeffs
    layers, rows_x, rows_y = east.shape
    coarse_east = east[:, 1::2, :].reshape(layers, rows_x // 2, rows_y // 2, 2).sum(axis=3)
    coarse_west = west[:, 0::2, :].reshape(layers, rows_x // 2, rows_y // 2, 2).sum(axis=3)
    coarse_north = north[:, :, 1::2].reshape(layers, rows_x // 2, 2, rows_y // 2).sum(axis=2)
    coarse_south = south[:, :, 0::2].reshape(layers, rows_x // 2, 2, rows_y // 2).sum(axis=2)
    return (block_sum(storage), coarse_east, coarse_west, coarse_north, coarse_south, block_sum(upward), block_sum(downward))

def descend(source, coeffs, diagonal, colour, pad_fn):
    field = jnp.zeros_like(source)
    field = half_sweep(field, source, coeffs, diagonal, colour, 0, pad_fn)
    field = half_sweep(field, source, coeffs, diagonal, colour, 1, pad_fn)
    residual = source - apply_operator(field, coeffs, diagonal, pad_fn)
    return (field, block_sum(residual))

def ascend(field, correction, source, coeffs, diagonal, colour, pad_fn):
    field = field + prolong(correction)
    field = half_sweep(field, source, coeffs, diagonal, colour, 1, pad_fn)
    field = half_sweep(field, source, coeffs, diagonal, colour, 0, pad_fn)
    return field

def coarsest(source, coeffs, diagonal, colour):
    level_mean = jnp.sum(source) / jnp.sum(coeffs[0])
    field = jnp.zeros_like(source) + level_mean
    for sweep_pair in range(COARSE_PAIRS):
        for wanted in (0, 1, 1, 0):
            field = half_sweep(field, source, coeffs, diagonal, colour, wanted, pad_zero)
    return field

def cycle_whole(source, coeffs, level_index):
    diagonal = diagonal_of(coeffs)
    colour = colours(source.shape, 0, 0)
    if level_index == LEVELS - 1:
        return coarsest(source, coeffs, diagonal, colour)
    field, coarse_source = descend(source, coeffs, diagonal, colour, pad_zero)
    correction = cycle_whole(coarse_source, coarsen(coeffs), level_index + 1)
    return ascend(field, correction, source, coeffs, diagonal, colour, pad_zero)

def reference(pressure, soil, vg_alpha, vg_n, sat_cond, storage, right_side):
    cond = conductivity(pressure, soil, vg_alpha, vg_n, sat_cond)
    coeffs = fine_coeffs(cond, storage)
    precond = cycle_whole(right_side, coeffs, 0)
    diagonal = diagonal_of(coeffs)
    residual_precond = jnp.sum(right_side * precond)
    image = apply_operator(precond, coeffs, diagonal, pad_zero)
    curvature = jnp.sum(precond * image)
    step_length = residual_precond / curvature
    solution = step_length * precond
    new_residual = right_side - step_length * image
    residual_norm = jnp.sqrt(jnp.sum(new_residual * new_residual) / (NZ * NX * NY)).reshape(1)
    return (solution, new_residual, residual_norm)
```

```python
import functools

import jax
import jax.numpy as jnp
from jax import lax
from jax.experimental import pallas as pl
from jax.experimental.pallas import tpu as pltpu
from jax.sharding import PartitionSpec as P

NSOIL = 23
PAIRS = 5
HALO = 24
ROWS, LANES = 32, 128
EXT = ROWS + 2 * HALO
WIDE = 2 * LANES
ROWS1, ROWS2 = 48, 24
TILES = 11
MIB = 1 << 20


def iota(shape, dim):
    return lax.broadcasted_iota(jnp.int32, shape, dim)


def odd_cells(shape, level, start=0):
    return ((iota(shape, 0) + start + (iota(shape, 1) >> level)) & 1) == 1


def lane_bit(shape, level):
    return ((iota(shape, 1) >> level) & 1) == 1


def row_next(x):
    return pltpu.roll(x, x.shape[0] - 1, 0)


def row_prev(x):
    return pltpu.roll(x, 1, 0)


def lane_next(x, step):
    return pltpu.roll(x, x.shape[1] - step, 1)


def lane_prev(x, step):
    return pltpu.roll(x, step, 1)


def pair_sum(x, level):
    step = 1 << level
    return x + jnp.where(lane_bit(x.shape, level), lane_prev(x, step), lane_next(x, step))


def beside(c, u, coeffs, m, odd, step):
    east, north, inner, outer = coeffs
    um = u[m]
    t = east[c, m] * row_next(um) + row_prev(east[1 - c, m] * um)
    t = t + (north[c, m] * lane_next(um, step) + lane_prev(north[1 - c, m] * um, step))
    t = t + inner[m] * um
    above = outer[m] * u[m + 1] if m < PAIRS - 1 else 0.0
    below = outer[m - 1] * u[m - 1] if m > 0 else 0.0
    return t + (jnp.where(odd, above, below) if c == 0 else jnp.where(odd, below, above))


def params(limit=32):
    return pltpu.CompilerParams(vmem_limit_bytes=limit * MIB)


VM = pl.BlockSpec(memory_space=pltpu.VMEM)
SM = pl.BlockSpec(memory_space=pltpu.SMEM)


def shape(*dims):
    return jax.ShapeDtypeStruct(dims, jnp.float32)


class Wide:
    def __init__(self, ref):
        self.ref, self.lead = ref, len(ref.shape) - 3

    def parts(self, ids):
        ids = ids if isinstance(ids, tuple) else (ids,)
        rows = ids[self.lead] if len(ids) > self.lead else slice(None)
        return [self.ref.at[(*ids[: self.lead], half)] for half in range(2)], rows

    def __getitem__(self, ids):
        refs, rows = self.parts(ids)
        return jnp.concatenate([ref[rows, :] for ref in refs], axis=1)

    def __setitem__(self, ids, x):
        refs, rows = self.parts(ids)
        for half, ref in enumerate(refs):
            ref[rows, :] = x[:, LANES * half : LANES * (half + 1)]


def first_kernel(place, pressure, soil, table, storage, source, packed, to_sibling, to_other):
    even = (place[0] & 1) == 0
    odd = odd_cells((ROWS, LANES), 0)
    rows = [jnp.broadcast_to(table[q : q + 1, :], (8, LANES)) for q in range(3)]

    def look_up(row, ids):
        parts = [jnp.take_along_axis(row, ids[8 * b : 8 * b + 8], axis=1) for b in range(ROWS // 8)]
        return jnp.concatenate(parts, axis=0)

    def cond_of(k):
        ids = soil[k]
        log_scale, power, saturated = [look_up(r, ids) for r in rows]
        exponent = 1.0 - 1.0 / power
        log_s = power * (log_scale + jnp.log(jnp.abs(pressure[k])))
        log_1s = jnp.log(1.0 + jnp.exp(log_s))
        outer = 1.0 - jnp.exp(exponent * (log_s - log_1s))
        return saturated * jnp.exp(-0.5 * exponent * log_1s) * outer * outer

    def put(t, x):
        packed[t] = x
        high, low = x[ROWS - HALO :], x[:HALO]
        to_sibling[t] = jnp.where(even, high, low)
        to_other[t] = jnp.where(even, low, high)

    for m in range(PAIRS):
        triples = (
            (cond_of(2 * m), cond_of(2 * m + 1)),
            (storage[2 * m], storage[2 * m + 1]),
            (source[2 * m], source[2 * m + 1]),
        )
        for q, (a, b) in enumerate(triples):
            put(q * 10 + m, jnp.where(odd, b, a))
            put(q * 10 + PAIRS + m, jnp.where(odd, a, b))


def second_kernel(place, packed, from_sibling, from_other, to_pair, to_next):
    even_x = (place[0] & 1) == 0
    even_y = (place[1] & 1) == 0
    lane = iota((EXT, LANES), 1)
    for tile in range(6):
        pair, other = None, None
        for m in range(PAIRS):
            t = tile * PAIRS + m
            sib, oth = from_sibling[t], from_other[t]
            x = jnp.concatenate([jnp.where(even_x, oth, sib), packed[t], jnp.where(even_x, sib, oth)], axis=0)
            left = pltpu.roll(x, HALO * m, 1) if m else x
            right = pltpu.roll(x, (HALO * m - (LANES - HALO)) % LANES, 1)
            a, b = jnp.where(even_y, right, left), jnp.where(even_y, left, right)
            pair = a if pair is None else jnp.where(lane >= HALO * m, a, pair)
            other = b if other is None else jnp.where(lane >= HALO * m, b, other)
        to_pair[tile] = pair
        to_next[tile] = other


def coarsen_level(level, fine_rows, out_rows, fine, coarse):
    stor, east, north, inner, outer = fine
    cstor, ceast, cnorth, cinner, couter = coarse
    half = fine_rows // 2
    dims = (half, WIDE)
    bit = lane_bit(dims, level)
    odd = odd_cells(dims, level + 1, 1 if level == 2 else 0)
    step = 1 << level

    def even_rows(ref, *ids):
        return ref[(*ids, pl.ds(0, half, stride=2))]

    def odd_rows(ref, *ids):
        return ref[(*ids, pl.ds(1, half, stride=2))]

    def put(ref, m, low, high):
        ref[0, m, slice(0, half)] = jnp.where(odd, high, low)
        ref[1, m, slice(0, half)] = jnp.where(odd, low, high)

    for m in range(PAIRS):
        u = even_rows(stor, 0, m) + odd_rows(stor, 1, m)
        v = even_rows(stor, 1, m) + odd_rows(stor, 0, m)
        put(cstor, m, pair_sum(jnp.where(bit, v, u), level), pair_sum(jnp.where(bit, u, v), level))
        e0, e1 = odd_rows(east, 0, m), odd_rows(east, 1, m)
        put(ceast, m, pair_sum(jnp.where(bit, e0, e1), level), pair_sum(jnp.where(bit, e1, e0), level))
        low = even_rows(north, 1, m) + odd_rows(north, 0, m)
        high = even_rows(north, 0, m) + odd_rows(north, 1, m)
        put(
            cnorth,
            m,
            jnp.where(bit, low, lane_next(low, step)),
            jnp.where(bit, high, lane_next(high, step)),
        )
        cinner[m, slice(0, half)] = pair_sum(even_rows(inner, m) + odd_rows(inner, m), level)
        if m < PAIRS - 1:
            couter[m, slice(0, half)] = pair_sum(even_rows(outer, m) + odd_rows(outer, m), level)


def restrict_level(level, fine_rows, residual, coarse_source):
    half = fine_rows // 2
    dims = (half, WIDE)
    bit = lane_bit(dims, level)
    odd = odd_cells(dims, level + 1, 1 if level == 2 else 0)
    for m in range(PAIRS):
        a = residual[m, pl.ds(0, half, stride=2)]
        b = residual[m, pl.ds(1, half, stride=2)]
        low = pair_sum(jnp.where(bit, b, a), level)
        high = pair_sum(jnp.where(bit, a, b), level)
        coarse_source[0, m, slice(0, half)] = jnp.where(odd, high, low)
        coarse_source[1, m, slice(0, half)] = jnp.where(odd, low, high)


def invert_diagonal(level, rows, coeffs, inverse):
    stor, east, north, inner, outer = coeffs
    odd = odd_cells((rows, WIDE), level)
    step = 1 << level
    for m in range(PAIRS):
        above = outer[m] if m < PAIRS - 1 else 0.0
        below = outer[m - 1] if m > 0 else 0.0
        for c in range(2):
            diag = stor[c, m] + east[c, m] + row_prev(east[1 - c, m]) + north[c, m]
            diag = diag + lane_prev(north[1 - c, m], step) + inner[m]
            diag = diag + (jnp.where(odd, above, below) if c == 0 else jnp.where(odd, below, above))
            inverse[c, m] = 1.0 / diag


def descend_level(level, rows, coeffs, inverse, source, first, second, residual):
    odd = odd_cells((rows, WIDE), level)
    step = 1 << level
    for m in range(PAIRS):
        first[m] = source[0, m] * inverse[0, m]
    for m in range(PAIRS):
        second[m] = (source[1, m] + beside(1, first, coeffs[1:], m, odd, step)) * inverse[1, m]
    for m in range(PAIRS):
        residual[m] = beside(0, second, coeffs[1:], m, odd, step)


def third_kernel(
    place, packed, from_sibling, from_other, from_pair, from_next,
    source0, inv0, first0, east0, north0, inner0, outer0,
    source1, inv1, first1, east1, north1, inner1, outer1,
    source2, inv2, first2, east2, north2, inner2, outer2,
    tiles, sums,
    cond, stor, src, east, north, inner, outer, inv, first, second, residual,
    stor1, src1, e1, n1, in1, out1, i1, f1, s1, r1,
    stor2, s2, r2,
    stor3, src3, e3, n3, in3, out3,
):
    source0, inv0, first0, east0, north0, inner0, outer0 = map(Wide, (source0, inv0, first0, east0, north0, inner0, outer0))
    source1, inv1, first1, east1, north1, inner1, outer1 = map(Wide, (source1, inv1, first1, east1, north1, inner1, outer1))
    source2, inv2, first2, east2, north2, inner2, outer2 = map(Wide, (source2, inv2, first2, east2, north2, inner2, outer2))
    cond, stor, src, east, north, inner, outer = map(Wide, (cond, stor, src, east, north, inner, outer))
    inv, first, second, residual = map(Wide, (inv, first, second, residual))
    stor1, src1, e1, n1, in1, out1, i1, f1, s1, r1 = map(Wide, (stor1, src1, e1, n1, in1, out1, i1, f1, s1, r1))
    stor2, s2, r2 = map(Wide, (stor2, s2, r2))
    stor3, src3, e3, n3, in3, out3 = map(Wide, (stor3, src3, e3, n3, in3, out3))
    even_x = (place[0] & 1) == 0
    even_y = (place[1] & 1) == 0
    lane = iota((EXT, LANES), 1)
    for tile in range(6):
        pair, other = from_pair[tile], from_next[tile]
        right = jnp.where(even_y, pair, other)
        left = jnp.where(even_y, other, pair)
        ref = (cond, stor, src)[tile // 2]
        for m in range(PAIRS):
            t = tile * PAIRS + m
            sib, oth = from_sibling[t], from_other[t]
            x = jnp.concatenate([jnp.where(even_x, oth, sib), packed[t], jnp.where(even_x, sib, oth)], axis=0)
            r = pltpu.roll(right, (-HALO * m) % LANES, 1) if m else right
            l = pltpu.roll(left, (LANES - HALO - HALO * m) % LANES, 1)
            h = jnp.where(lane < HALO, r, jnp.where(lane >= LANES - HALO, l, 0.0))
            if tile // 2 == 1:
                x, h = jnp.where(x == 0.0, 1.0, x), jnp.where(h == 0.0, 1.0, h)
            ref.ref[tile % 2, m, 0] = x
            ref.ref[tile % 2, m, 1] = h

    dims = (EXT, WIDE)
    odd = odd_cells(dims, 0)
    row, column = iota(dims, 0), iota(dims, 1)
    last_row = (row == HALO + ROWS - 1) & (place[0] == place[2] - 1)
    before_row = (row == HALO - 1) & (place[0] == 0)
    keep_x = jnp.where(last_row | before_row, 0.0, 0.5)
    last_column = (column == LANES - 1) & (place[1] == place[3] - 1)
    before_column = (column == WIDE - 1) & (place[1] == 0)
    keep_y = jnp.where(last_column | before_column, 0.0, 0.5)
    for m in range(PAIRS):
        a, b = cond[0, m], cond[1, m]
        east[0, m] = (a + row_next(b)) * keep_x
        east[1, m] = (b + row_next(a)) * keep_x
        north[0, m] = (a + lane_next(b, 1)) * keep_y
        north[1, m] = (b + lane_next(a, 1)) * keep_y
        inner[m] = a + b
        if m < PAIRS - 1:
            outer[m] = jnp.where(odd, a + cond[1, m + 1], b + cond[0, m + 1])

    level0 = (stor, east, north, inner, outer)
    level1 = (stor1, e1, n1, in1, out1)
    level2 = (stor2, east2, north2, inner2, outer2)
    level3 = (stor3, e3, n3, in3, out3)
    invert_diagonal(0, EXT, level0, inv)
    descend_level(0, EXT, level0, inv, src, first, second, residual)

    half = EXT // 2
    for ref in (src1, e1, n1, in1, out1):
        ref.ref[..., half:, :] = jnp.zeros((*ref.ref.shape[:-2], ROWS1 - half, LANES), jnp.float32)
    stor1.ref[..., half:, :] = jnp.ones((2, PAIRS, 2, ROWS1 - half, LANES), jnp.float32)
    coarsen_level(0, EXT, ROWS1, level0, level1)
    restrict_level(0, EXT, residual, src1)
    invert_diagonal(1, ROWS1, level1, i1)
    descend_level(1, ROWS1, level1, i1, src1, f1, s1, r1)

    coarsen_level(1, ROWS1, ROWS2, level1, level2)
    restrict_level(1, ROWS1, r1, source2)
    invert_diagonal(2, ROWS2, level2, inv2)
    descend_level(2, ROWS2, level2, inv2, source2, first2, s2, r2)

    coarsen_level(2, ROWS2, 16, level2, level3)
    restrict_level(2, ROWS2, r2, src3)

    dims3 = (16, WIDE)
    odd3 = odd_cells(dims3, 3, 1)
    phase = iota((4, LANES), 1) & 7
    total_f, total_s = 0.0, 0.0
    compact = [None] * TILES
    for m in range(PAIRS):
        above = out3[m] if m < PAIRS - 1 else 0.0
        below = out3[m - 1] if m > 0 else 0.0
        invs = []
        for c in range(2):
            diag = stor3[c, m] + e3[c, m] + row_prev(e3[1 - c, m]) + n3[c, m]
            diag = diag + lane_prev(n3[1 - c, m], 8) + in3[m]
            diag = diag + (jnp.where(odd3, above, below) if c == 0 else jnp.where(odd3, below, above))
            invs.append(1.0 / diag)
            total_f = total_f + src3[c, m][3:7, :LANES]
            total_s = total_s + stor3[c, m][3:7, :LANES]
        values = (
            src3[0, m] * invs[0], src3[1, m] * invs[1], 1.0 - stor3[0, m] * invs[0], invs[0], invs[1],
            e3[0, m], e3[1, m], n3[0, m], n3[1, m], in3[m], out3[m] if m < PAIRS - 1 else jnp.zeros(dims3, jnp.float32),
        )
        for q, value in enumerate(values):
            own = value[3:7, :LANES]
            compact[q] = jnp.where(phase == m, own, 0.0 if m == 0 else compact[q])
    for q in range(TILES):
        tiles[4 * q : 4 * q + 4] = compact[q]
    sums[0:1] = jnp.broadcast_to(jnp.sum(total_f, keepdims=True), (1, LANES)) * 0.125
    sums[1:2] = jnp.broadcast_to(jnp.sum(total_s, keepdims=True), (1, LANES)) * 0.125

    for m in range(PAIRS):
        for c in range(2):
            for to, of in ((source0, src), (inv0, inv), (east0, east), (north0, north)):
                to[c, m] = of[c, m, slice(16, 64)]
            for to, of in ((source1, src1), (inv1, i1), (east1, e1), (north1, n1)):
                to[c, m] = of[c, m, slice(8, 32)]
        first0[m], first1[m] = first[m, slice(16, 64)], f1[m, slice(8, 32)]
        inner0[m], inner1[m] = inner[m, slice(16, 64)], in1[m, slice(8, 32)]
        if m < PAIRS - 1:
            outer0[m], outer1[m] = outer[m, slice(16, 64)], out1[m, slice(8, 32)]


def spread_rows(level, low, high, into, m):
    rows = low.shape[0]
    bit = lane_bit(low.shape, level)
    into[m, pl.ds(0, rows, stride=2)] = jnp.where(bit, high, low)
    into[m, pl.ds(1, rows, stride=2)] = jnp.where(bit, low, high)


def fourth_kernel(
    place, gathered, sums_in,
    source0, inv0, first0, east0, north0, inner0, outer0,
    source1, inv1, first1, east1, north1, inner1, outer1,
    source2, inv2, first2, east2, north2, inner2, outer2,
    fields, sums,
    whole, work2, work1, work0a, work0b, va, vb, wa, wb,
    ua2, ub2, ua1, ub1,
):
    source0, inv0, first0, east0, north0, inner0, outer0 = map(Wide, (source0, inv0, first0, east0, north0, inner0, outer0))
    source1, inv1, first1, east1, north1, inner1, outer1 = map(Wide, (source1, inv1, first1, east1, north1, inner1, outer1))
    source2, inv2, first2, east2, north2, inner2, outer2 = map(Wide, (source2, inv2, first2, east2, north2, inner2, outer2))
    work2, work1, work0a, work0b, va, vb, wa, wb = map(Wide, (work2, work1, work0a, work0b, va, vb, wa, wb))
    ua2, ub2, ua1, ub1 = map(Wide, (ua2, ub2, ua1, ub1))
    f32 = jnp.float32
    for q in range(TILES):
        for g in range(8):
            whole[q, 4 * g : 4 * g + 4] = gathered[g, 4 * q : 4 * q + 4]
    own_f, own_s = sums_in[0:1, 0:1], sums_in[1:2, 0:1]
    guess = own_f / own_s
    g0, g1, h0, i30, i31, e30, e31, n30, n31, in3, out3 = [whole[q] for q in range(TILES)]
    inv3, e3, n3 = (i30, i31), (e30, e31), (n30, n31)
    odd3 = odd_cells((ROWS, WIDE), 3)

    def beside3(c, u):
        t = e3[c] * row_next(u) + row_prev(e3[1 - c] * u)
        t = t + (n3[c] * lane_next(u, 8) + lane_prev(n3[1 - c] * u, 8)) + in3 * u
        above, below = out3 * lane_next(u, 1), lane_prev(out3 * u, 1)
        return t + (jnp.where(odd3, above, below) if c == 0 else jnp.where(odd3, below, above))

    a0, b0 = g0 + guess * h0, h0
    for _ in range(3):
        a1, b1 = g1 + beside3(1, a0) * inv3[1], beside3(1, b0) * inv3[1]
        a0, b0 = g0 + beside3(0, a1) * inv3[0], beside3(0, b1) * inv3[0]

    shift = lax.rem(35 - 4 * place[0], 32)
    a0, a1, b0, b1 = [pltpu.roll(x, shift, 0)[:16] for x in (a0, a1, b0, b1)]
    dims3 = (16, WIDE)
    phase = iota(dims3, 1) & 7
    odd3 = odd_cells(dims3, 3, 1)
    second_half = lane_bit(dims3, 1)

    def spread(x, m):
        x = jnp.where(phase == 0, lane_next(x, m) if m else x, 0.0)
        x = x + lane_prev(x, 1)
        x = x + lane_prev(x, 2)
        return x + lane_prev(x, 4)

    for m in range(PAIRS):
        x0 = jnp.where(second_half, spread(b0, m), spread(a0, m))
        x1 = jnp.where(second_half, spread(b1, m), spread(a1, m))
        low, high = jnp.where(odd3, x1, x0)[:12], jnp.where(odd3, x0, x1)[:12]
        spread_rows(2, low, high, work2, m)

    def smooth(level, rows, coeffs, inverse, source, first, work, ones, zeros, half_bit):
        odd = odd_cells((rows, WIDE), level)
        is_b = lane_bit((rows, WIDE), half_bit)
        step = 1 << level
        for m in range(PAIRS):
            work[m] = work[m] + jnp.where(is_b, 0.0, first[m])
        for m in range(PAIRS):
            ones[m] = (jnp.where(is_b, 0.0, source[1, m]) + beside(1, work, coeffs, m, odd, step)) * inverse[1, m]
        for m in range(PAIRS):
            zeros[m] = jnp.where(is_b, 0.0, first[m]) + beside(0, ones, coeffs, m, odd, step) * inverse[0, m]

    smooth(2, ROWS2, (east2, north2, inner2, outer2), inv2, source2, first2, work2, ub2, ua2, 1)
    dims2 = (ROWS2, WIDE)
    odd2 = odd_cells(dims2, 2)
    bit1, bit0 = lane_bit(dims2, 1), lane_bit(dims2, 0)

    def regroup2(x):
        a = jnp.where(bit1, lane_prev(x, 2), x)
        b = jnp.where(bit1, x, lane_next(x, 2))
        return jnp.where(bit0, b, a)

    for m in range(PAIRS):
        x0, x1 = regroup2(ua2[m]), regroup2(ub2[m])
        low, high = jnp.where(odd2, x1, x0)[4:16], jnp.where(odd2, x0, x1)[4:16]
        spread_rows(1, low, high, work1, m)

    smooth(1, 24, (east1, north1, inner1, outer1), inv1, source1, first1, work1, ub1, ua1, 0)
    dims1 = (24, WIDE)
    odd1 = odd_cells(dims1, 1)
    bit0 = lane_bit(dims1, 0)
    for m in range(PAIRS):
        x0, x1 = ua1[m], ub1[m]
        low, high = jnp.where(odd1, x1, x0), jnp.where(odd1, x0, x1)
        for work, pick in (
            (work0a, lambda x: jnp.where(bit0, lane_prev(x, 1), x)),
            (work0b, lambda x: jnp.where(bit0, x, lane_next(x, 1))),
        ):
            spread_rows(0, pick(low), pick(high), work, m)

    rows = 48
    odd = odd_cells((rows, WIDE), 0)
    coeffs = (east0, north0, inner0, outer0)
    for m in range(PAIRS):
        work0a[m] = work0a[m] + first0[m]
    for m in range(PAIRS):
        va[m] = (source0[1, m] + beside(1, work0a, coeffs, m, odd, 1)) * inv0[1, m]
        vb[m] = beside(1, work0b, coeffs, m, odd, 1) * inv0[1, m]
    for m in range(PAIRS):
        wa[m] = first0[m] + beside(0, va, coeffs, m, odd, 1) * inv0[0, m]
        wb[m] = beside(0, vb, coeffs, m, odd, 1) * inv0[0, m]
    for m in range(PAIRS):
        work0a[m] = work0a[m] - wa[m]
        work0b[m] = work0b[m] - wb[m]
    acc = [jnp.zeros((ROWS, LANES), f32)] * 11

    def own(x):
        return x[8 : 8 + ROWS, :LANES]

    for m in range(PAIRS):
        change_a = own(beside(1, work0a, coeffs, m, odd, 1))
        img_b = own(beside(1, work0b, coeffs, m, odd, 1))
        r0, r1 = own(source0[0, m]), own(source0[1, m])
        p0, p1, q0, q1 = own(wa[m]), own(va[m]), own(wb[m]), own(vb[m])
        img_a = r1 + change_a
        d = -change_a
        terms = (
            r0 * p0 + r1 * p1, r0 * q0 + r1 * q1,
            r0 * p0 + img_a * p1, r0 * q0 + img_a * q1 + img_b * p1, img_b * q1,
            d * d, d * img_a, img_a * img_a + r0 * r0, d * img_b, img_a * img_b, img_b * img_b,
        )
        acc = [x + y for x, y in zip(acc, terms, strict=True)]
        for t, x in enumerate((p0, p1, q0, q1, r0, r1, img_a, img_b)):
            fields[t, m] = x
    lane = iota((1, 16), 1)
    line = jnp.zeros((1, 16), f32)
    for q, x in enumerate(acc):
        line = jnp.where(lane == q, jnp.sum(x, keepdims=True), line)
    line = jnp.where(lane == 11, own_f, line)
    line = jnp.where(lane == 12, own_s, line)
    line = jnp.where(lane == 13, guess, line)
    sums[...] = jnp.broadcast_to(line, sums.shape)


def last_kernel(place, sums, fields, solution_ref, residual_ref, norm_ref, *, cells):
    x = sums[...]

    def column(q):
        return x[:, q : q + 1]

    def total(v):
        return jnp.sum(v, axis=0, keepdims=True)

    rp, rq, pa, pb, qb, dd, da, aa, db, ab, bb = [column(q) for q in range(11)]
    mean = total(column(11)) / total(column(12))
    shift = mean - column(13)
    step = total(rp + shift * rq) / total(pa + shift * (pb + shift * qb))
    s, t = step - 1.0, step * shift
    squares = total(dd - 2.0 * s * da + s * s * aa - 2.0 * t * db + 2.0 * s * t * ab + t * t * bb)
    norm_ref[...] = jnp.sqrt(jnp.maximum(squares, 0.0) / cells)
    mine = place[0] * place[3] + place[1]
    here = total(jnp.where(iota(shift.shape, 0) == mine, shift, 0.0))
    odd = odd_cells((ROWS, LANES), 0)
    for m in range(PAIRS):
        p0, p1, q0, q1, r0, r1, img_a, img_b = [fields[t, m] for t in range(8)]
        s0, s1 = step * (p0 + here * q0), step * (p1 + here * q1)
        n0, n1 = r0 - step * r0, r1 - step * (img_a + here * img_b)
        solution_ref[2 * m] = jnp.where(odd, s1, s0)
        solution_ref[2 * m + 1] = jnp.where(odd, s0, s1)
        residual_ref[2 * m] = jnp.where(odd, n1, n0)
        residual_ref[2 * m + 1] = jnp.where(odd, n0, n1)


def level_dims(rows):
    two, one, four = [(*lead, 2, rows, LANES) for lead in ((2, PAIRS), (PAIRS,), (PAIRS - 1,))]
    return two, one, four


def level_shapes(rows):
    two, one, four = [shape(*dims) for dims in level_dims(rows)]
    return two, two, one, two, two, one, four


def scratch(*dims):
    return pltpu.VMEM(dims, jnp.float32)


def pairs_of(count, first):
    return [(i, i + 1) for i in range(first, count - 1, 2)] + [(i + 1, i) for i in range(first, count - 1, 2)]


def shards(pressure, soil, vg_alpha, vg_n, sat_cond, storage, right_side):
    count_x, count_y = lax.axis_size("gx"), lax.axis_size("gy")
    index_x, index_y = lax.axis_index("gx"), lax.axis_index("gy")
    place = jnp.stack([index_x, index_y, jnp.int32(count_x), jnp.int32(count_y)])
    table = jnp.stack([jnp.log(vg_alpha), vg_n, sat_cond])
    table = jnp.pad(table, ((0, 5), (0, LANES - NSOIL)), constant_values=1.0)

    slab = shape(6 * PAIRS, HALO, LANES)
    packed, to_sibling, to_other = pl.pallas_call(
        first_kernel, out_shape=(shape(6 * PAIRS, ROWS, LANES), slab, slab),
        in_specs=[SM, VM, VM, VM, VM, VM], out_specs=(VM, VM, VM), compiler_params=params(16), name="conductivity",
    )(place, pressure, soil, table, storage, right_side)
    from_sibling = lax.ppermute(to_sibling, "gx", pairs_of(count_x, 0))
    from_other = lax.ppermute(to_other, "gx", pairs_of(count_x, 1))
    slab = shape(6, EXT, LANES)
    to_pair, to_next = pl.pallas_call(
        second_kernel, out_shape=(slab, slab), in_specs=[SM, VM, VM, VM], out_specs=(VM, VM),
        compiler_params=params(16), name="slabs",
    )(place, packed, from_sibling, from_other)
    from_pair = lax.ppermute(to_pair, "gy", pairs_of(count_y, 0))
    from_next = lax.ppermute(to_next, "gy", pairs_of(count_y, 1))

    def sized(rows):
        return [scratch(*dims) for dims in level_dims(rows)]

    two, one, four = sized(EXT)
    two1, one1, four1 = sized(ROWS1)
    two2, one2, _ = sized(ROWS2)
    two3, one3, four3 = sized(16)
    out = pl.pallas_call(
        third_kernel,
        out_shape=(*level_shapes(48), *level_shapes(24), *level_shapes(ROWS2), shape(4 * TILES, LANES), shape(8, LANES)),
        in_specs=[SM] + [VM] * 5, out_specs=(VM,) * 23,
        scratch_shapes=[
            two, two, two, two, two, one, four, two, one, one, one,
            two1, two1, two1, two1, one1, four1, two1, one1, one1, one1,
            two2, one2, one2,
            two3, two3, two3, two3, one3, four3,
        ],
        compiler_params=params(48), name="descent",
    )(place, packed, from_sibling, from_other, from_pair, from_next)
    levels, tiles, sums = out[:21], out[21], out[22]

    tile_pair = lax.ppermute(tiles, "gy", pairs_of(count_y, 0))
    tile_next = lax.ppermute(tiles, "gy", pairs_of(count_y, 1))
    even = (index_y & 1) == 0
    right, left = jnp.where(even, tile_pair, tile_next), jnp.where(even, tile_next, tile_pair)
    beyond = jnp.where(iota(tiles.shape, 1) < LANES // 2, right, left)
    window = jnp.concatenate([tiles, beyond], axis=1)
    window = jnp.broadcast_to(window[None], (count_x, *window.shape))
    gathered = lax.all_to_all(window, "gx", 0, 0, tiled=True)

    devices = count_x * count_y
    fields, partial = pl.pallas_call(
        fourth_kernel,
        out_shape=(shape(8, PAIRS, ROWS, LANES), shape(devices, 16)),
        in_specs=[SM] + [VM] * 23, out_specs=(VM, VM),
        scratch_shapes=[
            scratch(TILES, ROWS, WIDE), sized(ROWS2)[1], sized(24)[1],
            *[sized(48)[1]] * 6, *[sized(24)[1]] * 4,
        ],
        compiler_params=params(48), name="ascent",
    )(place, gathered, sums, *levels)
    every = lax.all_to_all(partial, ("gx", "gy"), 0, 0, tiled=True)

    layers = 2 * PAIRS
    solution_out, residual_out, norm = pl.pallas_call(
        functools.partial(last_kernel, cells=float(layers * ROWS * LANES * devices)),
        out_shape=(shape(layers, ROWS, LANES), shape(layers, ROWS, LANES), shape(1, 1)),
        in_specs=[SM, VM, VM], out_specs=(VM, VM, VM), compiler_params=params(16), name="outputs",
    )(place, every, fields)
    return solution_out, residual_out, norm.reshape(1)


def solution(mesh):
    split, whole = P(None, "gx", "gy"), P()
    return jax.shard_map(
        shards, mesh=mesh, in_specs=(split, split, whole, whole, whole, split, split),
        out_specs=(split, split, whole), check_vma=False,
    )
```

```python
import functools

import jax
import jax.numpy as jnp
from jax import lax
from jax.experimental import pallas as pl
from jax.experimental.pallas import tpu as pltpu
from jax.sharding import PartitionSpec as P

NSOIL = 23
PAIRS = 5
HALO = 24
ROWS, LANES = 32, 128
EXT = ROWS + 2 * HALO
WIDE = 2 * LANES
ROWS1, ROWS2 = 48, 24
TILES = 11
MIB = 1 << 20


def iota(shape, dim):
    return lax.broadcasted_iota(jnp.int32, shape, dim)


def odd_cells(shape, level, start=0):
    return ((iota(shape, 0) + start + (iota(shape, 1) >> level)) & 1) == 1


def lane_bit(shape, level):
    return ((iota(shape, 1) >> level) & 1) == 1


def row_next(x):
    return pltpu.roll(x, x.shape[0] - 1, 0)


def row_prev(x):
    return pltpu.roll(x, 1, 0)


def lane_next(x, step):
    return pltpu.roll(x, x.shape[1] - step, 1)


def lane_prev(x, step):
    return pltpu.roll(x, step, 1)


def pair_sum(x, level):
    step = 1 << level
    return x + jnp.where(lane_bit(x.shape, level), lane_prev(x, step), lane_next(x, step))


def beside(c, u, coeffs, m, odd, step):
    east, north, inner, outer = coeffs
    um = u[m]
    t = east[c, m] * row_next(um) + row_prev(east[1 - c, m] * um)
    t = t + (north[c, m] * lane_next(um, step) + lane_prev(north[1 - c, m] * um, step))
    t = t + inner[m] * um
    above = outer[m] * u[m + 1] if m < PAIRS - 1 else 0.0
    below = outer[m - 1] * u[m - 1] if m > 0 else 0.0
    return t + (jnp.where(odd, above, below) if c == 0 else jnp.where(odd, below, above))


def position():
    return lax.axis_index("gx"), lax.axis_index("gy")


def params(limit):
    return pltpu.CompilerParams(vmem_limit_bytes=limit * MIB)


VM = pl.BlockSpec(memory_space=pltpu.VMEM)
HBM = pl.BlockSpec(memory_space=pltpu.MemorySpace.HBM)


def shape(*dims):
    return jax.ShapeDtypeStruct(dims, jnp.float32)


class Wide:
    def __init__(self, ref):
        self.ref, self.lead = ref, len(ref.shape) - 3

    def parts(self, ids):
        ids = ids if isinstance(ids, tuple) else (ids,)
        rows = ids[self.lead] if len(ids) > self.lead else slice(None)
        return [self.ref.at[(*ids[: self.lead], half)] for half in range(2)], rows

    def __getitem__(self, ids):
        refs, rows = self.parts(ids)
        return jnp.concatenate([ref[rows, :] for ref in refs], axis=1)

    def __setitem__(self, ids, x):
        refs, rows = self.parts(ids)
        for half, ref in enumerate(refs):
            ref[rows, :] = x[:, LANES * half : LANES * (half + 1)]


def first_kernel(
    pressure_in, soil_in, storage_in, source_in, alpha_in, power_in, saturated_in, packed, to_sibling, to_other,
    pressure, soil, storage, source, table, sems,
):
    copies = [
        pltpu.make_async_copy(alpha_in, table.at[0], sems.at[4]),
        pltpu.make_async_copy(power_in, table.at[1], sems.at[5]),
        pltpu.make_async_copy(saturated_in, table.at[2], sems.at[6]),
        pltpu.make_async_copy(pressure_in, pressure, sems.at[0]),
        pltpu.make_async_copy(soil_in, soil, sems.at[1]),
        pltpu.make_async_copy(storage_in, storage, sems.at[2]),
        pltpu.make_async_copy(source_in, source, sems.at[3]),
    ]
    for copy in copies:
        copy.start()
    even = (position()[0] & 1) == 0
    odd = odd_cells((ROWS, LANES), 0)
    for copy in copies:
        copy.wait()
    rows = []
    for q in range(3):
        row = jnp.concatenate([table[q], jnp.ones((1, LANES - NSOIL), jnp.float32)], axis=1)
        rows.append(jnp.broadcast_to(jnp.log(row) if q == 0 else row, (8, LANES)))

    def look_up(row, ids):
        parts = [jnp.take_along_axis(row, ids[8 * b : 8 * b + 8], axis=1) for b in range(ROWS // 8)]
        return jnp.concatenate(parts, axis=0)

    def cond_of(k):
        ids = soil[k]
        log_scale, power, saturated = [look_up(r, ids) for r in rows]
        exponent = 1.0 - 1.0 / power
        log_s = power * (log_scale + jnp.log(jnp.abs(pressure[k])))
        log_1s = jnp.log(1.0 + jnp.exp(log_s))
        outer = 1.0 - jnp.exp(exponent * (log_s - log_1s))
        return saturated * jnp.exp(-0.5 * exponent * log_1s) * outer * outer

    def put(t, x):
        packed[t] = x
        high, low = x[ROWS - HALO :], x[:HALO]
        to_sibling[t] = jnp.where(even, high, low)
        to_other[t] = jnp.where(even, low, high)

    for m in range(PAIRS):
        triples = (
            (cond_of(2 * m), cond_of(2 * m + 1)),
            (storage[2 * m], storage[2 * m + 1]),
            (source[2 * m], source[2 * m + 1]),
        )
        for q, (a, b) in enumerate(triples):
            put(q * 10 + m, jnp.where(odd, b, a))
            put(q * 10 + PAIRS + m, jnp.where(odd, a, b))


def second_kernel(packed, from_sibling, from_other, to_pair, to_next):
    gx, gy = position()
    even_x, even_y = (gx & 1) == 0, (gy & 1) == 0
    lane = iota((EXT, LANES), 1)
    for tile in range(6):
        pair, other = None, None
        for m in range(PAIRS):
            t = tile * PAIRS + m
            sib, oth = from_sibling[t], from_other[t]
            x = jnp.concatenate([jnp.where(even_x, oth, sib), packed[t], jnp.where(even_x, sib, oth)], axis=0)
            left = pltpu.roll(x, HALO * m, 1) if m else x
            right = pltpu.roll(x, (HALO * m - (LANES - HALO)) % LANES, 1)
            a, b = jnp.where(even_y, right, left), jnp.where(even_y, left, right)
            pair = a if pair is None else jnp.where(lane >= HALO * m, a, pair)
            other = b if other is None else jnp.where(lane >= HALO * m, b, other)
        to_pair[tile] = pair
        to_next[tile] = other


def coarsen_level(level, fine_rows, out_rows, fine, coarse):
    stor, east, north, inner, outer = fine
    cstor, ceast, cnorth, cinner, couter = coarse
    half = fine_rows // 2
    dims = (half, WIDE)
    bit = lane_bit(dims, level)
    odd = odd_cells(dims, level + 1, 1 if level == 2 else 0)
    step = 1 << level

    def even_rows(ref, *ids):
        return ref[(*ids, pl.ds(0, half, stride=2))]

    def odd_rows(ref, *ids):
        return ref[(*ids, pl.ds(1, half, stride=2))]

    def put(ref, m, low, high):
        ref[0, m, slice(0, half)] = jnp.where(odd, high, low)
        ref[1, m, slice(0, half)] = jnp.where(odd, low, high)

    for m in range(PAIRS):
        u = even_rows(stor, 0, m) + odd_rows(stor, 1, m)
        v = even_rows(stor, 1, m) + odd_rows(stor, 0, m)
        put(cstor, m, pair_sum(jnp.where(bit, v, u), level), pair_sum(jnp.where(bit, u, v), level))
        e0, e1 = odd_rows(east, 0, m), odd_rows(east, 1, m)
        put(ceast, m, pair_sum(jnp.where(bit, e0, e1), level), pair_sum(jnp.where(bit, e1, e0), level))
        low = even_rows(north, 1, m) + odd_rows(north, 0, m)
        high = even_rows(north, 0, m) + odd_rows(north, 1, m)
        put(
            cnorth,
            m,
            jnp.where(bit, low, lane_next(low, step)),
            jnp.where(bit, high, lane_next(high, step)),
        )
        cinner[m, slice(0, half)] = pair_sum(even_rows(inner, m) + odd_rows(inner, m), level)
        if m < PAIRS - 1:
            couter[m, slice(0, half)] = pair_sum(even_rows(outer, m) + odd_rows(outer, m), level)


def restrict_level(level, fine_rows, residual, coarse_source):
    half = fine_rows // 2
    dims = (half, WIDE)
    bit = lane_bit(dims, level)
    odd = odd_cells(dims, level + 1, 1 if level == 2 else 0)
    for m in range(PAIRS):
        a = residual[m, pl.ds(0, half, stride=2)]
        b = residual[m, pl.ds(1, half, stride=2)]
        low = pair_sum(jnp.where(bit, b, a), level)
        high = pair_sum(jnp.where(bit, a, b), level)
        coarse_source[0, m, slice(0, half)] = jnp.where(odd, high, low)
        coarse_source[1, m, slice(0, half)] = jnp.where(odd, low, high)


def invert_diagonal(level, rows, coeffs, inverse):
    stor, east, north, inner, outer = coeffs
    odd = odd_cells((rows, WIDE), level)
    step = 1 << level
    for m in range(PAIRS):
        above = outer[m] if m < PAIRS - 1 else 0.0
        below = outer[m - 1] if m > 0 else 0.0
        for c in range(2):
            diag = stor[c, m] + east[c, m] + row_prev(east[1 - c, m]) + north[c, m]
            diag = diag + lane_prev(north[1 - c, m], step) + inner[m]
            diag = diag + (jnp.where(odd, above, below) if c == 0 else jnp.where(odd, below, above))
            inverse[c, m] = 1.0 / diag


def descend_level(level, rows, coeffs, inverse, source, first, second, residual):
    odd = odd_cells((rows, WIDE), level)
    step = 1 << level
    for m in range(PAIRS):
        first[m] = source[0, m] * inverse[0, m]
    for m in range(PAIRS):
        second[m] = (source[1, m] + beside(1, first, coeffs[1:], m, odd, step)) * inverse[1, m]
    for m in range(PAIRS):
        residual[m] = beside(0, second, coeffs[1:], m, odd, step)


def third_kernel(
    packed, from_sibling, from_other, from_pair, from_next,
    source0, inv0, first0, east0, north0, inner0, outer0,
    source1, inv1, first1, east1, north1, inner1, outer1,
    source2, inv2, first2, east2, north2, inner2, outer2,
    tiles, sums,
    cond, stor, src, east, north, inner, outer, inv, first, second, residual,
    stor1, src1, e1, n1, in1, out1, i1, f1, s1, r1,
    stor2, s2, r2,
    stor3, src3, e3, n3, in3, out3,
):
    source0, inv0, first0, east0, north0, inner0, outer0 = map(Wide, (source0, inv0, first0, east0, north0, inner0, outer0))
    source1, inv1, first1, east1, north1, inner1, outer1 = map(Wide, (source1, inv1, first1, east1, north1, inner1, outer1))
    source2, inv2, first2, east2, north2, inner2, outer2 = map(Wide, (source2, inv2, first2, east2, north2, inner2, outer2))
    cond, stor, src, east, north, inner, outer = map(Wide, (cond, stor, src, east, north, inner, outer))
    inv, first, second, residual = map(Wide, (inv, first, second, residual))
    stor1, src1, e1, n1, in1, out1, i1, f1, s1, r1 = map(Wide, (stor1, src1, e1, n1, in1, out1, i1, f1, s1, r1))
    stor2, s2, r2 = map(Wide, (stor2, s2, r2))
    stor3, src3, e3, n3, in3, out3 = map(Wide, (stor3, src3, e3, n3, in3, out3))
    gx, gy = position()
    even_x, even_y = (gx & 1) == 0, (gy & 1) == 0
    lane = iota((EXT, LANES), 1)
    for tile in range(6):
        pair, other = from_pair[tile], from_next[tile]
        right = jnp.where(even_y, pair, other)
        left = jnp.where(even_y, other, pair)
        ref = (cond, stor, src)[tile // 2]
        for m in range(PAIRS):
            t = tile * PAIRS + m
            sib, oth = from_sibling[t], from_other[t]
            x = jnp.concatenate([jnp.where(even_x, oth, sib), packed[t], jnp.where(even_x, sib, oth)], axis=0)
            r = pltpu.roll(right, (-HALO * m) % LANES, 1) if m else right
            l = pltpu.roll(left, (LANES - HALO - HALO * m) % LANES, 1)
            h = jnp.where(lane < HALO, r, jnp.where(lane >= LANES - HALO, l, 0.0))
            if tile // 2 == 1:
                x, h = jnp.where(x == 0.0, 1.0, x), jnp.where(h == 0.0, 1.0, h)
            ref.ref[tile % 2, m, 0] = x
            ref.ref[tile % 2, m, 1] = h

    dims = (EXT, WIDE)
    odd = odd_cells(dims, 0)
    row, column = iota(dims, 0), iota(dims, 1)
    last_row = (row == HALO + ROWS - 1) & (gx == lax.axis_size("gx") - 1)
    before_row = (row == HALO - 1) & (gx == 0)
    keep_x = jnp.where(last_row | before_row, 0.0, 0.5)
    last_column = (column == LANES - 1) & (gy == lax.axis_size("gy") - 1)
    before_column = (column == WIDE - 1) & (gy == 0)
    keep_y = jnp.where(last_column | before_column, 0.0, 0.5)
    for m in range(PAIRS):
        a, b = cond[0, m], cond[1, m]
        east[0, m] = (a + row_next(b)) * keep_x
        east[1, m] = (b + row_next(a)) * keep_x
        north[0, m] = (a + lane_next(b, 1)) * keep_y
        north[1, m] = (b + lane_next(a, 1)) * keep_y
        inner[m] = a + b
        if m < PAIRS - 1:
            outer[m] = jnp.where(odd, a + cond[1, m + 1], b + cond[0, m + 1])

    level0 = (stor, east, north, inner, outer)
    level1 = (stor1, e1, n1, in1, out1)
    level2 = (stor2, east2, north2, inner2, outer2)
    level3 = (stor3, e3, n3, in3, out3)
    invert_diagonal(0, EXT, level0, inv)
    descend_level(0, EXT, level0, inv, src, first, second, residual)

    half = EXT // 2
    for ref in (src1, e1, n1, in1, out1):
        ref.ref[..., half:, :] = jnp.zeros((*ref.ref.shape[:-2], ROWS1 - half, LANES), jnp.float32)
    stor1.ref[..., half:, :] = jnp.ones((2, PAIRS, 2, ROWS1 - half, LANES), jnp.float32)
    coarsen_level(0, EXT, ROWS1, level0, level1)
    restrict_level(0, EXT, residual, src1)
    invert_diagonal(1, ROWS1, level1, i1)
    descend_level(1, ROWS1, level1, i1, src1, f1, s1, r1)

    coarsen_level(1, ROWS1, ROWS2, level1, level2)
    restrict_level(1, ROWS1, r1, source2)
    invert_diagonal(2, ROWS2, level2, inv2)
    descend_level(2, ROWS2, level2, inv2, source2, first2, s2, r2)

    coarsen_level(2, ROWS2, 16, level2, level3)
    restrict_level(2, ROWS2, r2, src3)

    dims3 = (16, WIDE)
    odd3 = odd_cells(dims3, 3, 1)
    phase = iota((4, LANES), 1) & 7
    total_f, total_s = 0.0, 0.0
    compact = [None] * TILES
    for m in range(PAIRS):
        above = out3[m] if m < PAIRS - 1 else 0.0
        below = out3[m - 1] if m > 0 else 0.0
        invs = []
        for c in range(2):
            diag = stor3[c, m] + e3[c, m] + row_prev(e3[1 - c, m]) + n3[c, m]
            diag = diag + lane_prev(n3[1 - c, m], 8) + in3[m]
            diag = diag + (jnp.where(odd3, above, below) if c == 0 else jnp.where(odd3, below, above))
            invs.append(1.0 / diag)
            total_f = total_f + src3[c, m][3:7, :LANES]
            total_s = total_s + stor3[c, m][3:7, :LANES]
        values = (
            src3[0, m] * invs[0], src3[1, m] * invs[1], 1.0 - stor3[0, m] * invs[0], invs[0], invs[1],
            e3[0, m], e3[1, m], n3[0, m], n3[1, m], in3[m], out3[m] if m < PAIRS - 1 else jnp.zeros(dims3, jnp.float32),
        )
        for q, value in enumerate(values):
            own = value[3:7, :LANES]
            compact[q] = jnp.where(phase == m, own, 0.0 if m == 0 else compact[q])
    for q in range(TILES):
        tiles[4 * q : 4 * q + 4] = compact[q]
    sums[0:1] = jnp.broadcast_to(jnp.sum(total_f, keepdims=True), (1, LANES)) * 0.125
    sums[1:2] = jnp.broadcast_to(jnp.sum(total_s, keepdims=True), (1, LANES)) * 0.125

    for m in range(PAIRS):
        for c in range(2):
            for to, of in ((source0, src), (inv0, inv), (east0, east), (north0, north)):
                to[c, m] = of[c, m, slice(16, 64)]
            for to, of in ((source1, src1), (inv1, i1), (east1, e1), (north1, n1)):
                to[c, m] = of[c, m, slice(8, 32)]
        first0[m], first1[m] = first[m, slice(16, 64)], f1[m, slice(8, 32)]
        inner0[m], inner1[m] = inner[m, slice(16, 64)], in1[m, slice(8, 32)]
        if m < PAIRS - 1:
            outer0[m], outer1[m] = outer[m, slice(16, 64)], out1[m, slice(8, 32)]


def window_kernel(tiles, from_pair, from_next, window):
    even = (position()[1] & 1) == 0
    window[:, :LANES] = tiles[...]
    a, b = from_pair[...], from_next[...]
    right_first = (iota(a.shape, 1) < LANES // 2) == even
    window[:, LANES:] = jnp.where(right_first, a, b)


def spread_rows(level, low, high, into, m):
    rows = low.shape[0]
    bit = lane_bit(low.shape, level)
    into[m, pl.ds(0, rows, stride=2)] = jnp.where(bit, high, low)
    into[m, pl.ds(1, rows, stride=2)] = jnp.where(bit, low, high)


def fourth_kernel(
    mine, before, after, sib_mine, sib_before, sib_after, sums_in,
    source0, inv0, first0, east0, north0, inner0, outer0,
    source1, inv1, first1, east1, north1, inner1, outer1,
    source2, inv2, first2, east2, north2, inner2, outer2,
    fields, sums,
    whole, work2, work1, work0a, work0b, va, vb, wa, wb,
    ua2, ub2, ua1, ub1,
):
    source0, inv0, first0, east0, north0, inner0, outer0 = map(Wide, (source0, inv0, first0, east0, north0, inner0, outer0))
    source1, inv1, first1, east1, north1, inner1, outer1 = map(Wide, (source1, inv1, first1, east1, north1, inner1, outer1))
    source2, inv2, first2, east2, north2, inner2, outer2 = map(Wide, (source2, inv2, first2, east2, north2, inner2, outer2))
    work2, work1, work0a, work0b, va, vb, wa, wb = map(Wide, (work2, work1, work0a, work0b, va, vb, wa, wb))
    ua2, ub2, ua1, ub1 = map(Wide, (ua2, ub2, ua1, ub1))
    f32 = jnp.float32
    even = (position()[0] & 1) == 0
    for slot, (same, sib) in enumerate(((before, sib_before), (mine, sib_mine), (after, sib_after))):
        a, b = same[...], sib[...]
        low, high = jnp.where(even, a, b), jnp.where(even, b, a)
        for q in range(TILES):
            whole[q, 8 * slot : 8 * slot + 4] = low[4 * q : 4 * q + 4]
            whole[q, 8 * slot + 4 : 8 * slot + 8] = high[4 * q : 4 * q + 4]
    own_f, own_s = sums_in[0:1, 0:1], sums_in[1:2, 0:1]
    guess = own_f / own_s
    g0, g1, h0, i30, i31, e30, e31, n30, n31, in3, out3 = [whole[q] for q in range(TILES)]
    inv3, e3, n3 = (i30, i31), (e30, e31), (n30, n31)
    odd3 = odd_cells((24, WIDE), 3)

    def beside3(c, u):
        t = e3[c] * row_next(u) + row_prev(e3[1 - c] * u)
        t = t + (n3[c] * lane_next(u, 8) + lane_prev(n3[1 - c] * u, 8)) + in3 * u
        above, below = out3 * lane_next(u, 1), lane_prev(out3 * u, 1)
        return t + (jnp.where(odd3, above, below) if c == 0 else jnp.where(odd3, below, above))

    a0, b0 = g0 + guess * h0, h0
    for _ in range(3):
        a1, b1 = g1 + beside3(1, a0) * inv3[1], beside3(1, b0) * inv3[1]
        a0, b0 = g0 + beside3(0, a1) * inv3[0], beside3(0, b1) * inv3[0]

    a0, a1, b0, b1 = [jnp.where(even, pltpu.roll(x, 19, 0), pltpu.roll(x, 15, 0))[:16] for x in (a0, a1, b0, b1)]
    dims3 = (16, WIDE)
    phase = iota(dims3, 1) & 7
    odd3 = odd_cells(dims3, 3, 1)
    second_half = lane_bit(dims3, 1)

    def spread(x, m):
        x = jnp.where(phase == 0, lane_next(x, m) if m else x, 0.0)
        x = x + lane_prev(x, 1)
        x = x + lane_prev(x, 2)
        return x + lane_prev(x, 4)

    for m in range(PAIRS):
        x0 = jnp.where(second_half, spread(b0, m), spread(a0, m))
        x1 = jnp.where(second_half, spread(b1, m), spread(a1, m))
        low, high = jnp.where(odd3, x1, x0)[:12], jnp.where(odd3, x0, x1)[:12]
        spread_rows(2, low, high, work2, m)

    def smooth(level, rows, coeffs, inverse, source, first, work, ones, zeros, half_bit):
        odd = odd_cells((rows, WIDE), level)
        is_b = lane_bit((rows, WIDE), half_bit)
        step = 1 << level
        for m in range(PAIRS):
            work[m] = work[m] + jnp.where(is_b, 0.0, first[m])
        for m in range(PAIRS):
            ones[m] = (jnp.where(is_b, 0.0, source[1, m]) + beside(1, work, coeffs, m, odd, step)) * inverse[1, m]
        for m in range(PAIRS):
            zeros[m] = jnp.where(is_b, 0.0, first[m]) + beside(0, ones, coeffs, m, odd, step) * inverse[0, m]

    smooth(2, ROWS2, (east2, north2, inner2, outer2), inv2, source2, first2, work2, ub2, ua2, 1)
    dims2 = (ROWS2, WIDE)
    odd2 = odd_cells(dims2, 2)
    bit1, bit0 = lane_bit(dims2, 1), lane_bit(dims2, 0)

    def regroup2(x):
        a = jnp.where(bit1, lane_prev(x, 2), x)
        b = jnp.where(bit1, x, lane_next(x, 2))
        return jnp.where(bit0, b, a)

    for m in range(PAIRS):
        x0, x1 = regroup2(ua2[m]), regroup2(ub2[m])
        low, high = jnp.where(odd2, x1, x0)[4:16], jnp.where(odd2, x0, x1)[4:16]
        spread_rows(1, low, high, work1, m)

    smooth(1, 24, (east1, north1, inner1, outer1), inv1, source1, first1, work1, ub1, ua1, 0)
    dims1 = (24, WIDE)
    odd1 = odd_cells(dims1, 1)
    bit0 = lane_bit(dims1, 0)
    for m in range(PAIRS):
        x0, x1 = ua1[m], ub1[m]
        low, high = jnp.where(odd1, x1, x0), jnp.where(odd1, x0, x1)
        for work, pick in (
            (work0a, lambda x: jnp.where(bit0, lane_prev(x, 1), x)),
            (work0b, lambda x: jnp.where(bit0, x, lane_next(x, 1))),
        ):
            spread_rows(0, pick(low), pick(high), work, m)

    rows = 48
    odd = odd_cells((rows, WIDE), 0)
    coeffs = (east0, north0, inner0, outer0)
    for m in range(PAIRS):
        work0a[m] = work0a[m] + first0[m]
    for m in range(PAIRS):
        va[m] = (source0[1, m] + beside(1, work0a, coeffs, m, odd, 1)) * inv0[1, m]
        vb[m] = beside(1, work0b, coeffs, m, odd, 1) * inv0[1, m]
    for m in range(PAIRS):
        wa[m] = first0[m] + beside(0, va, coeffs, m, odd, 1) * inv0[0, m]
        wb[m] = beside(0, vb, coeffs, m, odd, 1) * inv0[0, m]
    for m in range(PAIRS):
        work0a[m] = work0a[m] - wa[m]
        work0b[m] = work0b[m] - wb[m]
    acc = [jnp.zeros((ROWS, LANES), f32)] * 11

    def own(x):
        return x[8 : 8 + ROWS, :LANES]

    for m in range(PAIRS):
        change_a = own(beside(1, work0a, coeffs, m, odd, 1))
        img_b = own(beside(1, work0b, coeffs, m, odd, 1))
        r0, r1 = own(source0[0, m]), own(source0[1, m])
        p0, p1, q0, q1 = own(wa[m]), own(va[m]), own(wb[m]), own(vb[m])
        img_a = r1 + change_a
        d = -change_a
        terms = (
            r0 * p0 + r1 * p1, r0 * q0 + r1 * q1,
            r0 * p0 + img_a * p1, r0 * q0 + img_a * q1 + img_b * p1, img_b * q1,
            d * d, d * img_a, img_a * img_a + r0 * r0, d * img_b, img_a * img_b, img_b * img_b,
        )
        acc = [x + y for x, y in zip(acc, terms, strict=True)]
        for t, x in enumerate((p0, p1, q0, q1, r0, r1, img_a, img_b)):
            fields[t, m] = x
    lane = iota((1, 16), 1)
    line = jnp.zeros((1, 16), f32)
    for q, x in enumerate(acc):
        line = jnp.where(lane == q, jnp.sum(x, keepdims=True), line)
    line = jnp.where(lane == 11, own_f, line)
    line = jnp.where(lane == 12, own_s, line)
    line = jnp.where(lane == 13, guess, line)
    sums[...] = jnp.broadcast_to(line, sums.shape)


def last_kernel(sums, fields, solution_out, residual_out, norm_ref, solution_ref, residual_ref, sems, *, cells):
    x = sums[...]

    def column(q):
        return x[:, q : q + 1]

    def total(v):
        return jnp.sum(v, axis=0, keepdims=True)

    rp, rq, pa, pb, qb, dd, da, aa, db, ab, bb = [column(q) for q in range(11)]
    mean = total(column(11)) / total(column(12))
    shift = mean - column(13)
    step = total(rp + shift * rq) / total(pa + shift * (pb + shift * qb))
    s, t = step - 1.0, step * shift
    squares = total(dd - 2.0 * s * da + s * s * aa - 2.0 * t * db + 2.0 * s * t * ab + t * t * bb)
    norm_ref[...] = jnp.sqrt(jnp.maximum(squares, 0.0) / cells)
    gx, gy = position()
    mine = gx * lax.axis_size("gy") + gy
    here = total(jnp.where(iota(shift.shape, 0) == mine, shift, 0.0))
    odd = odd_cells((ROWS, LANES), 0)
    copies = []
    for m in range(PAIRS):
        p0, p1, q0, q1, r0, r1, img_a, img_b = [fields[t, m] for t in range(8)]
        s0, s1 = step * (p0 + here * q0), step * (p1 + here * q1)
        n0, n1 = r0 - step * r0, r1 - step * (img_a + here * img_b)
        solution_ref[2 * m] = jnp.where(odd, s1, s0)
        solution_ref[2 * m + 1] = jnp.where(odd, s0, s1)
        residual_ref[2 * m] = jnp.where(odd, n1, n0)
        residual_ref[2 * m + 1] = jnp.where(odd, n0, n1)
        layers = pl.ds(2 * m, 2)
        for q, (ref, out) in enumerate(((solution_ref, solution_out), (residual_ref, residual_out))):
            copies.append(pltpu.make_async_copy(ref.at[layers], out.at[layers], sems.at[q, m]))
            copies[-1].start()
    for copy in copies:
        copy.wait()


def level_dims(rows):
    two, one, four = [(*lead, 2, rows, LANES) for lead in ((2, PAIRS), (PAIRS,), (PAIRS - 1,))]
    return two, one, four


def level_shapes(rows):
    two, one, four = [shape(*dims) for dims in level_dims(rows)]
    return two, two, one, two, two, one, four


def scratch(*dims):
    return pltpu.VMEM(dims, jnp.float32)


def pairs_of(count, first):
    return [(i, i + 1) for i in range(first, count - 1, 2)] + [(i + 1, i) for i in range(first, count - 1, 2)]


def pair_exchange(x, axis):
    count = lax.axis_size(axis)
    return [lax.ppermute(x_i, axis, pairs_of(count, first)) for first, x_i in enumerate(x)]


def shards(pressure, soil, vg_alpha, vg_n, sat_cond, storage, right_side):
    count_x, count_y = lax.axis_size("gx"), lax.axis_size("gy")
    block, slab = scratch(2 * PAIRS, ROWS, LANES), shape(6 * PAIRS, HALO, LANES)
    arguments = (pressure, soil, storage, right_side, *[v.reshape(1, NSOIL) for v in (vg_alpha, vg_n, sat_cond)])
    packed, to_sibling, to_other = pl.pallas_call(
        first_kernel, out_shape=(shape(6 * PAIRS, ROWS, LANES), slab, slab),
        in_specs=[HBM] * 7, out_specs=(VM, VM, VM),
        scratch_shapes=[
            block, pltpu.VMEM((2 * PAIRS, ROWS, LANES), jnp.int32), block, block, scratch(3, 1, NSOIL), pltpu.SemaphoreType.DMA((7,)),
        ],
        compiler_params=params(4), name="conductivity",
    )(*[pltpu.with_memory_space_constraint(v, pltpu.MemorySpace.HBM) for v in arguments])
    from_sibling, from_other = pair_exchange((to_sibling, to_other), "gx")
    slab = shape(6, EXT, LANES)
    to_pair, to_next = pl.pallas_call(
        second_kernel, out_shape=(slab, slab), in_specs=[VM, VM, VM], out_specs=(VM, VM),
        compiler_params=params(4), name="slabs",
    )(packed, from_sibling, from_other)
    from_pair, from_next = pair_exchange((to_pair, to_next), "gy")

    def sized(rows):
        return [scratch(*dims) for dims in level_dims(rows)]

    two, one, four = sized(EXT)
    two1, one1, four1 = sized(ROWS1)
    two2, one2, _ = sized(ROWS2)
    two3, one3, four3 = sized(16)
    out = pl.pallas_call(
        third_kernel,
        out_shape=(*level_shapes(48), *level_shapes(24), *level_shapes(ROWS2), shape(4 * TILES, LANES), shape(8, LANES)),
        in_specs=[VM] * 5, out_specs=(VM,) * 23,
        scratch_shapes=[
            two, two, two, two, two, one, four, two, one, one, one,
            two1, two1, two1, two1, one1, four1, two1, one1, one1, one1,
            two2, one2, one2,
            two3, two3, two3, two3, one3, four3,
        ],
        compiler_params=params(12), name="descent",
    )(packed, from_sibling, from_other, from_pair, from_next)
    levels, tiles, sums = out[:21], out[21], out[22]

    tile_pair, tile_next = pair_exchange((tiles, tiles), "gy")
    window = pl.pallas_call(
        window_kernel, out_shape=shape(4 * TILES, WIDE), in_specs=[VM] * 3, out_specs=VM, compiler_params=params(2), name="window",
    )(tiles, tile_pair, tile_next)
    sibling = pairs_of(count_x, 0)
    before = lax.ppermute(window, "gx", [(i, i + 2) for i in range(count_x - 2)])
    after = lax.ppermute(window, "gx", [(i + 2, i) for i in range(count_x - 2)])
    blocks = (window, before, after, *[lax.ppermute(x, "gx", sibling) for x in (window, before, after)])

    devices = count_x * count_y
    fields, partial = pl.pallas_call(
        fourth_kernel,
        out_shape=(shape(8, PAIRS, ROWS, LANES), shape(devices, 16)),
        in_specs=[VM] * 28, out_specs=(VM, VM),
        scratch_shapes=[
            scratch(TILES, 24, WIDE), sized(ROWS2)[1], sized(24)[1],
            *[sized(48)[1]] * 6, *[sized(24)[1]] * 4,
        ],
        compiler_params=params(8), name="ascent",
    )(*blocks, sums, *levels)
    every = lax.all_to_all(partial, ("gx", "gy"), 0, 0, tiled=True)

    layers = 2 * PAIRS
    out = shape(layers, ROWS, LANES)
    solution_out, residual_out, norm = pl.pallas_call(
        functools.partial(last_kernel, cells=float(layers * ROWS * LANES * devices)),
        out_shape=(out, out, shape(1, 1)), in_specs=[VM, VM], out_specs=(HBM, HBM, VM),
        scratch_shapes=[scratch(*out.shape), scratch(*out.shape), pltpu.SemaphoreType.DMA((2, PAIRS))],
        compiler_params=params(4), name="outputs",
    )(every, fields)
    return solution_out, residual_out, norm.reshape(1)


def solution(mesh):
    split, whole = P(None, "gx", "gy"), P()
    return jax.shard_map(
        shards, mesh=mesh, in_specs=(split, split, whole, whole, whole, split, split),
        out_specs=(split, split, whole), check_vma=False,
    )
```

```python
import functools

import jax
import jax.numpy as jnp
from jax import lax
from jax.experimental import pallas as pl
from jax.experimental.pallas import tpu as pltpu
from jax.sharding import PartitionSpec as P

NSOIL = 23
PAIRS = 5
HALO = 24
ROWS, LANES = 32, 128
EXT = ROWS + 2 * HALO
WIDE = 2 * LANES
ROWS1, ROWS2 = EXT // 2, 24
TILES = 11
MIB = 1 << 20


def iota(shape, dim):
    return lax.broadcasted_iota(jnp.int32, shape, dim)


def odd_cells(shape, level, start=0):
    return ((iota(shape, 0) + start + (iota(shape, 1) >> level)) & 1) == 1


def lane_bit(shape, level):
    return ((iota(shape, 1) >> level) & 1) == 1


def row_next(x):
    return pltpu.roll(x, x.shape[0] - 1, 0)


def row_prev(x):
    return pltpu.roll(x, 1, 0)


def lane_next(x, step):
    return pltpu.roll(x, x.shape[1] - step, 1)


def lane_prev(x, step):
    return pltpu.roll(x, step, 1)


def by_halves(f, x):
    return jnp.concatenate([f(x[:, start : start + LANES]) for start in range(0, x.shape[1], LANES)], axis=1)


def near_next(x, step):
    return by_halves(lambda h: lane_next(h, step), x)


def near_prev(x, step):
    return by_halves(lambda h: lane_prev(h, step), x)


def pair_sum(x, level):
    step = 1 << level
    return x + jnp.where(lane_bit(x.shape, level), near_prev(x, step), near_next(x, step))


def beside(c, u, coeffs, m, odd, step):
    east, north, inner, outer = coeffs
    um = u[m]
    t = east[c, m] * row_next(um) + row_prev(east[1 - c, m] * um)
    t = t + (north[c, m] * lane_next(um, step) + lane_prev(north[1 - c, m] * um, step))
    t = t + inner[m] * um
    above = outer[m] * u[m + 1] if m < PAIRS - 1 else 0.0
    below = outer[m - 1] * u[m - 1] if m > 0 else 0.0
    return t + (jnp.where(odd, above, below) if c == 0 else jnp.where(odd, below, above))


def position():
    return lax.axis_index("gx"), lax.axis_index("gy")


def params(limit):
    return pltpu.CompilerParams(vmem_limit_bytes=limit * MIB)


VM = pl.BlockSpec(memory_space=pltpu.VMEM)
HBM = pl.BlockSpec(memory_space=pltpu.MemorySpace.HBM)


def shape(*dims):
    return jax.ShapeDtypeStruct(dims, jnp.float32)


class Wide:
    def __init__(self, ref):
        self.ref, self.lead = ref, len(ref.shape) - 3

    def parts(self, ids):
        ids = ids if isinstance(ids, tuple) else (ids,)
        rows = ids[self.lead] if len(ids) > self.lead else slice(None)
        return [self.ref.at[(*ids[: self.lead], half)] for half in range(2)], rows

    def __getitem__(self, ids):
        refs, rows = self.parts(ids)
        return jnp.concatenate([ref[rows, :] for ref in refs], axis=1)

    def __setitem__(self, ids, x):
        refs, rows = self.parts(ids)
        for half, ref in enumerate(refs):
            ref[rows, :] = x[:, LANES * half : LANES * (half + 1)]


def first_kernel(
    pressure_in, soil_in, storage_in, source_in, alpha_in, power_in, saturated_in, packed, to_sibling, to_other, to_pair, to_next,
    pressure, soil, storage, source, table, sems,
):
    copies = [
        pltpu.make_async_copy(alpha_in, table.at[0], sems.at[4]),
        pltpu.make_async_copy(power_in, table.at[1], sems.at[5]),
        pltpu.make_async_copy(saturated_in, table.at[2], sems.at[6]),
        pltpu.make_async_copy(pressure_in, pressure, sems.at[0]),
        pltpu.make_async_copy(soil_in, soil, sems.at[1]),
        pltpu.make_async_copy(storage_in, storage, sems.at[2]),
        pltpu.make_async_copy(source_in, source, sems.at[3]),
    ]
    for copy in copies:
        copy.start()
    gx, gy = position()
    even, even_y = (gx & 1) == 0, (gy & 1) == 0
    odd = odd_cells((ROWS, LANES), 0)
    lane = iota((ROWS, LANES), 1)
    for copy in copies:
        copy.wait()
    rows = []
    for q in range(3):
        row = jnp.concatenate([table[q], jnp.ones((1, LANES - NSOIL), jnp.float32)], axis=1)
        rows.append(jnp.broadcast_to(jnp.log(row) if q == 0 else row, (8, LANES)))

    def look_up(row, ids):
        parts = [jnp.take_along_axis(row, ids[8 * b : 8 * b + 8], axis=1) for b in range(ROWS // 8)]
        return jnp.concatenate(parts, axis=0)

    def cond_of(k):
        ids = soil[k]
        log_scale, power, saturated = [look_up(r, ids) for r in rows]
        exponent = 1.0 - 1.0 / power
        log_s = power * (log_scale + jnp.log(jnp.abs(pressure[k])))
        log_1s = jnp.log(1.0 + jnp.exp(log_s))
        outer = 1.0 - jnp.exp(exponent * (log_s - log_1s))
        return saturated * jnp.exp(-0.5 * exponent * log_1s) * outer * outer

    def put(tile, m, x):
        t = tile * PAIRS + m
        packed[t] = x
        high, low = x[ROWS - HALO :], x[:HALO]
        to_sibling[t] = jnp.where(even, high, low)
        to_other[t] = jnp.where(even, low, high)
        left = pltpu.roll(x, HALO * m, 1) if m else x
        right = pltpu.roll(x, (HALO * m - (LANES - HALO)) % LANES, 1)
        for ref, y in ((to_pair, jnp.where(even_y, right, left)), (to_next, jnp.where(even_y, left, right))):
            ref[tile] = y if m == 0 else jnp.where(lane >= HALO * m, y, ref[tile])

    for m in range(PAIRS):
        triples = (
            (cond_of(2 * m), cond_of(2 * m + 1)),
            (storage[2 * m], storage[2 * m + 1]),
            (source[2 * m], source[2 * m + 1]),
        )
        for q, (a, b) in enumerate(triples):
            put(2 * q, m, jnp.where(odd, b, a))
            put(2 * q + 1, m, jnp.where(odd, a, b))


def second_kernel(from_pair, from_next, to_sibling, to_other):
    even = (position()[0] & 1) == 0
    for q, ref in enumerate((from_pair, from_next)):
        for tile in range(6):
            high, low = ref[tile, ROWS - HALO :], ref[tile, :HALO]
            to_sibling[6 * q + tile] = jnp.where(even, high, low)
            to_other[6 * q + tile] = jnp.where(even, low, high)


def coarsen_level(level, fine_rows, out_rows, fine, coarse):
    stor, east, north, inner, outer = fine
    cstor, ceast, cnorth, cinner, couter = coarse
    half = fine_rows // 2
    dims = (half, WIDE)
    bit = lane_bit(dims, level)
    odd = odd_cells(dims, level + 1, 1 if level == 2 else 0)
    step = 1 << level

    def even_rows(ref, *ids):
        return ref[(*ids, pl.ds(0, half, stride=2))]

    def odd_rows(ref, *ids):
        return ref[(*ids, pl.ds(1, half, stride=2))]

    swap = bit ^ odd

    def put(ref, m, a, b):
        ref[0, m, slice(0, half)] = a
        ref[1, m, slice(0, half)] = b

    for m in range(PAIRS):
        u = even_rows(stor, 0, m) + odd_rows(stor, 1, m)
        v = even_rows(stor, 1, m) + odd_rows(stor, 0, m)
        put(cstor, m, pair_sum(jnp.where(swap, v, u), level), pair_sum(jnp.where(swap, u, v), level))
        e0, e1 = odd_rows(east, 0, m), odd_rows(east, 1, m)
        put(ceast, m, pair_sum(jnp.where(swap, e0, e1), level), pair_sum(jnp.where(swap, e1, e0), level))
        low = even_rows(north, 1, m) + odd_rows(north, 0, m)
        high = even_rows(north, 0, m) + odd_rows(north, 1, m)
        a, b = jnp.where(odd, high, low), jnp.where(odd, low, high)
        put(cnorth, m, jnp.where(bit, a, near_next(a, step)), jnp.where(bit, b, near_next(b, step)))
        cinner[m, slice(0, half)] = pair_sum(even_rows(inner, m) + odd_rows(inner, m), level)
        if m < PAIRS - 1:
            couter[m, slice(0, half)] = pair_sum(even_rows(outer, m) + odd_rows(outer, m), level)


def restrict_level(level, fine_rows, residual, coarse_source):
    half = fine_rows // 2
    dims = (half, WIDE)
    bit = lane_bit(dims, level)
    odd = odd_cells(dims, level + 1, 1 if level == 2 else 0)
    swap = bit ^ odd
    for m in range(PAIRS):
        a = residual[m, pl.ds(0, half, stride=2)]
        b = residual[m, pl.ds(1, half, stride=2)]
        coarse_source[0, m, slice(0, half)] = pair_sum(jnp.where(swap, b, a), level)
        coarse_source[1, m, slice(0, half)] = pair_sum(jnp.where(swap, a, b), level)


def invert_diagonal(level, rows, coeffs, inverse):
    stor, east, north, inner, outer = coeffs
    odd = odd_cells((rows, WIDE), level)
    step = 1 << level
    for m in range(PAIRS):
        above = outer[m] if m < PAIRS - 1 else 0.0
        below = outer[m - 1] if m > 0 else 0.0
        for c in range(2):
            diag = stor[c, m] + east[c, m] + row_prev(east[1 - c, m]) + north[c, m]
            diag = diag + lane_prev(north[1 - c, m], step) + inner[m]
            diag = diag + (jnp.where(odd, above, below) if c == 0 else jnp.where(odd, below, above))
            inverse[c, m] = 1.0 / diag


def descend_level(level, rows, coeffs, inverse, source, first, second, residual):
    odd = odd_cells((rows, WIDE), level)
    step = 1 << level
    for m in range(PAIRS):
        first[m] = source[0, m] * inverse[0, m]
    for m in range(PAIRS):
        second[m] = (source[1, m] + beside(1, first, coeffs[1:], m, odd, step)) * inverse[1, m]
    for m in range(PAIRS):
        residual[m] = beside(0, second, coeffs[1:], m, odd, step)


def third_kernel(
    packed, from_sibling, from_other, from_pair, from_next, corner_sibling, corner_other,
    source0, inv0, first0, east0, north0, inner0, outer0,
    source1, inv1, first1, east1, north1, inner1, outer1,
    source2, inv2, first2, east2, north2, inner2, outer2,
    tiles, sums,
    cond, stor, src, east, north, inner, outer, inv, first, second, residual,
    stor1, src1, e1, n1, in1, out1, i1, f1, s1, r1,
    stor2, s2, r2,
    stor3, src3, e3, n3, in3, out3,
):
    source0, inv0, first0, east0, north0, inner0, outer0 = map(Wide, (source0, inv0, first0, east0, north0, inner0, outer0))
    source1, inv1, first1, east1, north1, inner1, outer1 = map(Wide, (source1, inv1, first1, east1, north1, inner1, outer1))
    source2, inv2, first2, east2, north2, inner2, outer2 = map(Wide, (source2, inv2, first2, east2, north2, inner2, outer2))
    cond, stor, src, east, north, inner, outer = map(Wide, (cond, stor, src, east, north, inner, outer))
    inv, first, second, residual = map(Wide, (inv, first, second, residual))
    stor1, src1, e1, n1, in1, out1, i1, f1, s1, r1 = map(Wide, (stor1, src1, e1, n1, in1, out1, i1, f1, s1, r1))
    stor2, s2, r2 = map(Wide, (stor2, s2, r2))
    stor3, src3, e3, n3, in3, out3 = map(Wide, (stor3, src3, e3, n3, in3, out3))
    gx, gy = position()
    even_x, even_y = (gx & 1) == 0, (gy & 1) == 0
    lane = iota((EXT, LANES), 1)

    def rows_of(sib, oth, own):
        return jnp.concatenate([jnp.where(even_x, oth, sib), own, jnp.where(even_x, sib, oth)], axis=0)

    for tile in range(6):
        pair, other = [
            rows_of(corner_sibling[q + tile], corner_other[q + tile], ref[tile]) for q, ref in ((0, from_pair), (6, from_next))
        ]
        right = jnp.where(even_y, pair, other)
        left = jnp.where(even_y, other, pair)
        ref = (cond, stor, src)[tile // 2]
        for m in range(PAIRS):
            t = tile * PAIRS + m
            x = rows_of(from_sibling[t], from_other[t], packed[t])
            r = pltpu.roll(right, (-HALO * m) % LANES, 1) if m else right
            l = pltpu.roll(left, (LANES - HALO - HALO * m) % LANES, 1)
            h = jnp.where(lane < HALO, r, jnp.where(lane >= LANES - HALO, l, 0.0))
            if tile // 2 == 1:
                x, h = jnp.where(x == 0.0, 1.0, x), jnp.where(h == 0.0, 1.0, h)
            ref.ref[tile % 2, m, 0] = x
            ref.ref[tile % 2, m, 1] = h

    dims = (EXT, WIDE)
    odd = odd_cells(dims, 0)
    row, column = iota(dims, 0), iota(dims, 1)
    last_row = (row == HALO + ROWS - 1) & (gx == lax.axis_size("gx") - 1)
    before_row = (row == HALO - 1) & (gx == 0)
    keep_x = jnp.where(last_row | before_row, 0.0, 0.5)
    last_column = (column == LANES - 1) & (gy == lax.axis_size("gy") - 1)
    before_column = (column == WIDE - 1) & (gy == 0)
    keep_y = jnp.where(last_column | before_column, 0.0, 0.5)
    for m in range(PAIRS):
        a, b = cond[0, m], cond[1, m]
        east[0, m] = (a + row_next(b)) * keep_x
        east[1, m] = (b + row_next(a)) * keep_x
        north[0, m] = (a + lane_next(b, 1)) * keep_y
        north[1, m] = (b + lane_next(a, 1)) * keep_y
        inner[m] = a + b
        if m < PAIRS - 1:
            outer[m] = jnp.where(odd, a + cond[1, m + 1], b + cond[0, m + 1])

    level0 = (stor, east, north, inner, outer)
    level1 = (stor1, e1, n1, in1, out1)
    level2 = (stor2, east2, north2, inner2, outer2)
    level3 = (stor3, e3, n3, in3, out3)
    invert_diagonal(0, EXT, level0, inv)
    descend_level(0, EXT, level0, inv, src, first, second, residual)

    coarsen_level(0, EXT, ROWS1, level0, level1)
    restrict_level(0, EXT, residual, src1)
    invert_diagonal(1, ROWS1, level1, i1)
    descend_level(1, ROWS1, level1, i1, src1, f1, s1, r1)

    half = ROWS1 // 2
    for ref in (source2, east2, north2, inner2, outer2):
        ref.ref[..., half:, :] = jnp.zeros((*ref.ref.shape[:-2], ROWS2 - half, LANES), jnp.float32)
    stor2.ref[..., half:, :] = jnp.ones((2, PAIRS, 2, ROWS2 - half, LANES), jnp.float32)
    coarsen_level(1, ROWS1, ROWS2, level1, level2)
    restrict_level(1, ROWS1, r1, source2)
    invert_diagonal(2, ROWS2, level2, inv2)
    descend_level(2, ROWS2, level2, inv2, source2, first2, s2, r2)

    coarsen_level(2, ROWS2, 16, level2, level3)
    restrict_level(2, ROWS2, r2, src3)

    dims3 = (16, WIDE)
    odd3 = odd_cells(dims3, 3, 1)
    phase = iota((4, LANES), 1) & 7
    total_f, total_s = 0.0, 0.0
    compact = [None] * TILES
    for m in range(PAIRS):
        above = out3[m] if m < PAIRS - 1 else 0.0
        below = out3[m - 1] if m > 0 else 0.0
        invs = []
        for c in range(2):
            diag = stor3[c, m] + e3[c, m] + row_prev(e3[1 - c, m]) + n3[c, m]
            diag = diag + lane_prev(n3[1 - c, m], 8) + in3[m]
            diag = diag + (jnp.where(odd3, above, below) if c == 0 else jnp.where(odd3, below, above))
            invs.append(1.0 / diag)
            total_f = total_f + src3[c, m][3:7, :LANES]
            total_s = total_s + stor3[c, m][3:7, :LANES]
        values = (
            src3[0, m] * invs[0], src3[1, m] * invs[1], 1.0 - stor3[0, m] * invs[0], invs[0], invs[1],
            e3[0, m], e3[1, m], n3[0, m], n3[1, m], in3[m], out3[m] if m < PAIRS - 1 else jnp.zeros(dims3, jnp.float32),
        )
        for q, value in enumerate(values):
            own = value[3:7, :LANES]
            compact[q] = jnp.where(phase == m, own, 0.0 if m == 0 else compact[q])
    for q in range(TILES):
        tiles[4 * q : 4 * q + 4] = compact[q]
    sums[0:1] = jnp.broadcast_to(jnp.sum(total_f, keepdims=True), (1, LANES)) * 0.125
    sums[1:2] = jnp.broadcast_to(jnp.sum(total_s, keepdims=True), (1, LANES)) * 0.125

    for m in range(PAIRS):
        for c in range(2):
            for to, of in ((source0, src), (inv0, inv), (east0, east), (north0, north)):
                to[c, m] = of[c, m, slice(16, 64)]
            for to, of in ((source1, src1), (inv1, i1), (east1, e1), (north1, n1)):
                to[c, m] = of[c, m, slice(8, 32)]
        first0[m], first1[m] = first[m, slice(16, 64)], f1[m, slice(8, 32)]
        inner0[m], inner1[m] = inner[m, slice(16, 64)], in1[m, slice(8, 32)]
        if m < PAIRS - 1:
            outer0[m], outer1[m] = outer[m, slice(16, 64)], out1[m, slice(8, 32)]


def window_kernel(tiles, from_pair, from_next, window):
    even = (position()[1] & 1) == 0
    window[:, :LANES] = tiles[...]
    a, b = from_pair[...], from_next[...]
    right_first = (iota(a.shape, 1) < LANES // 2) == even
    window[:, LANES:] = jnp.where(right_first, a, b)


def spread_rows(level, low, high, into, m):
    rows = low.shape[0]
    bit = lane_bit(low.shape, level)
    into[m, pl.ds(0, rows, stride=2)] = jnp.where(bit, high, low)
    into[m, pl.ds(1, rows, stride=2)] = jnp.where(bit, low, high)


def join_kernel(mine, sibling, both):
    both[: 4 * TILES] = mine[...]
    both[4 * TILES :] = sibling[...]


def fourth_kernel(
    mine, sibling, received, passed_on, sums_in,
    source0, inv0, first0, east0, north0, inner0, outer0,
    source1, inv1, first1, east1, north1, inner1, outer1,
    source2, inv2, first2, east2, north2, inner2, outer2,
    fields, sums,
    whole, work2, work1, work0a, work0b, va, vb, wa, wb,
    ua2, ub2, ua1, ub1,
):
    source0, inv0, first0, east0, north0, inner0, outer0 = map(Wide, (source0, inv0, first0, east0, north0, inner0, outer0))
    source1, inv1, first1, east1, north1, inner1, outer1 = map(Wide, (source1, inv1, first1, east1, north1, inner1, outer1))
    source2, inv2, first2, east2, north2, inner2, outer2 = map(Wide, (source2, inv2, first2, east2, north2, inner2, outer2))
    work2, work1, work0a, work0b, va, vb, wa, wb = map(Wide, (work2, work1, work0a, work0b, va, vb, wa, wb))
    ua2, ub2, ua1, ub1 = map(Wide, (ua2, ub2, ua1, ub1))
    f32 = jnp.float32
    even = (position()[0] & 1) == 0
    size = 4 * TILES
    own, sib = mine[...], sibling[...]
    direct, relayed = received[...], passed_on[...]
    before, after = jnp.where(even, direct, relayed), jnp.where(even, relayed, direct)
    blocks = (
        before[size:], before[:size], jnp.where(even, own, sib), jnp.where(even, sib, own), after[:size], after[size:],
    )
    for slot, block in enumerate(blocks):
        for q in range(TILES):
            whole[q, 4 * slot : 4 * slot + 4] = block[4 * q : 4 * q + 4]
    own_f, own_s = sums_in[0:1, 0:1], sums_in[1:2, 0:1]
    guess = own_f / own_s
    g0, g1, h0, i30, i31, e30, e31, n30, n31, in3, out3 = [whole[q] for q in range(TILES)]
    inv3, e3, n3 = (i30, i31), (e30, e31), (n30, n31)
    odd3 = odd_cells((24, WIDE), 3)

    def beside3(c, u):
        t = e3[c] * row_next(u) + row_prev(e3[1 - c] * u)
        t = t + (n3[c] * lane_next(u, 8) + lane_prev(n3[1 - c] * u, 8)) + in3 * u
        above, below = out3 * lane_next(u, 1), lane_prev(out3 * u, 1)
        return t + (jnp.where(odd3, above, below) if c == 0 else jnp.where(odd3, below, above))

    a0, b0 = g0 + guess * h0, h0
    for _ in range(3):
        a1, b1 = g1 + beside3(1, a0) * inv3[1], beside3(1, b0) * inv3[1]
        a0, b0 = g0 + beside3(0, a1) * inv3[0], beside3(0, b1) * inv3[0]

    a0, a1, b0, b1 = [jnp.where(even, pltpu.roll(x, 19, 0), pltpu.roll(x, 15, 0))[:16] for x in (a0, a1, b0, b1)]
    dims3 = (16, WIDE)
    phase = iota(dims3, 1) & 7
    odd3 = odd_cells(dims3, 3, 1)
    second_half = lane_bit(dims3, 1)

    def spread(x, m):
        x = jnp.where(phase == 0, near_next(x, m) if m else x, 0.0)
        x = x + near_prev(x, 1)
        x = x + near_prev(x, 2)
        return x + near_prev(x, 4)

    for m in range(PAIRS):
        x0 = jnp.where(second_half, spread(b0, m), spread(a0, m))
        x1 = jnp.where(second_half, spread(b1, m), spread(a1, m))
        low, high = jnp.where(odd3, x1, x0)[:12], jnp.where(odd3, x0, x1)[:12]
        spread_rows(2, low, high, work2, m)

    def smooth(level, rows, coeffs, inverse, source, first, work, ones, zeros, half_bit):
        odd = odd_cells((rows, WIDE), level)
        is_b = lane_bit((rows, WIDE), half_bit)
        step = 1 << level
        for m in range(PAIRS):
            work[m] = work[m] + jnp.where(is_b, 0.0, first[m])
        for m in range(PAIRS):
            ones[m] = (jnp.where(is_b, 0.0, source[1, m]) + beside(1, work, coeffs, m, odd, step)) * inverse[1, m]
        for m in range(PAIRS):
            zeros[m] = jnp.where(is_b, 0.0, first[m]) + beside(0, ones, coeffs, m, odd, step) * inverse[0, m]

    smooth(2, ROWS2, (east2, north2, inner2, outer2), inv2, source2, first2, work2, ub2, ua2, 1)
    dims2 = (ROWS2, WIDE)
    odd2 = odd_cells(dims2, 2)
    bit1, bit0 = lane_bit(dims2, 1), lane_bit(dims2, 0)

    def regroup2(x):
        a = jnp.where(bit1, near_prev(x, 2), x)
        b = jnp.where(bit1, x, near_next(x, 2))
        return jnp.where(bit0, b, a)

    for m in range(PAIRS):
        x0, x1 = regroup2(ua2[m]), regroup2(ub2[m])
        low, high = jnp.where(odd2, x1, x0)[4:16], jnp.where(odd2, x0, x1)[4:16]
        spread_rows(1, low, high, work1, m)

    smooth(1, 24, (east1, north1, inner1, outer1), inv1, source1, first1, work1, ub1, ua1, 0)
    dims1 = (24, WIDE)
    odd1 = odd_cells(dims1, 1)
    bit0 = lane_bit(dims1, 0)
    for m in range(PAIRS):
        x0, x1 = ua1[m], ub1[m]
        low, high = jnp.where(odd1, x1, x0), jnp.where(odd1, x0, x1)
        for work, pick in (
            (work0a, lambda x: jnp.where(bit0, near_prev(x, 1), x)),
            (work0b, lambda x: jnp.where(bit0, x, near_next(x, 1))),
        ):
            spread_rows(0, pick(low), pick(high), work, m)

    rows = 48
    odd = odd_cells((rows, WIDE), 0)
    coeffs = (east0, north0, inner0, outer0)
    for m in range(PAIRS):
        work0a[m] = work0a[m] + first0[m]
    for m in range(PAIRS):
        va[m] = (source0[1, m] + beside(1, work0a, coeffs, m, odd, 1)) * inv0[1, m]
        vb[m] = beside(1, work0b, coeffs, m, odd, 1) * inv0[1, m]
    for m in range(PAIRS):
        wa[m] = first0[m] + beside(0, va, coeffs, m, odd, 1) * inv0[0, m]
        wb[m] = beside(0, vb, coeffs, m, odd, 1) * inv0[0, m]
    for m in range(PAIRS):
        work0a[m] = work0a[m] - wa[m]
        work0b[m] = work0b[m] - wb[m]
    acc = [jnp.zeros((ROWS, LANES), f32)] * 11

    def own(x):
        return x[8 : 8 + ROWS, :LANES]

    for m in range(PAIRS):
        change_a = own(beside(1, work0a, coeffs, m, odd, 1))
        img_b = own(beside(1, work0b, coeffs, m, odd, 1))
        r0, r1 = own(source0[0, m]), own(source0[1, m])
        p0, p1, q0, q1 = own(wa[m]), own(va[m]), own(wb[m]), own(vb[m])
        img_a = r1 + change_a
        d = -change_a
        terms = (
            r0 * p0 + r1 * p1, r0 * q0 + r1 * q1,
            r0 * p0 + img_a * p1, r0 * q0 + img_a * q1 + img_b * p1, img_b * q1,
            d * d, d * img_a, img_a * img_a + r0 * r0, d * img_b, img_a * img_b, img_b * img_b,
        )
        acc = [x + y for x, y in zip(acc, terms, strict=True)]
        for t, x in enumerate((p0, p1, q0, q1, r0, r1, img_a, img_b)):
            fields[t, m] = x
    lane = iota((1, LANES), 1)
    line = jnp.zeros((1, LANES), f32)
    for q, x in enumerate(acc):
        line = jnp.where(lane == q, jnp.sum(x, keepdims=True), line)
    line = jnp.where(lane == 11, own_f, line)
    line = jnp.where(lane == 12, own_s, line)
    line = jnp.where(lane == 13, guess, line)
    sums[...] = jnp.broadcast_to(line, sums.shape)


def last_kernel(sums, line, fields, solution_out, residual_out, norm_ref, solution_ref, residual_ref, sems, *, cells):
    x = jnp.concatenate([sums[:, :16], sums[:, 16:]], axis=0)

    def column(q):
        return x[:, q : q + 1]

    def total(v):
        return jnp.sum(v, axis=0, keepdims=True)

    rp, rq, pa, pb, qb, dd, da, aa, db, ab, bb = [column(q) for q in range(11)]
    mean = total(column(11)) / total(column(12))
    shift = mean - column(13)
    step = total(rp + shift * rq) / total(pa + shift * (pb + shift * qb))
    s, t = step - 1.0, step * shift
    squares = total(dd - 2.0 * s * da + s * s * aa - 2.0 * t * db + 2.0 * s * t * ab + t * t * bb)
    norm_ref[...] = jnp.sqrt(jnp.maximum(squares, 0.0) / cells)
    here = mean - line[0:1, 13:14]
    odd = odd_cells((ROWS, LANES), 0)
    copies = []
    for m in range(PAIRS):
        p0, p1, q0, q1, r0, r1, img_a, img_b = [fields[t, m] for t in range(8)]
        s0, s1 = step * (p0 + here * q0), step * (p1 + here * q1)
        n0, n1 = r0 - step * r0, r1 - step * (img_a + here * img_b)
        solution_ref[2 * m] = jnp.where(odd, s1, s0)
        solution_ref[2 * m + 1] = jnp.where(odd, s0, s1)
        residual_ref[2 * m] = jnp.where(odd, n1, n0)
        residual_ref[2 * m + 1] = jnp.where(odd, n0, n1)
        layers = pl.ds(2 * m, 2)
        for q, (ref, out) in enumerate(((solution_ref, solution_out), (residual_ref, residual_out))):
            copies.append(pltpu.make_async_copy(ref.at[layers], out.at[layers], sems.at[q, m]))
            copies[-1].start()
    for copy in copies:
        copy.wait()


def level_dims(rows):
    two, one, four = [(*lead, 2, rows, LANES) for lead in ((2, PAIRS), (PAIRS,), (PAIRS - 1,))]
    return two, one, four


def level_shapes(rows):
    two, one, four = [shape(*dims) for dims in level_dims(rows)]
    return two, two, one, two, two, one, four


def scratch(*dims):
    return pltpu.VMEM(dims, jnp.float32)


def pairs_of(count, first):
    return [(i, i + 1) for i in range(first, count - 1, 2)] + [(i + 1, i) for i in range(first, count - 1, 2)]


def pair_exchange(x, axis):
    count = lax.axis_size(axis)
    return [lax.ppermute(x_i, axis, pairs_of(count, first)) for first, x_i in enumerate(x)]


def shards(pressure, soil, vg_alpha, vg_n, sat_cond, storage, right_side):
    count_x, count_y = lax.axis_size("gx"), lax.axis_size("gy")
    block, slab = scratch(2 * PAIRS, ROWS, LANES), shape(6 * PAIRS, HALO, LANES)
    side, corner = shape(6, ROWS, LANES), shape(12, HALO, LANES)
    arguments = (pressure, soil, storage, right_side, *[v.reshape(1, NSOIL) for v in (vg_alpha, vg_n, sat_cond)])
    packed, *slabs = pl.pallas_call(
        first_kernel, out_shape=(shape(6 * PAIRS, ROWS, LANES), slab, slab, side, side),
        in_specs=[HBM] * 7, out_specs=(VM,) * 5,
        scratch_shapes=[
            block, pltpu.VMEM((2 * PAIRS, ROWS, LANES), jnp.int32), block, block, scratch(3, 1, NSOIL), pltpu.SemaphoreType.DMA((7,)),
        ],
        compiler_params=params(4), name="conductivity",
    )(*[pltpu.with_memory_space_constraint(v, pltpu.MemorySpace.HBM) for v in arguments])
    halos = pair_exchange(slabs[:2], "gx") + pair_exchange(slabs[2:], "gy")
    corners = pl.pallas_call(
        second_kernel, out_shape=(corner, corner), in_specs=[VM, VM], out_specs=(VM, VM), compiler_params=params(2), name="corners",
    )(*halos[2:])
    halos = halos + pair_exchange(corners, "gx")

    def sized(rows):
        return [scratch(*dims) for dims in level_dims(rows)]

    two, one, four = sized(EXT)
    two1, one1, four1 = sized(ROWS1)
    two2, one2, _ = sized(ROWS2)
    two3, one3, four3 = sized(16)
    out = pl.pallas_call(
        third_kernel,
        out_shape=(*level_shapes(48), *level_shapes(24), *level_shapes(ROWS2), shape(4 * TILES, LANES), shape(8, LANES)),
        in_specs=[VM] * 7, out_specs=(VM,) * 23,
        scratch_shapes=[
            two, two, two, two, two, one, four, two, one, one, one,
            two1, two1, two1, two1, one1, four1, two1, one1, one1, one1,
            two2, one2, one2,
            two3, two3, two3, two3, one3, four3,
        ],
        compiler_params=params(12), name="descent",
    )(packed, *halos)
    levels, tiles, sums = out[:21], out[21], out[22]

    tile_pair, tile_next = pair_exchange((tiles, tiles), "gy")
    window = pl.pallas_call(
        window_kernel, out_shape=shape(4 * TILES, WIDE), in_specs=[VM] * 3, out_specs=VM, compiler_params=params(2), name="window",
    )(tiles, tile_pair, tile_next)
    sibling = lax.ppermute(window, "gx", pairs_of(count_x, 0))
    both = pl.pallas_call(
        join_kernel, out_shape=shape(8 * TILES, WIDE), in_specs=[VM] * 2, out_specs=VM, compiler_params=params(2), name="join",
    )(window, sibling)
    received = lax.ppermute(both, "gx", pairs_of(count_x, 1))
    passed_on = lax.ppermute(received, "gx", pairs_of(count_x, 0))
    blocks = (window, sibling, received, passed_on)

    devices = count_x * count_y
    fields, line = pl.pallas_call(
        fourth_kernel,
        out_shape=(shape(8, PAIRS, ROWS, LANES), shape(8, LANES)),
        in_specs=[VM] * 26, out_specs=(VM, VM),
        scratch_shapes=[
            scratch(TILES, 24, WIDE), sized(ROWS2)[1], sized(24)[1],
            *[sized(48)[1]] * 6, *[sized(24)[1]] * 4,
        ],
        compiler_params=params(8), name="ascent",
    )(*blocks, sums, *levels)
    both = jnp.concatenate([line[:1, :16], lax.ppermute(line, "gx", pairs_of(count_x, 0))[:1, :16]], axis=1)
    kinds = [[x * count_y + y for x in range(c, count_x, 2) for y in range(count_y)] for c in range(2)]
    both = jnp.broadcast_to(both, (devices // 2, 32))
    every = lax.all_to_all(both, ("gx", "gy"), 0, 0, axis_index_groups=kinds, tiled=True)

    layers = 2 * PAIRS
    out = shape(layers, ROWS, LANES)
    solution_out, residual_out, norm = pl.pallas_call(
        functools.partial(last_kernel, cells=float(layers * ROWS * LANES * devices)),
        out_shape=(out, out, shape(1, 1)), in_specs=[VM, VM, VM], out_specs=(HBM, HBM, VM),
        scratch_shapes=[scratch(*out.shape), scratch(*out.shape), pltpu.SemaphoreType.DMA((2, PAIRS))],
        compiler_params=params(4), name="outputs",
    )(every, line, fields)
    return solution_out, residual_out, norm.reshape(1)


def solution(mesh):
    split, whole = P(None, "gx", "gy"), P()
    return jax.shard_map(
        shards, mesh=mesh, in_specs=(split, split, whole, whole, whole, split, split),
        out_specs=(split, split, whole), check_vma=False,
    )
```

```python
import functools

import jax
import jax.numpy as jnp
from jax import lax
from jax.experimental import pallas as pl
from jax.experimental.pallas import tpu as pltpu
from jax.sharding import PartitionSpec as P

NSOIL = 23
PAIRS = 5
HALO = 24
ROWS, LANES = 32, 128
EXT = ROWS + 2 * HALO
WIDE = 2 * LANES
ROWS1, ROWS2 = EXT // 2, 24
TILES = 11
MIB = 1 << 20


def iota(shape, dim):
    return lax.broadcasted_iota(jnp.int32, shape, dim)


def odd_cells(shape, level, start=0):
    return ((iota(shape, 0) + start + (iota(shape, 1) >> level)) & 1) == 1


def lane_bit(shape, level):
    return ((iota(shape, 1) >> level) & 1) == 1


def row_next(x):
    return pltpu.roll(x, x.shape[0] - 1, 0)


def row_prev(x):
    return pltpu.roll(x, 1, 0)


def lane_next(x, step):
    return pltpu.roll(x, x.shape[1] - step, 1)


def lane_prev(x, step):
    return pltpu.roll(x, step, 1)


def by_halves(f, x):
    return jnp.concatenate([f(x[:, start : start + LANES]) for start in range(0, x.shape[1], LANES)], axis=1)


def near_next(x, step):
    return by_halves(lambda h: lane_next(h, step), x)


def near_prev(x, step):
    return by_halves(lambda h: lane_prev(h, step), x)


def pair_sum(x, level):
    step = 1 << level
    return x + jnp.where(lane_bit(x.shape, level), near_prev(x, step), near_next(x, step))


def beside(c, u, coeffs, m, odd, step):
    east, north, inner, outer = coeffs
    um = u[m]
    t = east[c, m] * row_next(um) + row_prev(east[1 - c, m] * um)
    t = t + (north[c, m] * lane_next(um, step) + lane_prev(north[1 - c, m] * um, step))
    t = t + inner[m] * um
    above = outer[m] * u[m + 1] if m < PAIRS - 1 else 0.0
    below = outer[m - 1] * u[m - 1] if m > 0 else 0.0
    return t + (jnp.where(odd, above, below) if c == 0 else jnp.where(odd, below, above))


def position():
    return lax.axis_index("gx"), lax.axis_index("gy")


def params(limit):
    return pltpu.CompilerParams(vmem_limit_bytes=limit * MIB)


VM = pl.BlockSpec(memory_space=pltpu.VMEM)
HBM = pl.BlockSpec(memory_space=pltpu.MemorySpace.HBM)


def shape(*dims):
    return jax.ShapeDtypeStruct(dims, jnp.float32)


class Wide:
    def __init__(self, ref):
        self.ref, self.lead = ref, len(ref.shape) - 3

    def parts(self, ids):
        ids = ids if isinstance(ids, tuple) else (ids,)
        rows = ids[self.lead] if len(ids) > self.lead else slice(None)
        return [self.ref.at[(*ids[: self.lead], half)] for half in range(2)], rows

    def __getitem__(self, ids):
        refs, rows = self.parts(ids)
        return jnp.concatenate([ref[rows, :] for ref in refs], axis=1)

    def __setitem__(self, ids, x):
        refs, rows = self.parts(ids)
        for half, ref in enumerate(refs):
            ref[rows, :] = x[:, LANES * half : LANES * (half + 1)]


def first_kernel(
    pressure_in, soil_in, storage_in, source_in, alpha_in, power_in, saturated_in, packed, to_pair, to_next,
    pressure, soil, storage, source, table, sems,
):
    copies = [
        pltpu.make_async_copy(alpha_in, table.at[0], sems.at[4]),
        pltpu.make_async_copy(power_in, table.at[1], sems.at[5]),
        pltpu.make_async_copy(saturated_in, table.at[2], sems.at[6]),
        pltpu.make_async_copy(pressure_in, pressure, sems.at[0]),
        pltpu.make_async_copy(soil_in, soil, sems.at[1]),
        pltpu.make_async_copy(storage_in, storage, sems.at[2]),
        pltpu.make_async_copy(source_in, source, sems.at[3]),
    ]
    for copy in copies:
        copy.start()
    even_y = (position()[1] & 1) == 0
    odd = odd_cells((ROWS, LANES), 0)
    lane = iota((ROWS, LANES), 1)
    for copy in copies:
        copy.wait()
    rows = []
    for q in range(3):
        row = jnp.concatenate([table[q], jnp.ones((1, LANES - NSOIL), jnp.float32)], axis=1)
        rows.append(jnp.broadcast_to(jnp.log(row) if q == 0 else row, (8, LANES)))

    def look_up(row, ids):
        parts = [jnp.take_along_axis(row, ids[8 * b : 8 * b + 8], axis=1) for b in range(ROWS // 8)]
        return jnp.concatenate(parts, axis=0)

    def cond_of(k):
        ids = soil[k]
        log_scale, power, saturated = [look_up(r, ids) for r in rows]
        exponent = 1.0 - 1.0 / power
        log_s = power * (log_scale + jnp.log(jnp.abs(pressure[k])))
        log_1s = jnp.log(1.0 + jnp.exp(log_s))
        outer = 1.0 - jnp.exp(exponent * (log_s - log_1s))
        return saturated * jnp.exp(-0.5 * exponent * log_1s) * outer * outer

    def put(tile, m, x):
        t = tile * PAIRS + m
        packed[t] = x
        left = pltpu.roll(x, HALO * m, 1) if m else x
        right = pltpu.roll(x, (HALO * m - (LANES - HALO)) % LANES, 1)
        for ref, y in ((to_pair, jnp.where(even_y, right, left)), (to_next, jnp.where(even_y, left, right))):
            ref[tile] = y if m == 0 else jnp.where(lane >= HALO * m, y, ref[tile])

    for m in range(PAIRS):
        triples = (
            (cond_of(2 * m), cond_of(2 * m + 1)),
            (storage[2 * m], storage[2 * m + 1]),
            (source[2 * m], source[2 * m + 1]),
        )
        for q, (a, b) in enumerate(triples):
            put(2 * q, m, jnp.where(odd, b, a))
            put(2 * q + 1, m, jnp.where(odd, a, b))


def edge_kernel(packed, to_sibling, to_other):
    even = (position()[0] & 1) == 0
    for t in range(6 * PAIRS):
        high, low = packed[t, ROWS - HALO :], packed[t, :HALO]
        to_sibling[t] = jnp.where(even, high, low)
        to_other[t] = jnp.where(even, low, high)


def second_kernel(from_pair, from_next, to_sibling, to_other):
    even = (position()[0] & 1) == 0
    for q, ref in enumerate((from_pair, from_next)):
        for tile in range(6):
            high, low = ref[tile, ROWS - HALO :], ref[tile, :HALO]
            to_sibling[6 * q + tile] = jnp.where(even, high, low)
            to_other[6 * q + tile] = jnp.where(even, low, high)


def coarsen_level(level, fine_rows, out_rows, fine, coarse):
    stor, east, north, inner, outer = fine
    cstor, ceast, cnorth, cinner, couter = coarse
    half = fine_rows // 2
    dims = (half, WIDE)
    bit = lane_bit(dims, level)
    odd = odd_cells(dims, level + 1, 1 if level == 2 else 0)
    step = 1 << level

    def even_rows(ref, *ids):
        return ref[(*ids, pl.ds(0, half, stride=2))]

    def odd_rows(ref, *ids):
        return ref[(*ids, pl.ds(1, half, stride=2))]

    swap = bit ^ odd

    def put(ref, m, a, b):
        ref[0, m, slice(0, half)] = a
        ref[1, m, slice(0, half)] = b

    for m in range(PAIRS):
        u = even_rows(stor, 0, m) + odd_rows(stor, 1, m)
        v = even_rows(stor, 1, m) + odd_rows(stor, 0, m)
        put(cstor, m, pair_sum(jnp.where(swap, v, u), level), pair_sum(jnp.where(swap, u, v), level))
        e0, e1 = odd_rows(east, 0, m), odd_rows(east, 1, m)
        put(ceast, m, pair_sum(jnp.where(swap, e0, e1), level), pair_sum(jnp.where(swap, e1, e0), level))
        low = even_rows(north, 1, m) + odd_rows(north, 0, m)
        high = even_rows(north, 0, m) + odd_rows(north, 1, m)
        a, b = jnp.where(odd, high, low), jnp.where(odd, low, high)
        put(cnorth, m, jnp.where(bit, a, near_next(a, step)), jnp.where(bit, b, near_next(b, step)))
        cinner[m, slice(0, half)] = pair_sum(even_rows(inner, m) + odd_rows(inner, m), level)
        if m < PAIRS - 1:
            couter[m, slice(0, half)] = pair_sum(even_rows(outer, m) + odd_rows(outer, m), level)


def restrict_level(level, fine_rows, residual, coarse_source):
    half = fine_rows // 2
    dims = (half, WIDE)
    bit = lane_bit(dims, level)
    odd = odd_cells(dims, level + 1, 1 if level == 2 else 0)
    swap = bit ^ odd
    for m in range(PAIRS):
        a = residual[m, pl.ds(0, half, stride=2)]
        b = residual[m, pl.ds(1, half, stride=2)]
        coarse_source[0, m, slice(0, half)] = pair_sum(jnp.where(swap, b, a), level)
        coarse_source[1, m, slice(0, half)] = pair_sum(jnp.where(swap, a, b), level)


def invert_diagonal(level, rows, coeffs, inverse):
    stor, east, north, inner, outer = coeffs
    odd = odd_cells((rows, WIDE), level)
    step = 1 << level
    for m in range(PAIRS):
        above = outer[m] if m < PAIRS - 1 else 0.0
        below = outer[m - 1] if m > 0 else 0.0
        for c in range(2):
            diag = stor[c, m] + east[c, m] + row_prev(east[1 - c, m]) + north[c, m]
            diag = diag + lane_prev(north[1 - c, m], step) + inner[m]
            diag = diag + (jnp.where(odd, above, below) if c == 0 else jnp.where(odd, below, above))
            inverse[c, m] = 1.0 / diag


def descend_level(level, rows, coeffs, inverse, source, first, second, residual):
    odd = odd_cells((rows, WIDE), level)
    step = 1 << level
    for m in range(PAIRS):
        first[m] = source[0, m] * inverse[0, m]
    for m in range(PAIRS):
        second[m] = (source[1, m] + beside(1, first, coeffs[1:], m, odd, step)) * inverse[1, m]
    for m in range(PAIRS):
        residual[m] = beside(0, second, coeffs[1:], m, odd, step)


def third_kernel(
    packed, from_sibling, from_other, from_pair, from_next, corner_sibling, corner_other,
    source0, inv0, first0, east0, north0, inner0, outer0,
    source1, inv1, first1, east1, north1, inner1, outer1,
    source2, inv2, first2, east2, north2, inner2, outer2,
    tiles, sums,
    cond, stor, src, east, north, inner, outer, inv, first, second, residual,
    stor1, src1, e1, n1, in1, out1, i1, f1, s1, r1,
    stor2, s2, r2,
    stor3, src3, e3, n3, in3, out3,
):
    source0, inv0, first0, east0, north0, inner0, outer0 = map(Wide, (source0, inv0, first0, east0, north0, inner0, outer0))
    source1, inv1, first1, east1, north1, inner1, outer1 = map(Wide, (source1, inv1, first1, east1, north1, inner1, outer1))
    source2, inv2, first2, east2, north2, inner2, outer2 = map(Wide, (source2, inv2, first2, east2, north2, inner2, outer2))
    cond, stor, src, east, north, inner, outer = map(Wide, (cond, stor, src, east, north, inner, outer))
    inv, first, second, residual = map(Wide, (inv, first, second, residual))
    stor1, src1, e1, n1, in1, out1, i1, f1, s1, r1 = map(Wide, (stor1, src1, e1, n1, in1, out1, i1, f1, s1, r1))
    stor2, s2, r2 = map(Wide, (stor2, s2, r2))
    stor3, src3, e3, n3, in3, out3 = map(Wide, (stor3, src3, e3, n3, in3, out3))
    gx, gy = position()
    even_x, even_y = (gx & 1) == 0, (gy & 1) == 0
    lane = iota((EXT, LANES), 1)

    def rows_of(sib, oth, own):
        return jnp.concatenate([jnp.where(even_x, oth, sib), own, jnp.where(even_x, sib, oth)], axis=0)

    for tile in range(6):
        pair, other = [
            rows_of(corner_sibling[q + tile], corner_other[q + tile], ref[tile]) for q, ref in ((0, from_pair), (6, from_next))
        ]
        right = jnp.where(even_y, pair, other)
        left = jnp.where(even_y, other, pair)
        ref = (cond, stor, src)[tile // 2]
        for m in range(PAIRS):
            t = tile * PAIRS + m
            x = rows_of(from_sibling[t], from_other[t], packed[t])
            r = pltpu.roll(right, (-HALO * m) % LANES, 1) if m else right
            l = pltpu.roll(left, (LANES - HALO - HALO * m) % LANES, 1)
            h = jnp.where(lane < HALO, r, jnp.where(lane >= LANES - HALO, l, 0.0))
            if tile // 2 == 1:
                x, h = jnp.where(x == 0.0, 1.0, x), jnp.where(h == 0.0, 1.0, h)
            ref.ref[tile % 2, m, 0] = x
            ref.ref[tile % 2, m, 1] = h

    dims = (EXT, WIDE)
    odd = odd_cells(dims, 0)
    row, column = iota(dims, 0), iota(dims, 1)
    last_row = (row == HALO + ROWS - 1) & (gx == lax.axis_size("gx") - 1)
    before_row = (row == HALO - 1) & (gx == 0)
    keep_x = jnp.where(last_row | before_row, 0.0, 0.5)
    last_column = (column == LANES - 1) & (gy == lax.axis_size("gy") - 1)
    before_column = (column == WIDE - 1) & (gy == 0)
    keep_y = jnp.where(last_column | before_column, 0.0, 0.5)
    for m in range(PAIRS):
        a, b = cond[0, m], cond[1, m]
        east[0, m] = (a + row_next(b)) * keep_x
        east[1, m] = (b + row_next(a)) * keep_x
        north[0, m] = (a + lane_next(b, 1)) * keep_y
        north[1, m] = (b + lane_next(a, 1)) * keep_y
        inner[m] = a + b
        if m < PAIRS - 1:
            outer[m] = jnp.where(odd, a + cond[1, m + 1], b + cond[0, m + 1])

    level0 = (stor, east, north, inner, outer)
    level1 = (stor1, e1, n1, in1, out1)
    level2 = (stor2, east2, north2, inner2, outer2)
    level3 = (stor3, e3, n3, in3, out3)
    invert_diagonal(0, EXT, level0, inv)
    descend_level(0, EXT, level0, inv, src, first, second, residual)

    coarsen_level(0, EXT, ROWS1, level0, level1)
    restrict_level(0, EXT, residual, src1)
    invert_diagonal(1, ROWS1, level1, i1)
    descend_level(1, ROWS1, level1, i1, src1, f1, s1, r1)

    half = ROWS1 // 2
    for ref in (source2, east2, north2, inner2, outer2):
        ref.ref[..., half:, :] = jnp.zeros((*ref.ref.shape[:-2], ROWS2 - half, LANES), jnp.float32)
    stor2.ref[..., half:, :] = jnp.ones((2, PAIRS, 2, ROWS2 - half, LANES), jnp.float32)
    coarsen_level(1, ROWS1, ROWS2, level1, level2)
    restrict_level(1, ROWS1, r1, source2)
    invert_diagonal(2, ROWS2, level2, inv2)
    descend_level(2, ROWS2, level2, inv2, source2, first2, s2, r2)

    coarsen_level(2, ROWS2, 16, level2, level3)
    restrict_level(2, ROWS2, r2, src3)

    dims3 = (16, WIDE)
    odd3 = odd_cells(dims3, 3, 1)
    phase = iota((4, LANES), 1) & 7
    total_f, total_s = 0.0, 0.0
    compact = [None] * TILES
    for m in range(PAIRS):
        above = out3[m] if m < PAIRS - 1 else 0.0
        below = out3[m - 1] if m > 0 else 0.0
        invs = []
        for c in range(2):
            diag = stor3[c, m] + e3[c, m] + row_prev(e3[1 - c, m]) + n3[c, m]
            diag = diag + lane_prev(n3[1 - c, m], 8) + in3[m]
            diag = diag + (jnp.where(odd3, above, below) if c == 0 else jnp.where(odd3, below, above))
            invs.append(1.0 / diag)
            total_f = total_f + src3[c, m][3:7, :LANES]
            total_s = total_s + stor3[c, m][3:7, :LANES]
        values = (
            src3[0, m] * invs[0], src3[1, m] * invs[1], 1.0 - stor3[0, m] * invs[0], invs[0], invs[1],
            e3[0, m], e3[1, m], n3[0, m], n3[1, m], in3[m], out3[m] if m < PAIRS - 1 else jnp.zeros(dims3, jnp.float32),
        )
        for q, value in enumerate(values):
            own = value[3:7, :LANES]
            compact[q] = jnp.where(phase == m, own, 0.0 if m == 0 else compact[q])
    for q in range(TILES):
        tiles[4 * q : 4 * q + 4] = compact[q]
    sums[0:1] = jnp.broadcast_to(jnp.sum(total_f, keepdims=True), (1, LANES)) * 0.125
    sums[1:2] = jnp.broadcast_to(jnp.sum(total_s, keepdims=True), (1, LANES)) * 0.125

    for m in range(PAIRS):
        for c in range(2):
            for to, of in ((source0, src), (inv0, inv), (east0, east), (north0, north)):
                to[c, m] = of[c, m, slice(16, 64)]
            for to, of in ((source1, src1), (inv1, i1), (east1, e1), (north1, n1)):
                to[c, m] = of[c, m, slice(8, 32)]
        first0[m], first1[m] = first[m, slice(16, 64)], f1[m, slice(8, 32)]
        inner0[m], inner1[m] = inner[m, slice(16, 64)], in1[m, slice(8, 32)]
        if m < PAIRS - 1:
            outer0[m], outer1[m] = outer[m, slice(16, 64)], out1[m, slice(8, 32)]


def window_kernel(tiles, from_pair, from_next, window):
    even = (position()[1] & 1) == 0
    window[:, :LANES] = tiles[...]
    a, b = from_pair[...], from_next[...]
    right_first = (iota(a.shape, 1) < LANES // 2) == even
    window[:, LANES:] = jnp.where(right_first, a, b)


def spread_rows(level, low, high, into, m):
    rows = low.shape[0]
    bit = lane_bit(low.shape, level)
    into[m, pl.ds(0, rows, stride=2)] = jnp.where(bit, high, low)
    into[m, pl.ds(1, rows, stride=2)] = jnp.where(bit, low, high)


def join_kernel(mine, sibling, both):
    both[: 4 * TILES] = mine[...]
    both[4 * TILES :] = sibling[...]


def fourth_kernel(
    mine, sibling, received, passed_on, sums_in,
    source0, inv0, first0, east0, north0, inner0, outer0,
    source1, inv1, first1, east1, north1, inner1, outer1,
    source2, inv2, first2, east2, north2, inner2, outer2,
    fields, sums,
    whole, work2, work1, work0a, work0b, va, vb, wa, wb,
    ua2, ub2, ua1, ub1,
):
    source0, inv0, first0, east0, north0, inner0, outer0 = map(Wide, (source0, inv0, first0, east0, north0, inner0, outer0))
    source1, inv1, first1, east1, north1, inner1, outer1 = map(Wide, (source1, inv1, first1, east1, north1, inner1, outer1))
    source2, inv2, first2, east2, north2, inner2, outer2 = map(Wide, (source2, inv2, first2, east2, north2, inner2, outer2))
    work2, work1, work0a, work0b, va, vb, wa, wb = map(Wide, (work2, work1, work0a, work0b, va, vb, wa, wb))
    ua2, ub2, ua1, ub1 = map(Wide, (ua2, ub2, ua1, ub1))
    f32 = jnp.float32
    even = (position()[0] & 1) == 0
    size = 4 * TILES
    own, sib = mine[...], sibling[...]
    direct, relayed = received[...], passed_on[...]
    before, after = jnp.where(even, direct, relayed), jnp.where(even, relayed, direct)
    blocks = (
        before[size:], before[:size], jnp.where(even, own, sib), jnp.where(even, sib, own), after[:size], after[size:],
    )
    for slot, block in enumerate(blocks):
        for q in range(TILES):
            whole[q, 4 * slot : 4 * slot + 4] = block[4 * q : 4 * q + 4]
    own_f, own_s = sums_in[0:1, 0:1], sums_in[1:2, 0:1]
    guess = own_f / own_s
    g0, g1, h0, i30, i31, e30, e31, n30, n31, in3, out3 = [whole[q] for q in range(TILES)]
    inv3, e3, n3 = (i30, i31), (e30, e31), (n30, n31)
    odd3 = odd_cells((24, WIDE), 3)

    def beside3(c, u):
        t = e3[c] * row_next(u) + row_prev(e3[1 - c] * u)
        t = t + (n3[c] * lane_next(u, 8) + lane_prev(n3[1 - c] * u, 8)) + in3 * u
        above, below = out3 * lane_next(u, 1), lane_prev(out3 * u, 1)
        return t + (jnp.where(odd3, above, below) if c == 0 else jnp.where(odd3, below, above))

    a0, b0 = g0 + guess * h0, h0
    for _ in range(3):
        a1, b1 = g1 + beside3(1, a0) * inv3[1], beside3(1, b0) * inv3[1]
        a0, b0 = g0 + beside3(0, a1) * inv3[0], beside3(0, b1) * inv3[0]

    a0, a1, b0, b1 = [jnp.where(even, pltpu.roll(x, 19, 0), pltpu.roll(x, 15, 0))[:16] for x in (a0, a1, b0, b1)]
    dims3 = (16, WIDE)
    phase = iota(dims3, 1) & 7
    odd3 = odd_cells(dims3, 3, 1)
    second_half = lane_bit(dims3, 1)

    def spread(x, m):
        x = jnp.where(phase == 0, near_next(x, m) if m else x, 0.0)
        x = x + near_prev(x, 1)
        x = x + near_prev(x, 2)
        return x + near_prev(x, 4)

    for m in range(PAIRS):
        x0 = jnp.where(second_half, spread(b0, m), spread(a0, m))
        x1 = jnp.where(second_half, spread(b1, m), spread(a1, m))
        low, high = jnp.where(odd3, x1, x0)[:12], jnp.where(odd3, x0, x1)[:12]
        spread_rows(2, low, high, work2, m)

    def smooth(level, rows, coeffs, inverse, source, first, work, ones, zeros, half_bit):
        odd = odd_cells((rows, WIDE), level)
        is_b = lane_bit((rows, WIDE), half_bit)
        step = 1 << level
        for m in range(PAIRS):
            work[m] = work[m] + jnp.where(is_b, 0.0, first[m])
        for m in range(PAIRS):
            ones[m] = (jnp.where(is_b, 0.0, source[1, m]) + beside(1, work, coeffs, m, odd, step)) * inverse[1, m]
        for m in range(PAIRS):
            zeros[m] = jnp.where(is_b, 0.0, first[m]) + beside(0, ones, coeffs, m, odd, step) * inverse[0, m]

    smooth(2, ROWS2, (east2, north2, inner2, outer2), inv2, source2, first2, work2, ub2, ua2, 1)
    dims2 = (ROWS2, WIDE)
    odd2 = odd_cells(dims2, 2)
    bit1, bit0 = lane_bit(dims2, 1), lane_bit(dims2, 0)

    def regroup2(x):
        a = jnp.where(bit1, near_prev(x, 2), x)
        b = jnp.where(bit1, x, near_next(x, 2))
        return jnp.where(bit0, b, a)

    for m in range(PAIRS):
        x0, x1 = regroup2(ua2[m]), regroup2(ub2[m])
        low, high = jnp.where(odd2, x1, x0)[4:16], jnp.where(odd2, x0, x1)[4:16]
        spread_rows(1, low, high, work1, m)

    smooth(1, 24, (east1, north1, inner1, outer1), inv1, source1, first1, work1, ub1, ua1, 0)
    dims1 = (24, WIDE)
    odd1 = odd_cells(dims1, 1)
    bit0 = lane_bit(dims1, 0)
    for m in range(PAIRS):
        x0, x1 = ua1[m], ub1[m]
        low, high = jnp.where(odd1, x1, x0), jnp.where(odd1, x0, x1)
        for work, pick in (
            (work0a, lambda x: jnp.where(bit0, near_prev(x, 1), x)),
            (work0b, lambda x: jnp.where(bit0, x, near_next(x, 1))),
        ):
            spread_rows(0, pick(low), pick(high), work, m)

    rows = 48
    odd = odd_cells((rows, WIDE), 0)
    coeffs = (east0, north0, inner0, outer0)
    for m in range(PAIRS):
        work0a[m] = work0a[m] + first0[m]
    for m in range(PAIRS):
        va[m] = (source0[1, m] + beside(1, work0a, coeffs, m, odd, 1)) * inv0[1, m]
        vb[m] = beside(1, work0b, coeffs, m, odd, 1) * inv0[1, m]
    for m in range(PAIRS):
        wa[m] = first0[m] + beside(0, va, coeffs, m, odd, 1) * inv0[0, m]
        wb[m] = beside(0, vb, coeffs, m, odd, 1) * inv0[0, m]
    for m in range(PAIRS):
        work0a[m] = work0a[m] - wa[m]
        work0b[m] = work0b[m] - wb[m]
    acc = [jnp.zeros((ROWS, LANES), f32)] * 11

    def own(x):
        return x[8 : 8 + ROWS, :LANES]

    for m in range(PAIRS):
        change_a = own(beside(1, work0a, coeffs, m, odd, 1))
        img_b = own(beside(1, work0b, coeffs, m, odd, 1))
        r0, r1 = own(source0[0, m]), own(source0[1, m])
        p0, p1, q0, q1 = own(wa[m]), own(va[m]), own(wb[m]), own(vb[m])
        img_a = r1 + change_a
        d = -change_a
        terms = (
            r0 * p0 + r1 * p1, r0 * q0 + r1 * q1,
            r0 * p0 + img_a * p1, r0 * q0 + img_a * q1 + img_b * p1, img_b * q1,
            d * d, d * img_a, img_a * img_a + r0 * r0, d * img_b, img_a * img_b, img_b * img_b,
        )
        acc = [x + y for x, y in zip(acc, terms, strict=True)]
        for t, x in enumerate((p0, p1, q0, q1, r0, r1, img_a, img_b)):
            fields[t, m] = x
    lane = iota((1, LANES), 1)
    line = jnp.zeros((1, LANES), f32)
    for q, x in enumerate(acc):
        line = jnp.where(lane == q, jnp.sum(x, keepdims=True), line)
    line = jnp.where(lane == 11, own_f, line)
    line = jnp.where(lane == 12, own_s, line)
    line = jnp.where(lane == 13, guess, line)
    sums[...] = jnp.broadcast_to(line, sums.shape)


def last_kernel(sums, line, fields, solution_out, residual_out, norm_ref, solution_ref, residual_ref, sems, *, cells):
    x = jnp.concatenate([sums[:, :16], sums[:, 16:]], axis=0)

    def column(q):
        return x[:, q : q + 1]

    def total(v):
        return jnp.sum(v, axis=0, keepdims=True)

    rp, rq, pa, pb, qb, dd, da, aa, db, ab, bb = [column(q) for q in range(11)]
    mean = total(column(11)) / total(column(12))
    shift = mean - column(13)
    step = total(rp + shift * rq) / total(pa + shift * (pb + shift * qb))
    s, t = step - 1.0, step * shift
    squares = total(dd - 2.0 * s * da + s * s * aa - 2.0 * t * db + 2.0 * s * t * ab + t * t * bb)
    norm_ref[...] = jnp.sqrt(jnp.maximum(squares, 0.0) / cells)
    here = mean - line[0:1, 13:14]
    odd = odd_cells((ROWS, LANES), 0)
    copies = []
    for m in range(PAIRS):
        p0, p1, q0, q1, r0, r1, img_a, img_b = [fields[t, m] for t in range(8)]
        s0, s1 = step * (p0 + here * q0), step * (p1 + here * q1)
        n0, n1 = r0 - step * r0, r1 - step * (img_a + here * img_b)
        solution_ref[2 * m] = jnp.where(odd, s1, s0)
        solution_ref[2 * m + 1] = jnp.where(odd, s0, s1)
        residual_ref[2 * m] = jnp.where(odd, n1, n0)
        residual_ref[2 * m + 1] = jnp.where(odd, n0, n1)
        layers = pl.ds(2 * m, 2)
        for q, (ref, out) in enumerate(((solution_ref, solution_out), (residual_ref, residual_out))):
            copies.append(pltpu.make_async_copy(ref.at[layers], out.at[layers], sems.at[q, m]))
            copies[-1].start()
    for copy in copies:
        copy.wait()


def level_dims(rows):
    two, one, four = [(*lead, 2, rows, LANES) for lead in ((2, PAIRS), (PAIRS,), (PAIRS - 1,))]
    return two, one, four


def level_shapes(rows):
    two, one, four = [shape(*dims) for dims in level_dims(rows)]
    return two, two, one, two, two, one, four


def scratch(*dims):
    return pltpu.VMEM(dims, jnp.float32)


def pairs_of(count, first):
    return [(i, i + 1) for i in range(first, count - 1, 2)] + [(i + 1, i) for i in range(first, count - 1, 2)]


def pair_exchange(x, axis):
    count = lax.axis_size(axis)
    return [lax.ppermute(x_i, axis, pairs_of(count, first)) for first, x_i in enumerate(x)]


def shards(pressure, soil, vg_alpha, vg_n, sat_cond, storage, right_side):
    count_x, count_y = lax.axis_size("gx"), lax.axis_size("gy")
    block, slab = scratch(2 * PAIRS, ROWS, LANES), shape(6 * PAIRS, HALO, LANES)
    side, corner = shape(6, ROWS, LANES), shape(12, HALO, LANES)
    arguments = (pressure, soil, storage, right_side, *[v.reshape(1, NSOIL) for v in (vg_alpha, vg_n, sat_cond)])
    packed, *sides = pl.pallas_call(
        first_kernel, out_shape=(shape(6 * PAIRS, ROWS, LANES), side, side),
        in_specs=[HBM] * 7, out_specs=(VM,) * 3,
        scratch_shapes=[
            block, pltpu.VMEM((2 * PAIRS, ROWS, LANES), jnp.int32), block, block, scratch(3, 1, NSOIL), pltpu.SemaphoreType.DMA((7,)),
        ],
        compiler_params=params(4), name="conductivity",
    )(*[pltpu.with_memory_space_constraint(v, pltpu.MemorySpace.HBM) for v in arguments])
    beside_y = pair_exchange(sides, "gy")
    slabs = pl.pallas_call(
        edge_kernel, out_shape=(slab, slab), in_specs=[VM], out_specs=(VM, VM), compiler_params=params(2), name="edges",
    )(packed)
    halos = pair_exchange(slabs, "gx") + beside_y
    corners = pl.pallas_call(
        second_kernel, out_shape=(corner, corner), in_specs=[VM, VM], out_specs=(VM, VM), compiler_params=params(2), name="corners",
    )(*beside_y)
    halos = halos + pair_exchange(corners, "gx")

    def sized(rows):
        return [scratch(*dims) for dims in level_dims(rows)]

    two, one, four = sized(EXT)
    two1, one1, four1 = sized(ROWS1)
    two2, one2, _ = sized(ROWS2)
    two3, one3, four3 = sized(16)
    out = pl.pallas_call(
        third_kernel,
        out_shape=(*level_shapes(48), *level_shapes(24), *level_shapes(ROWS2), shape(4 * TILES, LANES), shape(8, LANES)),
        in_specs=[VM] * 7, out_specs=(VM,) * 23,
        scratch_shapes=[
            two, two, two, two, two, one, four, two, one, one, one,
            two1, two1, two1, two1, one1, four1, two1, one1, one1, one1,
            two2, one2, one2,
            two3, two3, two3, two3, one3, four3,
        ],
        compiler_params=params(12), name="descent",
    )(packed, *halos)
    levels, tiles, sums = out[:21], out[21], out[22]

    tile_pair, tile_next = pair_exchange((tiles, tiles), "gy")
    window = pl.pallas_call(
        window_kernel, out_shape=shape(4 * TILES, WIDE), in_specs=[VM] * 3, out_specs=VM, compiler_params=params(2), name="window",
    )(tiles, tile_pair, tile_next)
    sibling = lax.ppermute(window, "gx", pairs_of(count_x, 0))
    both = pl.pallas_call(
        join_kernel, out_shape=shape(8 * TILES, WIDE), in_specs=[VM] * 2, out_specs=VM, compiler_params=params(2), name="join",
    )(window, sibling)
    received = lax.ppermute(both, "gx", pairs_of(count_x, 1))
    passed_on = lax.ppermute(received, "gx", pairs_of(count_x, 0))
    blocks = (window, sibling, received, passed_on)

    devices = count_x * count_y
    fields, line = pl.pallas_call(
        fourth_kernel,
        out_shape=(shape(8, PAIRS, ROWS, LANES), shape(8, LANES)),
        in_specs=[VM] * 26, out_specs=(VM, VM),
        scratch_shapes=[
            scratch(TILES, 24, WIDE), sized(ROWS2)[1], sized(24)[1],
            *[sized(48)[1]] * 6, *[sized(24)[1]] * 4,
        ],
        compiler_params=params(8), name="ascent",
    )(*blocks, sums, *levels)
    both = jnp.concatenate([line[:1, :16], lax.ppermute(line, "gx", pairs_of(count_x, 0))[:1, :16]], axis=1)
    kinds = [[x * count_y + y for x in range(c, count_x, 2) for y in range(count_y)][::-1] for c in range(2)]
    both = jnp.broadcast_to(both, (devices // 2, 32))
    every = lax.all_to_all(both, ("gx", "gy"), 0, 0, axis_index_groups=kinds, tiled=True)

    layers = 2 * PAIRS
    out = shape(layers, ROWS, LANES)
    solution_out, residual_out, norm = pl.pallas_call(
        functools.partial(last_kernel, cells=float(layers * ROWS * LANES * devices)),
        out_shape=(out, out, shape(1, 1)), in_specs=[VM, VM, VM], out_specs=(HBM, HBM, VM),
        scratch_shapes=[scratch(*out.shape), scratch(*out.shape), pltpu.SemaphoreType.DMA((2, PAIRS))],
        compiler_params=params(4), name="outputs",
    )(every, line, fields)
    return solution_out, residual_out, norm.reshape(1)


def solution(mesh):
    split, whole = P(None, "gx", "gy"), P()
    return jax.shard_map(
        shards, mesh=mesh, in_specs=(split, split, whole, whole, whole, split, split),
        out_specs=(split, split, whole), check_vma=False,
    )
```

```python
import functools

import jax
import jax.numpy as jnp
from jax import lax
from jax.experimental import pallas as pl
from jax.experimental.pallas import tpu as pltpu
from jax.sharding import PartitionSpec as P

NSOIL = 23
PAIRS = 5
HALO = 24
ROWS, LANES = 32, 128
EXT = ROWS + 2 * HALO
WIDE = 2 * LANES
ROWS1, ROWS2 = EXT // 2, 24
TILES = 11
MIB = 1 << 20


def iota(shape, dim):
    return lax.broadcasted_iota(jnp.int32, shape, dim)


def odd_cells(shape, level, start=0):
    return ((iota(shape, 0) + start + (iota(shape, 1) >> level)) & 1) == 1


def lane_bit(shape, level):
    return ((iota(shape, 1) >> level) & 1) == 1


def row_next(x):
    return pltpu.roll(x, x.shape[0] - 1, 0)


def row_prev(x):
    return pltpu.roll(x, 1, 0)


def lane_next(x, step):
    return pltpu.roll(x, x.shape[1] - step, 1)


def lane_prev(x, step):
    return pltpu.roll(x, step, 1)


def by_halves(f, x):
    return jnp.concatenate([f(x[:, start : start + LANES]) for start in range(0, x.shape[1], LANES)], axis=1)


def near_next(x, step):
    return by_halves(lambda h: lane_next(h, step), x)


def near_prev(x, step):
    return by_halves(lambda h: lane_prev(h, step), x)


def pair_sum(x, level):
    step = 1 << level
    return x + jnp.where(lane_bit(x.shape, level), near_prev(x, step), near_next(x, step))


def beside(c, u, coeffs, m, odd, step):
    east, north, inner, outer = coeffs
    um = u[m]
    t = east[c, m] * row_next(um) + row_prev(east[1 - c, m] * um)
    t = t + (north[c, m] * lane_next(um, step) + lane_prev(north[1 - c, m] * um, step))
    t = t + inner[m] * um
    above = outer[m] * u[m + 1] if m < PAIRS - 1 else 0.0
    below = outer[m - 1] * u[m - 1] if m > 0 else 0.0
    return t + (jnp.where(odd, above, below) if c == 0 else jnp.where(odd, below, above))


def position():
    return lax.axis_index("gx"), lax.axis_index("gy")


def params(limit):
    return pltpu.CompilerParams(vmem_limit_bytes=limit * MIB)


VM = pl.BlockSpec(memory_space=pltpu.VMEM)
HBM = pl.BlockSpec(memory_space=pltpu.MemorySpace.HBM)


def shape(*dims):
    return jax.ShapeDtypeStruct(dims, jnp.float32)


class Wide:
    def __init__(self, ref):
        self.ref, self.lead = ref, len(ref.shape) - 3

    def parts(self, ids):
        ids = ids if isinstance(ids, tuple) else (ids,)
        rows = ids[self.lead] if len(ids) > self.lead else slice(None)
        return [self.ref.at[(*ids[: self.lead], half)] for half in range(2)], rows

    def __getitem__(self, ids):
        refs, rows = self.parts(ids)
        return jnp.concatenate([ref[rows, :] for ref in refs], axis=1)

    def __setitem__(self, ids, x):
        refs, rows = self.parts(ids)
        for half, ref in enumerate(refs):
            ref[rows, :] = x[:, LANES * half : LANES * (half + 1)]


def first_kernel(
    pressure_in, soil_in, storage_in, source_in, alpha_in, power_in, saturated_in, packed, to_pair, to_next,
    pressure, soil, storage, source, table, sems,
):
    copies = [
        pltpu.make_async_copy(alpha_in, table.at[0], sems.at[4]),
        pltpu.make_async_copy(power_in, table.at[1], sems.at[5]),
        pltpu.make_async_copy(saturated_in, table.at[2], sems.at[6]),
        pltpu.make_async_copy(pressure_in, pressure, sems.at[0]),
        pltpu.make_async_copy(soil_in, soil, sems.at[1]),
        pltpu.make_async_copy(storage_in, storage, sems.at[2]),
        pltpu.make_async_copy(source_in, source, sems.at[3]),
    ]
    for copy in copies:
        copy.start()
    even_y = (position()[1] & 1) == 0
    odd = odd_cells((ROWS, LANES), 0)
    lane = iota((ROWS, LANES), 1)
    for copy in copies:
        copy.wait()
    rows = []
    for q in range(3):
        row = jnp.concatenate([table[q], jnp.ones((1, LANES - NSOIL), jnp.float32)], axis=1)
        rows.append(jnp.broadcast_to(jnp.log(row) if q == 0 else row, (8, LANES)))

    def look_up(row, ids):
        parts = [jnp.take_along_axis(row, ids[8 * b : 8 * b + 8], axis=1) for b in range(ROWS // 8)]
        return jnp.concatenate(parts, axis=0)

    def cond_of(k):
        ids = soil[k]
        log_scale, power, saturated = [look_up(r, ids) for r in rows]
        exponent = 1.0 - 1.0 / power
        log_s = power * (log_scale + jnp.log(jnp.abs(pressure[k])))
        log_1s = jnp.log(1.0 + jnp.exp(log_s))
        outer = 1.0 - jnp.exp(exponent * (log_s - log_1s))
        return saturated * jnp.exp(-0.5 * exponent * log_1s) * outer * outer

    def put(tile, m, x):
        t = tile * PAIRS + m
        packed[t] = x
        left = pltpu.roll(x, HALO * m, 1) if m else x
        right = pltpu.roll(x, (HALO * m - (LANES - HALO)) % LANES, 1)
        for ref, y in ((to_pair, jnp.where(even_y, right, left)), (to_next, jnp.where(even_y, left, right))):
            ref[tile] = y if m == 0 else jnp.where(lane >= HALO * m, y, ref[tile])

    for m in range(PAIRS):
        triples = (
            (cond_of(2 * m), cond_of(2 * m + 1)),
            (storage[2 * m], storage[2 * m + 1]),
            (source[2 * m], source[2 * m + 1]),
        )
        for q, (a, b) in enumerate(triples):
            put(2 * q, m, jnp.where(odd, b, a))
            put(2 * q + 1, m, jnp.where(odd, a, b))


def edge_kernel(packed, to_sibling, to_other):
    even = (position()[0] & 1) == 0
    for t in range(6 * PAIRS):
        high, low = packed[t, ROWS - HALO :], packed[t, :HALO]
        to_sibling[t] = jnp.where(even, high, low)
        to_other[t] = jnp.where(even, low, high)


def second_kernel(from_next, from_pair, to_sibling, to_other):
    even = (position()[0] & 1) == 0
    for q, ref in enumerate((from_pair, from_next)):
        for tile in range(6):
            high, low = ref[tile, ROWS - HALO :], ref[tile, :HALO]
            to_sibling[6 * q + tile] = jnp.where(even, high, low)
            to_other[6 * q + tile] = jnp.where(even, low, high)


def coarsen_level(level, fine_rows, out_rows, fine, coarse):
    stor, east, north, inner, outer = fine
    cstor, ceast, cnorth, cinner, couter = coarse
    half = fine_rows // 2
    dims = (half, WIDE)
    bit = lane_bit(dims, level)
    odd = odd_cells(dims, level + 1, 1 if level == 2 else 0)
    step = 1 << level

    def even_rows(ref, *ids):
        return ref[(*ids, pl.ds(0, half, stride=2))]

    def odd_rows(ref, *ids):
        return ref[(*ids, pl.ds(1, half, stride=2))]

    swap = bit ^ odd

    def put(ref, m, a, b):
        ref[0, m, slice(0, half)] = a
        ref[1, m, slice(0, half)] = b

    for m in range(PAIRS):
        u = even_rows(stor, 0, m) + odd_rows(stor, 1, m)
        v = even_rows(stor, 1, m) + odd_rows(stor, 0, m)
        put(cstor, m, pair_sum(jnp.where(swap, v, u), level), pair_sum(jnp.where(swap, u, v), level))
        e0, e1 = odd_rows(east, 0, m), odd_rows(east, 1, m)
        put(ceast, m, pair_sum(jnp.where(swap, e0, e1), level), pair_sum(jnp.where(swap, e1, e0), level))
        low = even_rows(north, 1, m) + odd_rows(north, 0, m)
        high = even_rows(north, 0, m) + odd_rows(north, 1, m)
        a, b = jnp.where(odd, high, low), jnp.where(odd, low, high)
        put(cnorth, m, jnp.where(bit, a, near_next(a, step)), jnp.where(bit, b, near_next(b, step)))
        cinner[m, slice(0, half)] = pair_sum(even_rows(inner, m) + odd_rows(inner, m), level)
        if m < PAIRS - 1:
            couter[m, slice(0, half)] = pair_sum(even_rows(outer, m) + odd_rows(outer, m), level)


def restrict_level(level, fine_rows, residual, coarse_source):
    half = fine_rows // 2
    dims = (half, WIDE)
    bit = lane_bit(dims, level)
    odd = odd_cells(dims, level + 1, 1 if level == 2 else 0)
    swap = bit ^ odd
    for m in range(PAIRS):
        a = residual[m, pl.ds(0, half, stride=2)]
        b = residual[m, pl.ds(1, half, stride=2)]
        coarse_source[0, m, slice(0, half)] = pair_sum(jnp.where(swap, b, a), level)
        coarse_source[1, m, slice(0, half)] = pair_sum(jnp.where(swap, a, b), level)


def invert_diagonal(level, rows, coeffs, inverse):
    stor, east, north, inner, outer = coeffs
    odd = odd_cells((rows, WIDE), level)
    step = 1 << level
    for m in range(PAIRS):
        above = outer[m] if m < PAIRS - 1 else 0.0
        below = outer[m - 1] if m > 0 else 0.0
        for c in range(2):
            diag = stor[c, m] + east[c, m] + row_prev(east[1 - c, m]) + north[c, m]
            diag = diag + lane_prev(north[1 - c, m], step) + inner[m]
            diag = diag + (jnp.where(odd, above, below) if c == 0 else jnp.where(odd, below, above))
            inverse[c, m] = 1.0 / diag


def descend_level(level, rows, coeffs, inverse, source, first, second, residual):
    odd = odd_cells((rows, WIDE), level)
    step = 1 << level
    for m in range(PAIRS):
        first[m] = source[0, m] * inverse[0, m]
    for m in range(PAIRS):
        second[m] = (source[1, m] + beside(1, first, coeffs[1:], m, odd, step)) * inverse[1, m]
    for m in range(PAIRS):
        residual[m] = beside(0, second, coeffs[1:], m, odd, step)


def third_kernel(
    packed, corner_sibling, corner_other, from_next, from_pair, from_sibling, from_other,
    source0, inv0, first0, east0, north0, inner0, outer0,
    source1, inv1, first1, east1, north1, inner1, outer1,
    source2, inv2, first2, east2, north2, inner2, outer2,
    tiles, sums,
    cond, stor, src, east, north, inner, outer, inv, first, second, residual,
    stor1, src1, e1, n1, in1, out1, i1, f1, s1, r1,
    stor2, s2, r2,
    stor3, src3, e3, n3, in3, out3,
):
    source0, inv0, first0, east0, north0, inner0, outer0 = map(Wide, (source0, inv0, first0, east0, north0, inner0, outer0))
    source1, inv1, first1, east1, north1, inner1, outer1 = map(Wide, (source1, inv1, first1, east1, north1, inner1, outer1))
    source2, inv2, first2, east2, north2, inner2, outer2 = map(Wide, (source2, inv2, first2, east2, north2, inner2, outer2))
    cond, stor, src, east, north, inner, outer = map(Wide, (cond, stor, src, east, north, inner, outer))
    inv, first, second, residual = map(Wide, (inv, first, second, residual))
    stor1, src1, e1, n1, in1, out1, i1, f1, s1, r1 = map(Wide, (stor1, src1, e1, n1, in1, out1, i1, f1, s1, r1))
    stor2, s2, r2 = map(Wide, (stor2, s2, r2))
    stor3, src3, e3, n3, in3, out3 = map(Wide, (stor3, src3, e3, n3, in3, out3))
    gx, gy = position()
    even_x, even_y = (gx & 1) == 0, (gy & 1) == 0
    lane = iota((EXT, LANES), 1)

    def rows_of(sib, oth, own):
        return jnp.concatenate([jnp.where(even_x, oth, sib), own, jnp.where(even_x, sib, oth)], axis=0)

    for tile in range(6):
        pair, other = [
            rows_of(corner_sibling[q + tile], corner_other[q + tile], ref[tile]) for q, ref in ((0, from_pair), (6, from_next))
        ]
        right = jnp.where(even_y, pair, other)
        left = jnp.where(even_y, other, pair)
        ref = (cond, stor, src)[tile // 2]
        for m in range(PAIRS):
            t = tile * PAIRS + m
            x = rows_of(from_sibling[t], from_other[t], packed[t])
            r = pltpu.roll(right, (-HALO * m) % LANES, 1) if m else right
            l = pltpu.roll(left, (LANES - HALO - HALO * m) % LANES, 1)
            h = jnp.where(lane < HALO, r, jnp.where(lane >= LANES - HALO, l, 0.0))
            if tile // 2 == 1:
                x, h = jnp.where(x == 0.0, 1.0, x), jnp.where(h == 0.0, 1.0, h)
            ref.ref[tile % 2, m, 0] = x
            ref.ref[tile % 2, m, 1] = h

    dims = (EXT, WIDE)
    odd = odd_cells(dims, 0)
    row, column = iota(dims, 0), iota(dims, 1)
    last_row = (row == HALO + ROWS - 1) & (gx == lax.axis_size("gx") - 1)
    before_row = (row == HALO - 1) & (gx == 0)
    keep_x = jnp.where(last_row | before_row, 0.0, 0.5)
    last_column = (column == LANES - 1) & (gy == lax.axis_size("gy") - 1)
    before_column = (column == WIDE - 1) & (gy == 0)
    keep_y = jnp.where(last_column | before_column, 0.0, 0.5)
    for m in range(PAIRS):
        a, b = cond[0, m], cond[1, m]
        east[0, m] = (a + row_next(b)) * keep_x
        east[1, m] = (b + row_next(a)) * keep_x
        north[0, m] = (a + lane_next(b, 1)) * keep_y
        north[1, m] = (b + lane_next(a, 1)) * keep_y
        inner[m] = a + b
        if m < PAIRS - 1:
            outer[m] = jnp.where(odd, a + cond[1, m + 1], b + cond[0, m + 1])

    level0 = (stor, east, north, inner, outer)
    level1 = (stor1, e1, n1, in1, out1)
    level2 = (stor2, east2, north2, inner2, outer2)
    level3 = (stor3, e3, n3, in3, out3)
    invert_diagonal(0, EXT, level0, inv)
    descend_level(0, EXT, level0, inv, src, first, second, residual)

    coarsen_level(0, EXT, ROWS1, level0, level1)
    restrict_level(0, EXT, residual, src1)
    invert_diagonal(1, ROWS1, level1, i1)
    descend_level(1, ROWS1, level1, i1, src1, f1, s1, r1)

    half = ROWS1 // 2
    for ref in (source2, east2, north2, inner2, outer2):
        ref.ref[..., half:, :] = jnp.zeros((*ref.ref.shape[:-2], ROWS2 - half, LANES), jnp.float32)
    stor2.ref[..., half:, :] = jnp.ones((2, PAIRS, 2, ROWS2 - half, LANES), jnp.float32)
    coarsen_level(1, ROWS1, ROWS2, level1, level2)
    restrict_level(1, ROWS1, r1, source2)
    invert_diagonal(2, ROWS2, level2, inv2)
    descend_level(2, ROWS2, level2, inv2, source2, first2, s2, r2)

    coarsen_level(2, ROWS2, 16, level2, level3)
    restrict_level(2, ROWS2, r2, src3)

    dims3 = (16, WIDE)
    odd3 = odd_cells(dims3, 3, 1)
    phase = iota((4, LANES), 1) & 7
    total_f, total_s = 0.0, 0.0
    compact = [None] * TILES
    for m in range(PAIRS):
        above = out3[m] if m < PAIRS - 1 else 0.0
        below = out3[m - 1] if m > 0 else 0.0
        invs = []
        for c in range(2):
            diag = stor3[c, m] + e3[c, m] + row_prev(e3[1 - c, m]) + n3[c, m]
            diag = diag + lane_prev(n3[1 - c, m], 8) + in3[m]
            diag = diag + (jnp.where(odd3, above, below) if c == 0 else jnp.where(odd3, below, above))
            invs.append(1.0 / diag)
            total_f = total_f + src3[c, m][3:7, :LANES]
            total_s = total_s + stor3[c, m][3:7, :LANES]
        values = (
            src3[0, m] * invs[0], src3[1, m] * invs[1], 1.0 - stor3[0, m] * invs[0], invs[0], invs[1],
            e3[0, m], e3[1, m], n3[0, m], n3[1, m], in3[m], out3[m] if m < PAIRS - 1 else jnp.zeros(dims3, jnp.float32),
        )
        for q, value in enumerate(values):
            own = value[3:7, :LANES]
            compact[q] = jnp.where(phase == m, own, 0.0 if m == 0 else compact[q])
    for q in range(TILES):
        tiles[4 * q : 4 * q + 4] = compact[q]
    sums[0:1] = jnp.broadcast_to(jnp.sum(total_f, keepdims=True), (1, LANES)) * 0.125
    sums[1:2] = jnp.broadcast_to(jnp.sum(total_s, keepdims=True), (1, LANES)) * 0.125

    for m in range(PAIRS):
        for c in range(2):
            for to, of in ((source0, src), (inv0, inv), (east0, east), (north0, north)):
                to[c, m] = of[c, m, slice(16, 64)]
            for to, of in ((source1, src1), (inv1, i1), (east1, e1), (north1, n1)):
                to[c, m] = of[c, m, slice(8, 32)]
        first0[m], first1[m] = first[m, slice(16, 64)], f1[m, slice(8, 32)]
        inner0[m], inner1[m] = inner[m, slice(16, 64)], in1[m, slice(8, 32)]
        if m < PAIRS - 1:
            outer0[m], outer1[m] = outer[m, slice(16, 64)], out1[m, slice(8, 32)]


def window_kernel(tiles, from_pair, from_next, window):
    even = (position()[1] & 1) == 0
    window[:, :LANES] = tiles[...]
    a, b = from_pair[...], from_next[...]
    right_first = (iota(a.shape, 1) < LANES // 2) == even
    window[:, LANES:] = jnp.where(right_first, a, b)


def spread_rows(level, low, high, into, m):
    rows = low.shape[0]
    bit = lane_bit(low.shape, level)
    into[m, pl.ds(0, rows, stride=2)] = jnp.where(bit, high, low)
    into[m, pl.ds(1, rows, stride=2)] = jnp.where(bit, low, high)


def join_kernel(mine, sibling, both):
    both[: 4 * TILES] = mine[...]
    both[4 * TILES :] = sibling[...]


def fourth_kernel(
    mine, sibling, received, passed_on, sums_in,
    source0, inv0, first0, east0, north0, inner0, outer0,
    source1, inv1, first1, east1, north1, inner1, outer1,
    source2, inv2, first2, east2, north2, inner2, outer2,
    fields, sums,
    whole, work2, work1, work0a, work0b, va, vb, wa, wb,
    ua2, ub2, ua1, ub1,
):
    source0, inv0, first0, east0, north0, inner0, outer0 = map(Wide, (source0, inv0, first0, east0, north0, inner0, outer0))
    source1, inv1, first1, east1, north1, inner1, outer1 = map(Wide, (source1, inv1, first1, east1, north1, inner1, outer1))
    source2, inv2, first2, east2, north2, inner2, outer2 = map(Wide, (source2, inv2, first2, east2, north2, inner2, outer2))
    work2, work1, work0a, work0b, va, vb, wa, wb = map(Wide, (work2, work1, work0a, work0b, va, vb, wa, wb))
    ua2, ub2, ua1, ub1 = map(Wide, (ua2, ub2, ua1, ub1))
    f32 = jnp.float32
    even = (position()[0] & 1) == 0
    size = 4 * TILES
    own, sib = mine[...], sibling[...]
    direct, relayed = received[...], passed_on[...]
    before, after = jnp.where(even, direct, relayed), jnp.where(even, relayed, direct)
    blocks = (
        before[size:], before[:size], jnp.where(even, own, sib), jnp.where(even, sib, own), after[:size], after[size:],
    )
    for slot, block in enumerate(blocks):
        for q in range(TILES):
            whole[q, 4 * slot : 4 * slot + 4] = block[4 * q : 4 * q + 4]
    own_f, own_s = sums_in[0:1, 0:1], sums_in[1:2, 0:1]
    guess = own_f / own_s
    g0, g1, h0, i30, i31, e30, e31, n30, n31, in3, out3 = [whole[q] for q in range(TILES)]
    inv3, e3, n3 = (i30, i31), (e30, e31), (n30, n31)
    odd3 = odd_cells((24, WIDE), 3)

    def beside3(c, u):
        t = e3[c] * row_next(u) + row_prev(e3[1 - c] * u)
        t = t + (n3[c] * lane_next(u, 8) + lane_prev(n3[1 - c] * u, 8)) + in3 * u
        above, below = out3 * lane_next(u, 1), lane_prev(out3 * u, 1)
        return t + (jnp.where(odd3, above, below) if c == 0 else jnp.where(odd3, below, above))

    a0, b0 = g0 + guess * h0, h0
    for _ in range(3):
        a1, b1 = g1 + beside3(1, a0) * inv3[1], beside3(1, b0) * inv3[1]
        a0, b0 = g0 + beside3(0, a1) * inv3[0], beside3(0, b1) * inv3[0]

    a0, a1, b0, b1 = [jnp.where(even, pltpu.roll(x, 19, 0), pltpu.roll(x, 15, 0))[:16] for x in (a0, a1, b0, b1)]
    dims3 = (16, WIDE)
    phase = iota(dims3, 1) & 7
    odd3 = odd_cells(dims3, 3, 1)
    second_half = lane_bit(dims3, 1)

    def spread(x, m):
        x = jnp.where(phase == 0, near_next(x, m) if m else x, 0.0)
        x = x + near_prev(x, 1)
        x = x + near_prev(x, 2)
        return x + near_prev(x, 4)

    for m in range(PAIRS):
        x0 = jnp.where(second_half, spread(b0, m), spread(a0, m))
        x1 = jnp.where(second_half, spread(b1, m), spread(a1, m))
        low, high = jnp.where(odd3, x1, x0)[:12], jnp.where(odd3, x0, x1)[:12]
        spread_rows(2, low, high, work2, m)

    def smooth(level, rows, coeffs, inverse, source, first, work, ones, zeros, half_bit):
        odd = odd_cells((rows, WIDE), level)
        is_b = lane_bit((rows, WIDE), half_bit)
        step = 1 << level
        for m in range(PAIRS):
            work[m] = work[m] + jnp.where(is_b, 0.0, first[m])
        for m in range(PAIRS):
            ones[m] = (jnp.where(is_b, 0.0, source[1, m]) + beside(1, work, coeffs, m, odd, step)) * inverse[1, m]
        for m in range(PAIRS):
            zeros[m] = jnp.where(is_b, 0.0, first[m]) + beside(0, ones, coeffs, m, odd, step) * inverse[0, m]

    smooth(2, ROWS2, (east2, north2, inner2, outer2), inv2, source2, first2, work2, ub2, ua2, 1)
    dims2 = (ROWS2, WIDE)
    odd2 = odd_cells(dims2, 2)
    bit1, bit0 = lane_bit(dims2, 1), lane_bit(dims2, 0)

    def regroup2(x):
        a = jnp.where(bit1, near_prev(x, 2), x)
        b = jnp.where(bit1, x, near_next(x, 2))
        return jnp.where(bit0, b, a)

    for m in range(PAIRS):
        x0, x1 = regroup2(ua2[m]), regroup2(ub2[m])
        low, high = jnp.where(odd2, x1, x0)[4:16], jnp.where(odd2, x0, x1)[4:16]
        spread_rows(1, low, high, work1, m)

    smooth(1, 24, (east1, north1, inner1, outer1), inv1, source1, first1, work1, ub1, ua1, 0)
    dims1 = (24, WIDE)
    odd1 = odd_cells(dims1, 1)
    bit0 = lane_bit(dims1, 0)
    for m in range(PAIRS):
        x0, x1 = ua1[m], ub1[m]
        low, high = jnp.where(odd1, x1, x0), jnp.where(odd1, x0, x1)
        for work, pick in (
            (work0a, lambda x: jnp.where(bit0, near_prev(x, 1), x)),
            (work0b, lambda x: jnp.where(bit0, x, near_next(x, 1))),
        ):
            spread_rows(0, pick(low), pick(high), work, m)

    rows = 48
    odd = odd_cells((rows, WIDE), 0)
    coeffs = (east0, north0, inner0, outer0)
    for m in range(PAIRS):
        work0a[m] = work0a[m] + first0[m]
    for m in range(PAIRS):
        va[m] = (source0[1, m] + beside(1, work0a, coeffs, m, odd, 1)) * inv0[1, m]
        vb[m] = beside(1, work0b, coeffs, m, odd, 1) * inv0[1, m]
    for m in range(PAIRS):
        wa[m] = first0[m] + beside(0, va, coeffs, m, odd, 1) * inv0[0, m]
        wb[m] = beside(0, vb, coeffs, m, odd, 1) * inv0[0, m]
    for m in range(PAIRS):
        work0a[m] = work0a[m] - wa[m]
        work0b[m] = work0b[m] - wb[m]
    acc = [jnp.zeros((ROWS, LANES), f32)] * 11

    def own(x):
        return x[8 : 8 + ROWS, :LANES]

    for m in range(PAIRS):
        change_a = own(beside(1, work0a, coeffs, m, odd, 1))
        img_b = own(beside(1, work0b, coeffs, m, odd, 1))
        r0, r1 = own(source0[0, m]), own(source0[1, m])
        p0, p1, q0, q1 = own(wa[m]), own(va[m]), own(wb[m]), own(vb[m])
        img_a = r1 + change_a
        d = -change_a
        terms = (
            r0 * p0 + r1 * p1, r0 * q0 + r1 * q1,
            r0 * p0 + img_a * p1, r0 * q0 + img_a * q1 + img_b * p1, img_b * q1,
            d * d, d * img_a, img_a * img_a + r0 * r0, d * img_b, img_a * img_b, img_b * img_b,
        )
        acc = [x + y for x, y in zip(acc, terms, strict=True)]
        for t, x in enumerate((p0, p1, q0, q1, r0, r1, img_a, img_b)):
            fields[t, m] = x
    lane = iota((1, LANES), 1)
    line = jnp.zeros((1, LANES), f32)
    for q, x in enumerate(acc):
        line = jnp.where(lane == q, jnp.sum(x, keepdims=True), line)
    line = jnp.where(lane == 11, own_f, line)
    line = jnp.where(lane == 12, own_s, line)
    line = jnp.where(lane == 13, guess, line)
    sums[...] = jnp.broadcast_to(line, sums.shape)


def last_kernel(sums, line, fields, solution_out, residual_out, norm_ref, solution_ref, residual_ref, sems, *, cells):
    x = jnp.concatenate([sums[:, :16], sums[:, 16:]], axis=0)

    def column(q):
        return x[:, q : q + 1]

    def total(v):
        return jnp.sum(v, axis=0, keepdims=True)

    rp, rq, pa, pb, qb, dd, da, aa, db, ab, bb = [column(q) for q in range(11)]
    mean = total(column(11)) / total(column(12))
    shift = mean - column(13)
    step = total(rp + shift * rq) / total(pa + shift * (pb + shift * qb))
    s, t = step - 1.0, step * shift
    squares = total(dd - 2.0 * s * da + s * s * aa - 2.0 * t * db + 2.0 * s * t * ab + t * t * bb)
    norm_ref[...] = jnp.sqrt(jnp.maximum(squares, 0.0) / cells)
    here = mean - line[0:1, 13:14]
    odd = odd_cells((ROWS, LANES), 0)
    copies = []
    for m in range(PAIRS):
        p0, p1, q0, q1, r0, r1, img_a, img_b = [fields[t, m] for t in range(8)]
        s0, s1 = step * (p0 + here * q0), step * (p1 + here * q1)
        n0, n1 = r0 - step * r0, r1 - step * (img_a + here * img_b)
        solution_ref[2 * m] = jnp.where(odd, s1, s0)
        solution_ref[2 * m + 1] = jnp.where(odd, s0, s1)
        residual_ref[2 * m] = jnp.where(odd, n1, n0)
        residual_ref[2 * m + 1] = jnp.where(odd, n0, n1)
        layers = pl.ds(2 * m, 2)
        for q, (ref, out) in enumerate(((solution_ref, solution_out), (residual_ref, residual_out))):
            copies.append(pltpu.make_async_copy(ref.at[layers], out.at[layers], sems.at[q, m]))
            copies[-1].start()
    for copy in copies:
        copy.wait()


def level_dims(rows):
    two, one, four = [(*lead, 2, rows, LANES) for lead in ((2, PAIRS), (PAIRS,), (PAIRS - 1,))]
    return two, one, four


def level_shapes(rows):
    two, one, four = [shape(*dims) for dims in level_dims(rows)]
    return two, two, one, two, two, one, four


def scratch(*dims):
    return pltpu.VMEM(dims, jnp.float32)


def pairs_of(count, first):
    return [(i, i + 1) for i in range(first, count - 1, 2)] + [(i + 1, i) for i in range(first, count - 1, 2)]


def pair_exchange(x, axis):
    count = lax.axis_size(axis)
    return [lax.ppermute(x_i, axis, pairs_of(count, first)) for first, x_i in enumerate(x)]


def shards(pressure, soil, vg_alpha, vg_n, sat_cond, storage, right_side):
    count_x, count_y = lax.axis_size("gx"), lax.axis_size("gy")
    block, slab = scratch(2 * PAIRS, ROWS, LANES), shape(6 * PAIRS, HALO, LANES)
    side, corner = shape(6, ROWS, LANES), shape(12, HALO, LANES)
    arguments = (pressure, soil, storage, right_side, *[v.reshape(1, NSOIL) for v in (vg_alpha, vg_n, sat_cond)])
    packed, *sides = pl.pallas_call(
        first_kernel, out_shape=(shape(6 * PAIRS, ROWS, LANES), side, side),
        in_specs=[HBM] * 7, out_specs=(VM,) * 3,
        scratch_shapes=[
            block, pltpu.VMEM((2 * PAIRS, ROWS, LANES), jnp.int32), block, block, scratch(3, 1, NSOIL), pltpu.SemaphoreType.DMA((7,)),
        ],
        compiler_params=params(4), name="conductivity",
    )(*[pltpu.with_memory_space_constraint(v, pltpu.MemorySpace.HBM) for v in arguments])
    beside_y = pair_exchange(sides, "gy")
    slabs = pl.pallas_call(
        edge_kernel, out_shape=(slab, slab), in_specs=[VM], out_specs=(VM, VM), compiler_params=params(2), name="edges",
    )(packed)
    halos = pair_exchange(slabs, "gx") + beside_y
    corners = pl.pallas_call(
        second_kernel, out_shape=(corner, corner), in_specs=[VM, VM], out_specs=(VM, VM), compiler_params=params(2), name="corners",
    )(*beside_y[::-1])
    halos = pair_exchange(corners, "gx") + beside_y[::-1] + halos[:2]

    def sized(rows):
        return [scratch(*dims) for dims in level_dims(rows)]

    two, one, four = sized(EXT)
    two1, one1, four1 = sized(ROWS1)
    two2, one2, _ = sized(ROWS2)
    two3, one3, four3 = sized(16)
    out = pl.pallas_call(
        third_kernel,
        out_shape=(*level_shapes(48), *level_shapes(24), *level_shapes(ROWS2), shape(4 * TILES, LANES), shape(8, LANES)),
        in_specs=[VM] * 7, out_specs=(VM,) * 23,
        scratch_shapes=[
            two, two, two, two, two, one, four, two, one, one, one,
            two1, two1, two1, two1, one1, four1, two1, one1, one1, one1,
            two2, one2, one2,
            two3, two3, two3, two3, one3, four3,
        ],
        compiler_params=params(12), name="descent",
    )(packed, *halos)
    levels, tiles, sums = out[:21], out[21], out[22]

    tile_pair, tile_next = pair_exchange((tiles, tiles), "gy")
    window = pl.pallas_call(
        window_kernel, out_shape=shape(4 * TILES, WIDE), in_specs=[VM] * 3, out_specs=VM, compiler_params=params(2), name="window",
    )(tiles, tile_pair, tile_next)
    sibling = lax.ppermute(window, "gx", pairs_of(count_x, 0))
    both = pl.pallas_call(
        join_kernel, out_shape=shape(8 * TILES, WIDE), in_specs=[VM] * 2, out_specs=VM, compiler_params=params(2), name="join",
    )(window, sibling)
    received = lax.ppermute(both, "gx", pairs_of(count_x, 1))
    passed_on = lax.ppermute(received, "gx", pairs_of(count_x, 0))
    blocks = (window, sibling, received, passed_on)

    devices = count_x * count_y
    fields, line = pl.pallas_call(
        fourth_kernel,
        out_shape=(shape(8, PAIRS, ROWS, LANES), shape(8, LANES)),
        in_specs=[VM] * 26, out_specs=(VM, VM),
        scratch_shapes=[
            scratch(TILES, 24, WIDE), sized(ROWS2)[1], sized(24)[1],
            *[sized(48)[1]] * 6, *[sized(24)[1]] * 4,
        ],
        compiler_params=params(8), name="ascent",
    )(*blocks, sums, *levels)
    both = jnp.concatenate([line[:1, :16], lax.ppermute(line, "gx", pairs_of(count_x, 0))[:1, :16]], axis=1)
    kinds = [[x * count_y + y for y in range(count_y) for x in range(c, count_x, 2)][::-1] for c in range(2)]
    both = jnp.broadcast_to(both, (devices // 2, 32))
    every = lax.all_to_all(both, ("gx", "gy"), 0, 0, axis_index_groups=kinds, tiled=True)

    layers = 2 * PAIRS
    out = shape(layers, ROWS, LANES)
    solution_out, residual_out, norm = pl.pallas_call(
        functools.partial(last_kernel, cells=float(layers * ROWS * LANES * devices)),
        out_shape=(out, out, shape(1, 1)), in_specs=[VM, VM, VM], out_specs=(HBM, HBM, VM),
        scratch_shapes=[scratch(*out.shape), scratch(*out.shape), pltpu.SemaphoreType.DMA((2, PAIRS))],
        compiler_params=params(4), name="outputs",
    )(every, line, fields)
    return solution_out, residual_out, norm.reshape(1)


def solution(mesh):
    split, whole = P(None, "gx", "gy"), P()
    return jax.shard_map(
        shards, mesh=mesh, in_specs=(split, split, whole, whole, whole, split, split),
        out_specs=(split, split, whole), check_vma=False,
    )
```

```python
import functools

import jax
import jax.numpy as jnp
from jax import lax
from jax.experimental import pallas as pl
from jax.experimental.pallas import tpu as pltpu
from jax.sharding import PartitionSpec as P

NSOIL = 23
PAIRS = 5
HALO = 24
ROWS, LANES = 32, 128
EXT = ROWS + 2 * HALO
WIDE = 2 * LANES
ROWS1, ROWS2 = EXT // 2, 24
TILES = 11
MIB = 1 << 20


def iota(shape, dim):
    return lax.broadcasted_iota(jnp.int32, shape, dim)


def odd_cells(shape, level, start=0):
    return ((iota(shape, 0) + start + (iota(shape, 1) >> level)) & 1) == 1


def lane_bit(shape, level):
    return ((iota(shape, 1) >> level) & 1) == 1


def row_next(x):
    return pltpu.roll(x, x.shape[0] - 1, 0)


def row_prev(x):
    return pltpu.roll(x, 1, 0)


def lane_next(x, step):
    return pltpu.roll(x, x.shape[1] - step, 1)


def lane_prev(x, step):
    return pltpu.roll(x, step, 1)


def by_halves(f, x):
    return jnp.concatenate([f(x[:, start : start + LANES]) for start in range(0, x.shape[1], LANES)], axis=1)


def near_next(x, step):
    return by_halves(lambda h: lane_next(h, step), x)


def near_prev(x, step):
    return by_halves(lambda h: lane_prev(h, step), x)


def pair_sum(x, level):
    step = 1 << level
    return x + jnp.where(lane_bit(x.shape, level), near_prev(x, step), near_next(x, step))


def beside(c, u, coeffs, m, odd, step):
    east, north, inner, outer = coeffs
    um = u[m]
    t = east[c, m] * row_next(um) + row_prev(east[1 - c, m] * um)
    t = t + (north[c, m] * lane_next(um, step) + lane_prev(north[1 - c, m] * um, step))
    t = t + inner[m] * um
    above = outer[m] * u[m + 1] if m < PAIRS - 1 else 0.0
    below = outer[m - 1] * u[m - 1] if m > 0 else 0.0
    return t + (jnp.where(odd, above, below) if c == 0 else jnp.where(odd, below, above))


def position():
    return lax.axis_index("gx"), lax.axis_index("gy")


def params(limit):
    return pltpu.CompilerParams(vmem_limit_bytes=limit * MIB)


VM = pl.BlockSpec(memory_space=pltpu.VMEM)
HBM = pl.BlockSpec(memory_space=pltpu.MemorySpace.HBM)


def shape(*dims):
    return jax.ShapeDtypeStruct(dims, jnp.float32)


class Wide:
    def __init__(self, ref):
        self.ref, self.lead = ref, len(ref.shape) - 3

    def parts(self, ids):
        ids = ids if isinstance(ids, tuple) else (ids,)
        rows = ids[self.lead] if len(ids) > self.lead else slice(None)
        return [self.ref.at[(*ids[: self.lead], half)] for half in range(2)], rows

    def __getitem__(self, ids):
        refs, rows = self.parts(ids)
        return jnp.concatenate([ref[rows, :] for ref in refs], axis=1)

    def __setitem__(self, ids, x):
        refs, rows = self.parts(ids)
        for half, ref in enumerate(refs):
            ref[rows, :] = x[:, LANES * half : LANES * (half + 1)]


def first_kernel(
    pressure_in, soil_in, storage_in, source_in, alpha_in, power_in, saturated_in, packed, to_pair, to_next,
    pressure, soil, storage, source, table, sems,
):
    copies = [
        pltpu.make_async_copy(alpha_in, table.at[0], sems.at[4]),
        pltpu.make_async_copy(power_in, table.at[1], sems.at[5]),
        pltpu.make_async_copy(saturated_in, table.at[2], sems.at[6]),
        pltpu.make_async_copy(pressure_in, pressure, sems.at[0]),
        pltpu.make_async_copy(soil_in, soil, sems.at[1]),
        pltpu.make_async_copy(storage_in, storage, sems.at[2]),
        pltpu.make_async_copy(source_in, source, sems.at[3]),
    ]
    for copy in copies:
        copy.start()
    even_y = (position()[1] & 1) == 0
    odd = odd_cells((ROWS, LANES), 0)
    lane = iota((ROWS, LANES), 1)
    for copy in copies:
        copy.wait()
    rows = []
    for q in range(3):
        row = jnp.concatenate([table[q], jnp.ones((1, LANES - NSOIL), jnp.float32)], axis=1)
        rows.append(jnp.broadcast_to(jnp.log(row) if q == 0 else row, (8, LANES)))

    def look_up(row, ids):
        parts = [jnp.take_along_axis(row, ids[8 * b : 8 * b + 8], axis=1) for b in range(ROWS // 8)]
        return jnp.concatenate(parts, axis=0)

    def cond_of(k):
        ids = soil[k]
        log_scale, power, saturated = [look_up(r, ids) for r in rows]
        exponent = 1.0 - 1.0 / power
        log_s = power * (log_scale + jnp.log(jnp.abs(pressure[k])))
        log_1s = jnp.log(1.0 + jnp.exp(log_s))
        outer = 1.0 - jnp.exp(exponent * (log_s - log_1s))
        return saturated * jnp.exp(-0.5 * exponent * log_1s) * outer * outer

    def put(tile, m, x):
        t = tile * PAIRS + m
        packed[t] = x
        left = pltpu.roll(x, HALO * m, 1) if m else x
        right = pltpu.roll(x, (HALO * m - (LANES - HALO)) % LANES, 1)
        for ref, y in ((to_pair, jnp.where(even_y, right, left)), (to_next, jnp.where(even_y, left, right))):
            ref[tile] = y if m == 0 else jnp.where(lane >= HALO * m, y, ref[tile])

    for m in range(PAIRS):
        triples = (
            (cond_of(2 * m), cond_of(2 * m + 1)),
            (storage[2 * m], storage[2 * m + 1]),
            (source[2 * m], source[2 * m + 1]),
        )
        for q, (a, b) in enumerate(triples):
            put(2 * q, m, jnp.where(odd, b, a))
            put(2 * q + 1, m, jnp.where(odd, a, b))


def edge_kernel(packed, to_sibling, to_other):
    even = (position()[0] & 1) == 0
    for t in range(6 * PAIRS):
        high, low = packed[t, ROWS - HALO :], packed[t, :HALO]
        to_sibling[t] = jnp.where(even, high, low)
        to_other[t] = jnp.where(even, low, high)


def second_kernel(from_next, from_pair, to_sibling, to_other):
    even = (position()[0] & 1) == 0
    for q, ref in enumerate((from_pair, from_next)):
        for tile in range(6):
            high, low = ref[tile, ROWS - HALO :], ref[tile, :HALO]
            to_sibling[6 * q + tile] = jnp.where(even, high, low)
            to_other[6 * q + tile] = jnp.where(even, low, high)


def coarsen_level(level, fine_rows, out_rows, fine, coarse):
    stor, east, north, inner, outer = fine
    cstor, ceast, cnorth, cinner, couter = coarse
    half = fine_rows // 2
    dims = (half, WIDE)
    bit = lane_bit(dims, level)
    odd = odd_cells(dims, level + 1, 1 if level == 2 else 0)
    step = 1 << level

    def even_rows(ref, *ids):
        return ref[(*ids, pl.ds(0, half, stride=2))]

    def odd_rows(ref, *ids):
        return ref[(*ids, pl.ds(1, half, stride=2))]

    swap = bit ^ odd

    def put(ref, m, a, b):
        ref[0, m, slice(0, half)] = a
        ref[1, m, slice(0, half)] = b

    for m in range(PAIRS):
        u = even_rows(stor, 0, m) + odd_rows(stor, 1, m)
        v = even_rows(stor, 1, m) + odd_rows(stor, 0, m)
        put(cstor, m, pair_sum(jnp.where(swap, v, u), level), pair_sum(jnp.where(swap, u, v), level))
        e0, e1 = odd_rows(east, 0, m), odd_rows(east, 1, m)
        put(ceast, m, pair_sum(jnp.where(swap, e0, e1), level), pair_sum(jnp.where(swap, e1, e0), level))
        low = even_rows(north, 1, m) + odd_rows(north, 0, m)
        high = even_rows(north, 0, m) + odd_rows(north, 1, m)
        a, b = jnp.where(odd, high, low), jnp.where(odd, low, high)
        put(cnorth, m, jnp.where(bit, a, near_next(a, step)), jnp.where(bit, b, near_next(b, step)))
        cinner[m, slice(0, half)] = pair_sum(even_rows(inner, m) + odd_rows(inner, m), level)
        if m < PAIRS - 1:
            couter[m, slice(0, half)] = pair_sum(even_rows(outer, m) + odd_rows(outer, m), level)


def restrict_level(level, fine_rows, residual, coarse_source):
    half = fine_rows // 2
    dims = (half, WIDE)
    bit = lane_bit(dims, level)
    odd = odd_cells(dims, level + 1, 1 if level == 2 else 0)
    swap = bit ^ odd
    for m in range(PAIRS):
        a = residual[m, pl.ds(0, half, stride=2)]
        b = residual[m, pl.ds(1, half, stride=2)]
        coarse_source[0, m, slice(0, half)] = pair_sum(jnp.where(swap, b, a), level)
        coarse_source[1, m, slice(0, half)] = pair_sum(jnp.where(swap, a, b), level)


def invert_diagonal(level, rows, coeffs, inverse):
    stor, east, north, inner, outer = coeffs
    odd = odd_cells((rows, WIDE), level)
    step = 1 << level
    for m in range(PAIRS):
        above = outer[m] if m < PAIRS - 1 else 0.0
        below = outer[m - 1] if m > 0 else 0.0
        for c in range(2):
            diag = stor[c, m] + east[c, m] + row_prev(east[1 - c, m]) + north[c, m]
            diag = diag + lane_prev(north[1 - c, m], step) + inner[m]
            diag = diag + (jnp.where(odd, above, below) if c == 0 else jnp.where(odd, below, above))
            inverse[c, m] = 1.0 / diag


def descend_level(level, rows, coeffs, inverse, source, first, second, residual):
    odd = odd_cells((rows, WIDE), level)
    step = 1 << level
    for m in range(PAIRS):
        first[m] = source[0, m] * inverse[0, m]
    for m in range(PAIRS):
        second[m] = (source[1, m] + beside(1, first, coeffs[1:], m, odd, step)) * inverse[1, m]
    for m in range(PAIRS):
        residual[m] = beside(0, second, coeffs[1:], m, odd, step)


def third_kernel(
    packed, corner_sibling, corner_other, from_next, from_pair, from_sibling, from_other,
    source0, inv0, first0, east0, north0, inner0, outer0,
    source1, inv1, first1, east1, north1, inner1, outer1,
    source2, inv2, first2, east2, north2, inner2, outer2,
    tiles, sums,
    cond, stor, src, east, north, inner, outer, inv, first, second, residual,
    stor1, src1, e1, n1, in1, out1, i1, f1, s1, r1,
    stor2, s2, r2,
    stor3, src3, e3, n3, in3, out3,
):
    source0, inv0, first0, east0, north0, inner0, outer0 = map(Wide, (source0, inv0, first0, east0, north0, inner0, outer0))
    source1, inv1, first1, east1, north1, inner1, outer1 = map(Wide, (source1, inv1, first1, east1, north1, inner1, outer1))
    source2, inv2, first2, east2, north2, inner2, outer2 = map(Wide, (source2, inv2, first2, east2, north2, inner2, outer2))
    cond, stor, src, east, north, inner, outer = map(Wide, (cond, stor, src, east, north, inner, outer))
    inv, first, second, residual = map(Wide, (inv, first, second, residual))
    stor1, src1, e1, n1, in1, out1, i1, f1, s1, r1 = map(Wide, (stor1, src1, e1, n1, in1, out1, i1, f1, s1, r1))
    stor2, s2, r2 = map(Wide, (stor2, s2, r2))
    stor3, src3, e3, n3, in3, out3 = map(Wide, (stor3, src3, e3, n3, in3, out3))
    gx, gy = position()
    even_x, even_y = (gx & 1) == 0, (gy & 1) == 0
    lane = iota((EXT, LANES), 1)

    def rows_of(sib, oth, own):
        return jnp.concatenate([jnp.where(even_x, oth, sib), own, jnp.where(even_x, sib, oth)], axis=0)

    for tile in range(6):
        pair, other = [
            rows_of(corner_sibling[q + tile], corner_other[q + tile], ref[tile]) for q, ref in ((0, from_pair), (6, from_next))
        ]
        right = jnp.where(even_y, pair, other)
        left = jnp.where(even_y, other, pair)
        ref = (cond, stor, src)[tile // 2]
        for m in range(PAIRS):
            t = tile * PAIRS + m
            x = rows_of(from_sibling[t], from_other[t], packed[t])
            r = pltpu.roll(right, (-HALO * m) % LANES, 1) if m else right
            l = pltpu.roll(left, (LANES - HALO - HALO * m) % LANES, 1)
            h = jnp.where(lane < HALO, r, jnp.where(lane >= LANES - HALO, l, 0.0))
            if tile // 2 == 1:
                x, h = jnp.where(x == 0.0, 1.0, x), jnp.where(h == 0.0, 1.0, h)
            ref.ref[tile % 2, m, 0] = x
            ref.ref[tile % 2, m, 1] = h

    dims = (EXT, WIDE)
    odd = odd_cells(dims, 0)
    row, column = iota(dims, 0), iota(dims, 1)
    last_row = (row == HALO + ROWS - 1) & (gx == lax.axis_size("gx") - 1)
    before_row = (row == HALO - 1) & (gx == 0)
    keep_x = jnp.where(last_row | before_row, 0.0, 0.5)
    last_column = (column == LANES - 1) & (gy == lax.axis_size("gy") - 1)
    before_column = (column == WIDE - 1) & (gy == 0)
    keep_y = jnp.where(last_column | before_column, 0.0, 0.5)
    for m in range(PAIRS):
        a, b = cond[0, m], cond[1, m]
        east[0, m] = (a + row_next(b)) * keep_x
        east[1, m] = (b + row_next(a)) * keep_x
        north[0, m] = (a + lane_next(b, 1)) * keep_y
        north[1, m] = (b + lane_next(a, 1)) * keep_y
        inner[m] = a + b
        if m < PAIRS - 1:
            outer[m] = jnp.where(odd, a + cond[1, m + 1], b + cond[0, m + 1])

    level0 = (stor, east, north, inner, outer)
    level1 = (stor1, e1, n1, in1, out1)
    level2 = (stor2, east2, north2, inner2, outer2)
    level3 = (stor3, e3, n3, in3, out3)
    invert_diagonal(0, EXT, level0, inv)
    descend_level(0, EXT, level0, inv, src, first, second, residual)

    coarsen_level(0, EXT, ROWS1, level0, level1)
    restrict_level(0, EXT, residual, src1)
    invert_diagonal(1, ROWS1, level1, i1)
    descend_level(1, ROWS1, level1, i1, src1, f1, s1, r1)

    half = ROWS1 // 2
    for ref in (source2, east2, north2, inner2, outer2):
        ref.ref[..., half:, :] = jnp.zeros((*ref.ref.shape[:-2], ROWS2 - half, LANES), jnp.float32)
    stor2.ref[..., half:, :] = jnp.ones((2, PAIRS, 2, ROWS2 - half, LANES), jnp.float32)
    coarsen_level(1, ROWS1, ROWS2, level1, level2)
    restrict_level(1, ROWS1, r1, source2)
    invert_diagonal(2, ROWS2, level2, inv2)
    descend_level(2, ROWS2, level2, inv2, source2, first2, s2, r2)

    coarsen_level(2, ROWS2, 16, level2, level3)
    restrict_level(2, ROWS2, r2, src3)

    dims3 = (16, WIDE)
    odd3 = odd_cells(dims3, 3, 1)
    phase = iota((4, LANES), 1) & 7
    total_f, total_s = 0.0, 0.0
    compact = [None] * TILES
    for m in range(PAIRS):
        above = out3[m] if m < PAIRS - 1 else 0.0
        below = out3[m - 1] if m > 0 else 0.0
        invs = []
        for c in range(2):
            diag = stor3[c, m] + e3[c, m] + row_prev(e3[1 - c, m]) + n3[c, m]
            diag = diag + lane_prev(n3[1 - c, m], 8) + in3[m]
            diag = diag + (jnp.where(odd3, above, below) if c == 0 else jnp.where(odd3, below, above))
            invs.append(1.0 / diag)
            total_f = total_f + src3[c, m][3:7, :LANES]
            total_s = total_s + stor3[c, m][3:7, :LANES]
        values = (
            src3[0, m] * invs[0], src3[1, m] * invs[1], 1.0 - stor3[0, m] * invs[0], invs[0], invs[1],
            e3[0, m], e3[1, m], n3[0, m], n3[1, m], in3[m], out3[m] if m < PAIRS - 1 else jnp.zeros(dims3, jnp.float32),
        )
        for q, value in enumerate(values):
            own = value[3:7, :LANES]
            compact[q] = jnp.where(phase == m, own, 0.0 if m == 0 else compact[q])
    for q in range(TILES):
        tiles[4 * q : 4 * q + 4] = compact[q]
    sums[0:1] = jnp.broadcast_to(jnp.sum(total_f, keepdims=True), (1, LANES)) * 0.125
    sums[1:2] = jnp.broadcast_to(jnp.sum(total_s, keepdims=True), (1, LANES)) * 0.125

    for m in range(PAIRS):
        for c in range(2):
            for to, of in ((source0, src), (inv0, inv), (east0, east), (north0, north)):
                to[c, m] = of[c, m, slice(16, 64)]
            for to, of in ((source1, src1), (inv1, i1), (east1, e1), (north1, n1)):
                to[c, m] = of[c, m, slice(8, 32)]
        first0[m], first1[m] = first[m, slice(16, 64)], f1[m, slice(8, 32)]
        inner0[m], inner1[m] = inner[m, slice(16, 64)], in1[m, slice(8, 32)]
        if m < PAIRS - 1:
            outer0[m], outer1[m] = outer[m, slice(16, 64)], out1[m, slice(8, 32)]


def window_kernel(tiles, from_next, from_pair, window):
    even = (position()[1] & 1) == 0
    window[:, :LANES] = tiles[...]
    a, b = from_pair[...], from_next[...]
    right_first = (iota(a.shape, 1) < LANES // 2) == even
    window[:, LANES:] = jnp.where(right_first, a, b)


def spread_rows(level, low, high, into, m):
    rows = low.shape[0]
    bit = lane_bit(low.shape, level)
    into[m, pl.ds(0, rows, stride=2)] = jnp.where(bit, high, low)
    into[m, pl.ds(1, rows, stride=2)] = jnp.where(bit, low, high)


def join_kernel(mine, sibling, both):
    both[: 4 * TILES] = mine[...]
    both[4 * TILES :] = sibling[...]


def fourth_kernel(
    mine, sibling, received, passed_on, sums_in,
    source0, inv0, first0, east0, north0, inner0, outer0,
    source1, inv1, first1, east1, north1, inner1, outer1,
    source2, inv2, first2, east2, north2, inner2, outer2,
    fields, sums,
    whole, work2, work1, work0a, work0b, va, vb, wa, wb,
    ua2, ub2, ua1, ub1,
):
    source0, inv0, first0, east0, north0, inner0, outer0 = map(Wide, (source0, inv0, first0, east0, north0, inner0, outer0))
    source1, inv1, first1, east1, north1, inner1, outer1 = map(Wide, (source1, inv1, first1, east1, north1, inner1, outer1))
    source2, inv2, first2, east2, north2, inner2, outer2 = map(Wide, (source2, inv2, first2, east2, north2, inner2, outer2))
    work2, work1, work0a, work0b, va, vb, wa, wb = map(Wide, (work2, work1, work0a, work0b, va, vb, wa, wb))
    ua2, ub2, ua1, ub1 = map(Wide, (ua2, ub2, ua1, ub1))
    f32 = jnp.float32
    even = (position()[0] & 1) == 0
    size = 4 * TILES
    own, sib = mine[...], sibling[...]
    direct, relayed = received[...], passed_on[...]
    before, after = jnp.where(even, direct, relayed), jnp.where(even, relayed, direct)
    blocks = (
        before[size:], before[:size], jnp.where(even, own, sib), jnp.where(even, sib, own), after[:size], after[size:],
    )
    for slot, block in enumerate(blocks):
        for q in range(TILES):
            whole[q, 4 * slot : 4 * slot + 4] = block[4 * q : 4 * q + 4]
    own_f, own_s = sums_in[0:1, 0:1], sums_in[1:2, 0:1]
    guess = own_f / own_s
    g0, g1, h0, i30, i31, e30, e31, n30, n31, in3, out3 = [whole[q] for q in range(TILES)]
    inv3, e3, n3 = (i30, i31), (e30, e31), (n30, n31)
    odd3 = odd_cells((24, WIDE), 3)

    def beside3(c, u):
        t = e3[c] * row_next(u) + row_prev(e3[1 - c] * u)
        t = t + (n3[c] * lane_next(u, 8) + lane_prev(n3[1 - c] * u, 8)) + in3 * u
        above, below = out3 * lane_next(u, 1), lane_prev(out3 * u, 1)
        return t + (jnp.where(odd3, above, below) if c == 0 else jnp.where(odd3, below, above))

    a0, b0 = g0 + guess * h0, h0
    for _ in range(3):
        a1, b1 = g1 + beside3(1, a0) * inv3[1], beside3(1, b0) * inv3[1]
        a0, b0 = g0 + beside3(0, a1) * inv3[0], beside3(0, b1) * inv3[0]

    a0, a1, b0, b1 = [jnp.where(even, pltpu.roll(x, 19, 0), pltpu.roll(x, 15, 0))[:16] for x in (a0, a1, b0, b1)]
    dims3 = (16, WIDE)
    phase = iota(dims3, 1) & 7
    odd3 = odd_cells(dims3, 3, 1)
    second_half = lane_bit(dims3, 1)

    def spread(x, m):
        x = jnp.where(phase == 0, near_next(x, m) if m else x, 0.0)
        x = x + near_prev(x, 1)
        x = x + near_prev(x, 2)
        return x + near_prev(x, 4)

    for m in range(PAIRS):
        x0 = jnp.where(second_half, spread(b0, m), spread(a0, m))
        x1 = jnp.where(second_half, spread(b1, m), spread(a1, m))
        low, high = jnp.where(odd3, x1, x0)[:12], jnp.where(odd3, x0, x1)[:12]
        spread_rows(2, low, high, work2, m)

    def smooth(level, rows, coeffs, inverse, source, first, work, ones, zeros, half_bit):
        odd = odd_cells((rows, WIDE), level)
        is_b = lane_bit((rows, WIDE), half_bit)
        step = 1 << level
        for m in range(PAIRS):
            work[m] = work[m] + jnp.where(is_b, 0.0, first[m])
        for m in range(PAIRS):
            ones[m] = (jnp.where(is_b, 0.0, source[1, m]) + beside(1, work, coeffs, m, odd, step)) * inverse[1, m]
        for m in range(PAIRS):
            zeros[m] = jnp.where(is_b, 0.0, first[m]) + beside(0, ones, coeffs, m, odd, step) * inverse[0, m]

    smooth(2, ROWS2, (east2, north2, inner2, outer2), inv2, source2, first2, work2, ub2, ua2, 1)
    dims2 = (ROWS2, WIDE)
    odd2 = odd_cells(dims2, 2)
    bit1, bit0 = lane_bit(dims2, 1), lane_bit(dims2, 0)

    def regroup2(x):
        a = jnp.where(bit1, near_prev(x, 2), x)
        b = jnp.where(bit1, x, near_next(x, 2))
        return jnp.where(bit0, b, a)

    for m in range(PAIRS):
        x0, x1 = regroup2(ua2[m]), regroup2(ub2[m])
        low, high = jnp.where(odd2, x1, x0)[4:16], jnp.where(odd2, x0, x1)[4:16]
        spread_rows(1, low, high, work1, m)

    smooth(1, 24, (east1, north1, inner1, outer1), inv1, source1, first1, work1, ub1, ua1, 0)
    dims1 = (24, WIDE)
    odd1 = odd_cells(dims1, 1)
    bit0 = lane_bit(dims1, 0)
    for m in range(PAIRS):
        x0, x1 = ua1[m], ub1[m]
        low, high = jnp.where(odd1, x1, x0), jnp.where(odd1, x0, x1)
        for work, pick in (
            (work0a, lambda x: jnp.where(bit0, near_prev(x, 1), x)),
            (work0b, lambda x: jnp.where(bit0, x, near_next(x, 1))),
        ):
            spread_rows(0, pick(low), pick(high), work, m)

    rows = 48
    odd = odd_cells((rows, WIDE), 0)
    coeffs = (east0, north0, inner0, outer0)
    for m in range(PAIRS):
        work0a[m] = work0a[m] + first0[m]
    for m in range(PAIRS):
        va[m] = (source0[1, m] + beside(1, work0a, coeffs, m, odd, 1)) * inv0[1, m]
        vb[m] = beside(1, work0b, coeffs, m, odd, 1) * inv0[1, m]
    for m in range(PAIRS):
        wa[m] = first0[m] + beside(0, va, coeffs, m, odd, 1) * inv0[0, m]
        wb[m] = beside(0, vb, coeffs, m, odd, 1) * inv0[0, m]
    for m in range(PAIRS):
        work0a[m] = work0a[m] - wa[m]
        work0b[m] = work0b[m] - wb[m]
    acc = [jnp.zeros((ROWS, LANES), f32)] * 11

    def own(x):
        return x[8 : 8 + ROWS, :LANES]

    for m in range(PAIRS):
        change_a = own(beside(1, work0a, coeffs, m, odd, 1))
        img_b = own(beside(1, work0b, coeffs, m, odd, 1))
        r0, r1 = own(source0[0, m]), own(source0[1, m])
        p0, p1, q0, q1 = own(wa[m]), own(va[m]), own(wb[m]), own(vb[m])
        img_a = r1 + change_a
        d = -change_a
        terms = (
            r0 * p0 + r1 * p1, r0 * q0 + r1 * q1,
            r0 * p0 + img_a * p1, r0 * q0 + img_a * q1 + img_b * p1, img_b * q1,
            d * d, d * img_a, img_a * img_a + r0 * r0, d * img_b, img_a * img_b, img_b * img_b,
        )
        acc = [x + y for x, y in zip(acc, terms, strict=True)]
        for t, x in enumerate((p0, p1, q0, q1, r0, r1, img_a, img_b)):
            fields[t, m] = x
    lane = iota((1, LANES), 1)
    line = jnp.zeros((1, LANES), f32)
    for q, x in enumerate(acc):
        line = jnp.where(lane == q, jnp.sum(x, keepdims=True), line)
    line = jnp.where(lane == 11, own_f, line)
    line = jnp.where(lane == 12, own_s, line)
    line = jnp.where(lane == 13, guess, line)
    sums[...] = jnp.broadcast_to(line, sums.shape)


def last_kernel(sums, line, fields, solution_out, residual_out, norm_ref, solution_ref, residual_ref, sems, *, cells):
    wide = jnp.concatenate([sums[...], jnp.zeros((sums.shape[0], LANES - sums.shape[1]), jnp.float32)], axis=1).T
    x = jnp.concatenate([wide[:16], wide[16:32]], axis=1)

    def column(q):
        return x[q : q + 1]

    def total(v):
        return jnp.sum(v, axis=1, keepdims=True)

    rp, rq, pa, pb, qb, dd, da, aa, db, ab, bb = [column(q) for q in range(11)]
    mean = total(column(11)) / total(column(12))
    shift = mean - column(13)
    step = total(rp + shift * rq) / total(pa + shift * (pb + shift * qb))
    s, t = step - 1.0, step * shift
    squares = total(dd - 2.0 * s * da + s * s * aa - 2.0 * t * db + 2.0 * s * t * ab + t * t * bb)
    norm_ref[...] = jnp.sqrt(jnp.maximum(squares, 0.0) / cells)
    here = mean - line[0:1, 13:14]
    odd = odd_cells((ROWS, LANES), 0)
    copies = []
    for m in range(PAIRS):
        p0, p1, q0, q1, r0, r1, img_a, img_b = [fields[t, m] for t in range(8)]
        s0, s1 = step * (p0 + here * q0), step * (p1 + here * q1)
        n0, n1 = r0 - step * r0, r1 - step * (img_a + here * img_b)
        solution_ref[2 * m] = jnp.where(odd, s1, s0)
        solution_ref[2 * m + 1] = jnp.where(odd, s0, s1)
        residual_ref[2 * m] = jnp.where(odd, n1, n0)
        residual_ref[2 * m + 1] = jnp.where(odd, n0, n1)
        layers = pl.ds(2 * m, 2)
        for q, (ref, out) in enumerate(((solution_ref, solution_out), (residual_ref, residual_out))):
            copies.append(pltpu.make_async_copy(ref.at[layers], out.at[layers], sems.at[q, m]))
            copies[-1].start()
    for copy in copies:
        copy.wait()


def level_dims(rows):
    two, one, four = [(*lead, 2, rows, LANES) for lead in ((2, PAIRS), (PAIRS,), (PAIRS - 1,))]
    return two, one, four


def level_shapes(rows):
    two, one, four = [shape(*dims) for dims in level_dims(rows)]
    return two, two, one, two, two, one, four


def scratch(*dims):
    return pltpu.VMEM(dims, jnp.float32)


def pairs_of(count, first):
    return [(i, i + 1) for i in range(first, count - 1, 2)] + [(i + 1, i) for i in range(first, count - 1, 2)]


def pair_exchange(x, axis):
    count = lax.axis_size(axis)
    return [lax.ppermute(x_i, axis, pairs_of(count, first)) for first, x_i in enumerate(x)]


def shards(pressure, soil, vg_alpha, vg_n, sat_cond, storage, right_side):
    count_x, count_y = lax.axis_size("gx"), lax.axis_size("gy")
    block, slab = scratch(2 * PAIRS, ROWS, LANES), shape(6 * PAIRS, HALO, LANES)
    side, corner = shape(6, ROWS, LANES), shape(12, HALO, LANES)
    arguments = (pressure, soil, storage, right_side, *[v.reshape(1, NSOIL) for v in (vg_alpha, vg_n, sat_cond)])
    packed, *sides = pl.pallas_call(
        first_kernel, out_shape=(shape(6 * PAIRS, ROWS, LANES), side, side),
        in_specs=[HBM] * 7, out_specs=(VM,) * 3,
        scratch_shapes=[
            block, pltpu.VMEM((2 * PAIRS, ROWS, LANES), jnp.int32), block, block, scratch(3, 1, NSOIL), pltpu.SemaphoreType.DMA((7,)),
        ],
        compiler_params=params(4), name="conductivity",
    )(*[pltpu.with_memory_space_constraint(v, pltpu.MemorySpace.HBM) for v in arguments])
    beside_y = pair_exchange(sides, "gy")
    slabs = pl.pallas_call(
        edge_kernel, out_shape=(slab, slab), in_specs=[VM], out_specs=(VM, VM), compiler_params=params(2), name="edges",
    )(packed)
    halos = pair_exchange(slabs, "gx") + beside_y
    corners = pl.pallas_call(
        second_kernel, out_shape=(corner, corner), in_specs=[VM, VM], out_specs=(VM, VM), compiler_params=params(2), name="corners",
    )(*beside_y[::-1])
    halos = pair_exchange(corners, "gx") + beside_y[::-1] + halos[:2]

    def sized(rows):
        return [scratch(*dims) for dims in level_dims(rows)]

    two, one, four = sized(EXT)
    two1, one1, four1 = sized(ROWS1)
    two2, one2, _ = sized(ROWS2)
    two3, one3, four3 = sized(16)
    out = pl.pallas_call(
        third_kernel,
        out_shape=(*level_shapes(48), *level_shapes(24), *level_shapes(ROWS2), shape(4 * TILES, LANES), shape(8, LANES)),
        in_specs=[VM] * 7, out_specs=(VM,) * 23,
        scratch_shapes=[
            two, two, two, two, two, one, four, two, one, one, one,
            two1, two1, two1, two1, one1, four1, two1, one1, one1, one1,
            two2, one2, one2,
            two3, two3, two3, two3, one3, four3,
        ],
        compiler_params=params(12), name="descent",
    )(packed, *halos)
    levels, tiles, sums = out[:21], out[21], out[22]

    tile_pair, tile_next = pair_exchange((tiles, tiles), "gy")
    window = pl.pallas_call(
        window_kernel, out_shape=shape(4 * TILES, WIDE), in_specs=[VM] * 3, out_specs=VM, compiler_params=params(2), name="window",
    )(tiles, tile_next, tile_pair)
    sibling = lax.ppermute(window, "gx", pairs_of(count_x, 0))
    both = pl.pallas_call(
        join_kernel, out_shape=shape(8 * TILES, WIDE), in_specs=[VM] * 2, out_specs=VM, compiler_params=params(2), name="join",
    )(window, sibling)
    received = lax.ppermute(both, "gx", pairs_of(count_x, 1))
    passed_on = lax.ppermute(received, "gx", pairs_of(count_x, 0))
    blocks = (window, sibling, received, passed_on)

    devices = count_x * count_y
    fields, line = pl.pallas_call(
        fourth_kernel,
        out_shape=(shape(8, PAIRS, ROWS, LANES), shape(8, LANES)),
        in_specs=[VM] * 26, out_specs=(VM, VM),
        scratch_shapes=[
            scratch(TILES, 24, WIDE), sized(ROWS2)[1], sized(24)[1],
            *[sized(48)[1]] * 6, *[sized(24)[1]] * 4,
        ],
        compiler_params=params(8), name="ascent",
    )(*blocks, sums, *levels)
    both = jnp.concatenate([line[:1, :16], lax.ppermute(line, "gx", pairs_of(count_x, 0))[:1, :16]], axis=1)
    kinds = [[x * count_y + y for y in range(count_y) for x in range(c, count_x, 2)][::-1] for c in range(2)]
    both = jnp.broadcast_to(both, (devices // 2, 32))
    every = lax.all_to_all(both, ("gx", "gy"), 0, 0, axis_index_groups=kinds, tiled=True)

    layers = 2 * PAIRS
    out = shape(layers, ROWS, LANES)
    solution_out, residual_out, norm = pl.pallas_call(
        functools.partial(last_kernel, cells=float(layers * ROWS * LANES * devices)),
        out_shape=(out, out, shape(1, 1)), in_specs=[VM, VM, VM], out_specs=(HBM, HBM, VM),
        scratch_shapes=[scratch(*out.shape), scratch(*out.shape), pltpu.SemaphoreType.DMA((2, PAIRS))],
        compiler_params=params(4), name="outputs",
    )(every, line, fields)
    return solution_out, residual_out, norm.reshape(1)


def solution(mesh):
    split, whole = P(None, "gx", "gy"), P()
    return jax.shard_map(
        shards, mesh=mesh, in_specs=(split, split, whole, whole, whole, split, split),
        out_specs=(split, split, whole), check_vma=False,
    )
```

```python
import functools

import jax
import jax.numpy as jnp
from jax import lax
from jax.experimental import pallas as pl
from jax.experimental.pallas import tpu as pltpu
from jax.sharding import PartitionSpec as P

NSOIL = 23
PAIRS = 5
HALO = 24
ROWS, LANES = 32, 128
EXT = ROWS + 2 * HALO
WIDE = 2 * LANES
ROWS1, ROWS2 = EXT // 2, 24
TILES = 11
MIB = 1 << 20


def iota(shape, dim):
    return lax.broadcasted_iota(jnp.int32, shape, dim)


def odd_cells(shape, level, start=0):
    return ((iota(shape, 0) + start + (iota(shape, 1) >> level)) & 1) == 1


def lane_bit(shape, level):
    return ((iota(shape, 1) >> level) & 1) == 1


def row_next(x):
    return pltpu.roll(x, x.shape[0] - 1, 0)


def row_prev(x):
    return pltpu.roll(x, 1, 0)


def lane_next(x, step):
    return pltpu.roll(x, x.shape[1] - step, 1)


def lane_prev(x, step):
    return pltpu.roll(x, step, 1)


def by_halves(f, x):
    return jnp.concatenate([f(x[:, start : start + LANES]) for start in range(0, x.shape[1], LANES)], axis=1)


def near_next(x, step):
    return by_halves(lambda h: lane_next(h, step), x)


def near_prev(x, step):
    return by_halves(lambda h: lane_prev(h, step), x)


def pair_sum(x, level):
    step = 1 << level
    return x + jnp.where(lane_bit(x.shape, level), near_prev(x, step), near_next(x, step))


def beside(c, u, coeffs, m, odd, step):
    east, north, inner, outer = coeffs
    um = u[m]
    t = east[c, m] * row_next(um) + row_prev(east[1 - c, m] * um)
    t = t + (north[c, m] * lane_next(um, step) + lane_prev(north[1 - c, m] * um, step))
    t = t + inner[m] * um
    above = outer[m] * u[m + 1] if m < PAIRS - 1 else 0.0
    below = outer[m - 1] * u[m - 1] if m > 0 else 0.0
    return t + (jnp.where(odd, above, below) if c == 0 else jnp.where(odd, below, above))


def position():
    return lax.axis_index("gx"), lax.axis_index("gy")


def params(limit):
    return pltpu.CompilerParams(vmem_limit_bytes=limit * MIB)


VM = pl.BlockSpec(memory_space=pltpu.VMEM)
HBM = pl.BlockSpec(memory_space=pltpu.MemorySpace.HBM)


def shape(*dims):
    return jax.ShapeDtypeStruct(dims, jnp.float32)


class Wide:
    def __init__(self, ref):
        self.ref, self.lead = ref, len(ref.shape) - 3

    def parts(self, ids):
        ids = ids if isinstance(ids, tuple) else (ids,)
        rows = ids[self.lead] if len(ids) > self.lead else slice(None)
        return [self.ref.at[(*ids[: self.lead], half)] for half in range(2)], rows

    def __getitem__(self, ids):
        refs, rows = self.parts(ids)
        return jnp.concatenate([ref[rows, :] for ref in refs], axis=1)

    def __setitem__(self, ids, x):
        refs, rows = self.parts(ids)
        for half, ref in enumerate(refs):
            ref[rows, :] = x[:, LANES * half : LANES * (half + 1)]


def first_kernel(
    pressure_in, soil_in, storage_in, source_in, alpha_in, power_in, saturated_in, packed, to_pair, to_next,
    pressure, soil, storage, source, table, sems,
):
    copies = [
        pltpu.make_async_copy(alpha_in, table.at[0], sems.at[4]),
        pltpu.make_async_copy(power_in, table.at[1], sems.at[5]),
        pltpu.make_async_copy(saturated_in, table.at[2], sems.at[6]),
        pltpu.make_async_copy(pressure_in, pressure, sems.at[0]),
        pltpu.make_async_copy(soil_in, soil, sems.at[1]),
        pltpu.make_async_copy(storage_in, storage, sems.at[2]),
        pltpu.make_async_copy(source_in, source, sems.at[3]),
    ]
    for copy in copies:
        copy.start()
    even_y = (position()[1] & 1) == 0
    odd = odd_cells((ROWS, LANES), 0)
    lane = iota((ROWS, LANES), 1)
    for copy in copies:
        copy.wait()
    rows = []
    for q in range(3):
        row = jnp.concatenate([table[q], jnp.ones((1, LANES - NSOIL), jnp.float32)], axis=1)
        rows.append(jnp.broadcast_to(jnp.log(row) if q == 0 else row, (8, LANES)))

    def look_up(row, ids):
        parts = [jnp.take_along_axis(row, ids[8 * b : 8 * b + 8], axis=1) for b in range(ROWS // 8)]
        return jnp.concatenate(parts, axis=0)

    def cond_of(k):
        ids = soil[k]
        log_scale, power, saturated = [look_up(r, ids) for r in rows]
        exponent = 1.0 - 1.0 / power
        log_s = power * (log_scale + jnp.log(jnp.abs(pressure[k])))
        log_1s = jnp.log(1.0 + jnp.exp(log_s))
        outer = 1.0 - jnp.exp(exponent * (log_s - log_1s))
        return saturated * jnp.exp(-0.5 * exponent * log_1s) * outer * outer

    def put(tile, m, x):
        t = tile * PAIRS + m
        packed[t] = x
        left = pltpu.roll(x, HALO * m, 1) if m else x
        right = pltpu.roll(x, (HALO * m - (LANES - HALO)) % LANES, 1)
        for ref, y in ((to_pair, jnp.where(even_y, right, left)), (to_next, jnp.where(even_y, left, right))):
            ref[tile] = y if m == 0 else jnp.where(lane >= HALO * m, y, ref[tile])

    for m in range(PAIRS):
        triples = (
            (cond_of(2 * m), cond_of(2 * m + 1)),
            (storage[2 * m], storage[2 * m + 1]),
            (source[2 * m], source[2 * m + 1]),
        )
        for q, (a, b) in enumerate(triples):
            put(2 * q, m, jnp.where(odd, b, a))
            put(2 * q + 1, m, jnp.where(odd, a, b))


def edge_kernel(packed, from_next, from_pair, to_sibling, to_other):
    even = (position()[0] & 1) == 0
    for t in range(6 * PAIRS + 12):
        ref, at = (packed, t) if t < 30 else (from_pair, t - 30) if t < 36 else (from_next, t - 36)
        high, low = ref[at, ROWS - HALO :], ref[at, :HALO]
        to_sibling[t] = jnp.where(even, high, low)
        to_other[t] = jnp.where(even, low, high)


def coarsen_level(level, fine_rows, out_rows, fine, coarse):
    stor, east, north, inner, outer = fine
    cstor, ceast, cnorth, cinner, couter = coarse
    half = fine_rows // 2
    dims = (half, WIDE)
    bit = lane_bit(dims, level)
    odd = odd_cells(dims, level + 1, 1 if level == 2 else 0)
    step = 1 << level

    def even_rows(ref, *ids):
        return ref[(*ids, pl.ds(0, half, stride=2))]

    def odd_rows(ref, *ids):
        return ref[(*ids, pl.ds(1, half, stride=2))]

    swap = bit ^ odd

    def put(ref, m, a, b):
        ref[0, m, slice(0, half)] = a
        ref[1, m, slice(0, half)] = b

    for m in range(PAIRS):
        u = even_rows(stor, 0, m) + odd_rows(stor, 1, m)
        v = even_rows(stor, 1, m) + odd_rows(stor, 0, m)
        put(cstor, m, pair_sum(jnp.where(swap, v, u), level), pair_sum(jnp.where(swap, u, v), level))
        e0, e1 = odd_rows(east, 0, m), odd_rows(east, 1, m)
        put(ceast, m, pair_sum(jnp.where(swap, e0, e1), level), pair_sum(jnp.where(swap, e1, e0), level))
        low = even_rows(north, 1, m) + odd_rows(north, 0, m)
        high = even_rows(north, 0, m) + odd_rows(north, 1, m)
        a, b = jnp.where(odd, high, low), jnp.where(odd, low, high)
        put(cnorth, m, jnp.where(bit, a, near_next(a, step)), jnp.where(bit, b, near_next(b, step)))
        cinner[m, slice(0, half)] = pair_sum(even_rows(inner, m) + odd_rows(inner, m), level)
        if m < PAIRS - 1:
            couter[m, slice(0, half)] = pair_sum(even_rows(outer, m) + odd_rows(outer, m), level)


def restrict_level(level, fine_rows, residual, coarse_source):
    half = fine_rows // 2
    dims = (half, WIDE)
    bit = lane_bit(dims, level)
    odd = odd_cells(dims, level + 1, 1 if level == 2 else 0)
    swap = bit ^ odd
    for m in range(PAIRS):
        a = residual[m, pl.ds(0, half, stride=2)]
        b = residual[m, pl.ds(1, half, stride=2)]
        coarse_source[0, m, slice(0, half)] = pair_sum(jnp.where(swap, b, a), level)
        coarse_source[1, m, slice(0, half)] = pair_sum(jnp.where(swap, a, b), level)


def invert_diagonal(level, rows, coeffs, inverse):
    stor, east, north, inner, outer = coeffs
    odd = odd_cells((rows, WIDE), level)
    step = 1 << level
    for m in range(PAIRS):
        above = outer[m] if m < PAIRS - 1 else 0.0
        below = outer[m - 1] if m > 0 else 0.0
        for c in range(2):
            diag = stor[c, m] + east[c, m] + row_prev(east[1 - c, m]) + north[c, m]
            diag = diag + lane_prev(north[1 - c, m], step) + inner[m]
            diag = diag + (jnp.where(odd, above, below) if c == 0 else jnp.where(odd, below, above))
            inverse[c, m] = 1.0 / diag


def descend_level(level, rows, coeffs, inverse, source, first, second, residual):
    odd = odd_cells((rows, WIDE), level)
    step = 1 << level
    for m in range(PAIRS):
        first[m] = source[0, m] * inverse[0, m]
    for m in range(PAIRS):
        second[m] = (source[1, m] + beside(1, first, coeffs[1:], m, odd, step)) * inverse[1, m]
    for m in range(PAIRS):
        residual[m] = beside(0, second, coeffs[1:], m, odd, step)


def third_kernel(
    packed, from_sibling, from_other, from_next, from_pair,
    source0, inv0, first0, east0, north0, inner0, outer0,
    source1, inv1, first1, east1, north1, inner1, outer1,
    source2, inv2, first2, east2, north2, inner2, outer2,
    tiles, sums,
    cond, stor, src, east, north, inner, outer, inv, first, second, residual,
    stor1, src1, e1, n1, in1, out1, i1, f1, s1, r1,
    stor2, s2, r2,
    stor3, src3, e3, n3, in3, out3,
):
    source0, inv0, first0, east0, north0, inner0, outer0 = map(Wide, (source0, inv0, first0, east0, north0, inner0, outer0))
    source1, inv1, first1, east1, north1, inner1, outer1 = map(Wide, (source1, inv1, first1, east1, north1, inner1, outer1))
    source2, inv2, first2, east2, north2, inner2, outer2 = map(Wide, (source2, inv2, first2, east2, north2, inner2, outer2))
    cond, stor, src, east, north, inner, outer = map(Wide, (cond, stor, src, east, north, inner, outer))
    inv, first, second, residual = map(Wide, (inv, first, second, residual))
    stor1, src1, e1, n1, in1, out1, i1, f1, s1, r1 = map(Wide, (stor1, src1, e1, n1, in1, out1, i1, f1, s1, r1))
    stor2, s2, r2 = map(Wide, (stor2, s2, r2))
    stor3, src3, e3, n3, in3, out3 = map(Wide, (stor3, src3, e3, n3, in3, out3))
    gx, gy = position()
    even_x, even_y = (gx & 1) == 0, (gy & 1) == 0
    lane = iota((EXT, LANES), 1)

    def rows_of(sib, oth, own):
        return jnp.concatenate([jnp.where(even_x, oth, sib), own, jnp.where(even_x, sib, oth)], axis=0)

    for tile in range(6):
        pair, other = [
            rows_of(from_sibling[q + tile], from_other[q + tile], ref[tile]) for q, ref in ((30, from_pair), (36, from_next))
        ]
        right = jnp.where(even_y, pair, other)
        left = jnp.where(even_y, other, pair)
        ref = (cond, stor, src)[tile // 2]
        for m in range(PAIRS):
            t = tile * PAIRS + m
            x = rows_of(from_sibling[t], from_other[t], packed[t])
            r = pltpu.roll(right, (-HALO * m) % LANES, 1) if m else right
            l = pltpu.roll(left, (LANES - HALO - HALO * m) % LANES, 1)
            h = jnp.where(lane < HALO, r, jnp.where(lane >= LANES - HALO, l, 0.0))
            if tile // 2 == 1:
                x, h = jnp.where(x == 0.0, 1.0, x), jnp.where(h == 0.0, 1.0, h)
            ref.ref[tile % 2, m, 0] = x
            ref.ref[tile % 2, m, 1] = h

    dims = (EXT, WIDE)
    odd = odd_cells(dims, 0)
    row, column = iota(dims, 0), iota(dims, 1)
    last_row = (row == HALO + ROWS - 1) & (gx == lax.axis_size("gx") - 1)
    before_row = (row == HALO - 1) & (gx == 0)
    keep_x = jnp.where(last_row | before_row, 0.0, 0.5)
    last_column = (column == LANES - 1) & (gy == lax.axis_size("gy") - 1)
    before_column = (column == WIDE - 1) & (gy == 0)
    keep_y = jnp.where(last_column | before_column, 0.0, 0.5)
    for m in range(PAIRS):
        a, b = cond[0, m], cond[1, m]
        east[0, m] = (a + row_next(b)) * keep_x
        east[1, m] = (b + row_next(a)) * keep_x
        north[0, m] = (a + lane_next(b, 1)) * keep_y
        north[1, m] = (b + lane_next(a, 1)) * keep_y
        inner[m] = a + b
        if m < PAIRS - 1:
            outer[m] = jnp.where(odd, a + cond[1, m + 1], b + cond[0, m + 1])

    level0 = (stor, east, north, inner, outer)
    level1 = (stor1, e1, n1, in1, out1)
    level2 = (stor2, east2, north2, inner2, outer2)
    level3 = (stor3, e3, n3, in3, out3)
    invert_diagonal(0, EXT, level0, inv)
    descend_level(0, EXT, level0, inv, src, first, second, residual)

    coarsen_level(0, EXT, ROWS1, level0, level1)
    restrict_level(0, EXT, residual, src1)
    invert_diagonal(1, ROWS1, level1, i1)
    descend_level(1, ROWS1, level1, i1, src1, f1, s1, r1)

    half = ROWS1 // 2
    for ref in (source2, east2, north2, inner2, outer2):
        ref.ref[..., half:, :] = jnp.zeros((*ref.ref.shape[:-2], ROWS2 - half, LANES), jnp.float32)
    stor2.ref[..., half:, :] = jnp.ones((2, PAIRS, 2, ROWS2 - half, LANES), jnp.float32)
    coarsen_level(1, ROWS1, ROWS2, level1, level2)
    restrict_level(1, ROWS1, r1, source2)
    invert_diagonal(2, ROWS2, level2, inv2)
    descend_level(2, ROWS2, level2, inv2, source2, first2, s2, r2)

    coarsen_level(2, ROWS2, 16, level2, level3)
    restrict_level(2, ROWS2, r2, src3)

    dims3 = (16, WIDE)
    odd3 = odd_cells(dims3, 3, 1)
    phase = iota((4, LANES), 1) & 7
    total_f, total_s = 0.0, 0.0
    compact = [None] * TILES
    for m in range(PAIRS):
        above = out3[m] if m < PAIRS - 1 else 0.0
        below = out3[m - 1] if m > 0 else 0.0
        invs = []
        for c in range(2):
            diag = stor3[c, m] + e3[c, m] + row_prev(e3[1 - c, m]) + n3[c, m]
            diag = diag + lane_prev(n3[1 - c, m], 8) + in3[m]
            diag = diag + (jnp.where(odd3, above, below) if c == 0 else jnp.where(odd3, below, above))
            invs.append(1.0 / diag)
            total_f = total_f + src3[c, m][3:7, :LANES]
            total_s = total_s + stor3[c, m][3:7, :LANES]
        values = (
            src3[0, m] * invs[0], src3[1, m] * invs[1], 1.0 - stor3[0, m] * invs[0], invs[0], invs[1],
            e3[0, m], e3[1, m], n3[0, m], n3[1, m], in3[m], out3[m] if m < PAIRS - 1 else jnp.zeros(dims3, jnp.float32),
        )
        for q, value in enumerate(values):
            own = value[3:7, :LANES]
            compact[q] = jnp.where(phase == m, own, 0.0 if m == 0 else compact[q])
    for q in range(TILES):
        tiles[4 * q : 4 * q + 4] = compact[q]
    sums[0:1] = jnp.broadcast_to(jnp.sum(total_f, keepdims=True), (1, LANES)) * 0.125
    sums[1:2] = jnp.broadcast_to(jnp.sum(total_s, keepdims=True), (1, LANES)) * 0.125

    for m in range(PAIRS):
        for c in range(2):
            for to, of in ((source0, src), (inv0, inv), (east0, east), (north0, north)):
                to[c, m] = of[c, m, slice(16, 64)]
            for to, of in ((source1, src1), (inv1, i1), (east1, e1), (north1, n1)):
                to[c, m] = of[c, m, slice(8, 32)]
        first0[m], first1[m] = first[m, slice(16, 64)], f1[m, slice(8, 32)]
        inner0[m], inner1[m] = inner[m, slice(16, 64)], in1[m, slice(8, 32)]
        if m < PAIRS - 1:
            outer0[m], outer1[m] = outer[m, slice(16, 64)], out1[m, slice(8, 32)]


def window_kernel(tiles, from_pair, from_next, window):
    even = (position()[1] & 1) == 0
    window[:, :LANES] = tiles[...]
    a, b = from_pair[...], from_next[...]
    right_first = (iota(a.shape, 1) < LANES // 2) == even
    window[:, LANES:] = jnp.where(right_first, a, b)


def spread_rows(level, low, high, into, m):
    rows = low.shape[0]
    bit = lane_bit(low.shape, level)
    into[m, pl.ds(0, rows, stride=2)] = jnp.where(bit, high, low)
    into[m, pl.ds(1, rows, stride=2)] = jnp.where(bit, low, high)


def join_kernel(mine, sibling, both):
    both[: 4 * TILES] = mine[...]
    both[4 * TILES :] = sibling[...]


def fourth_kernel(
    mine, sibling, received, passed_on, sums_in,
    source0, inv0, first0, east0, north0, inner0, outer0,
    source1, inv1, first1, east1, north1, inner1, outer1,
    source2, inv2, first2, east2, north2, inner2, outer2,
    fields, sums,
    whole, work2, work1, work0a, work0b, va, vb, wa, wb,
    ua2, ub2, ua1, ub1,
):
    source0, inv0, first0, east0, north0, inner0, outer0 = map(Wide, (source0, inv0, first0, east0, north0, inner0, outer0))
    source1, inv1, first1, east1, north1, inner1, outer1 = map(Wide, (source1, inv1, first1, east1, north1, inner1, outer1))
    source2, inv2, first2, east2, north2, inner2, outer2 = map(Wide, (source2, inv2, first2, east2, north2, inner2, outer2))
    work2, work1, work0a, work0b, va, vb, wa, wb = map(Wide, (work2, work1, work0a, work0b, va, vb, wa, wb))
    ua2, ub2, ua1, ub1 = map(Wide, (ua2, ub2, ua1, ub1))
    f32 = jnp.float32
    even = (position()[0] & 1) == 0
    size = 4 * TILES
    own, sib = mine[...], sibling[...]
    direct, relayed = received[...], passed_on[...]
    before, after = jnp.where(even, direct, relayed), jnp.where(even, relayed, direct)
    blocks = (
        before[size:], before[:size], jnp.where(even, own, sib), jnp.where(even, sib, own), after[:size], after[size:],
    )
    for slot, block in enumerate(blocks):
        for q in range(TILES):
            whole[q, 4 * slot : 4 * slot + 4] = block[4 * q : 4 * q + 4]
    own_f, own_s = sums_in[0:1, 0:1], sums_in[1:2, 0:1]
    guess = own_f / own_s
    g0, g1, h0, i30, i31, e30, e31, n30, n31, in3, out3 = [whole[q] for q in range(TILES)]
    inv3, e3, n3 = (i30, i31), (e30, e31), (n30, n31)
    odd3 = odd_cells((24, WIDE), 3)

    def beside3(c, u):
        t = e3[c] * row_next(u) + row_prev(e3[1 - c] * u)
        t = t + (n3[c] * lane_next(u, 8) + lane_prev(n3[1 - c] * u, 8)) + in3 * u
        above, below = out3 * lane_next(u, 1), lane_prev(out3 * u, 1)
        return t + (jnp.where(odd3, above, below) if c == 0 else jnp.where(odd3, below, above))

    a0, b0 = g0 + guess * h0, h0
    for _ in range(3):
        a1, b1 = g1 + beside3(1, a0) * inv3[1], beside3(1, b0) * inv3[1]
        a0, b0 = g0 + beside3(0, a1) * inv3[0], beside3(0, b1) * inv3[0]

    a0, a1, b0, b1 = [jnp.where(even, pltpu.roll(x, 19, 0), pltpu.roll(x, 15, 0))[:16] for x in (a0, a1, b0, b1)]
    dims3 = (16, WIDE)
    phase = iota(dims3, 1) & 7
    odd3 = odd_cells(dims3, 3, 1)
    second_half = lane_bit(dims3, 1)

    def spread(x, m):
        x = jnp.where(phase == 0, near_next(x, m) if m else x, 0.0)
        x = x + near_prev(x, 1)
        x = x + near_prev(x, 2)
        return x + near_prev(x, 4)

    for m in range(PAIRS):
        x0 = jnp.where(second_half, spread(b0, m), spread(a0, m))
        x1 = jnp.where(second_half, spread(b1, m), spread(a1, m))
        low, high = jnp.where(odd3, x1, x0)[:12], jnp.where(odd3, x0, x1)[:12]
        spread_rows(2, low, high, work2, m)

    def smooth(level, rows, coeffs, inverse, source, first, work, ones, zeros, half_bit):
        odd = odd_cells((rows, WIDE), level)
        is_b = lane_bit((rows, WIDE), half_bit)
        step = 1 << level
        for m in range(PAIRS):
            work[m] = work[m] + jnp.where(is_b, 0.0, first[m])
        for m in range(PAIRS):
            ones[m] = (jnp.where(is_b, 0.0, source[1, m]) + beside(1, work, coeffs, m, odd, step)) * inverse[1, m]
        for m in range(PAIRS):
            zeros[m] = jnp.where(is_b, 0.0, first[m]) + beside(0, ones, coeffs, m, odd, step) * inverse[0, m]

    smooth(2, ROWS2, (east2, north2, inner2, outer2), inv2, source2, first2, work2, ub2, ua2, 1)
    dims2 = (ROWS2, WIDE)
    odd2 = odd_cells(dims2, 2)
    bit1, bit0 = lane_bit(dims2, 1), lane_bit(dims2, 0)

    def regroup2(x):
        a = jnp.where(bit1, near_prev(x, 2), x)
        b = jnp.where(bit1, x, near_next(x, 2))
        return jnp.where(bit0, b, a)

    for m in range(PAIRS):
        x0, x1 = regroup2(ua2[m]), regroup2(ub2[m])
        low, high = jnp.where(odd2, x1, x0)[4:16], jnp.where(odd2, x0, x1)[4:16]
        spread_rows(1, low, high, work1, m)

    smooth(1, 24, (east1, north1, inner1, outer1), inv1, source1, first1, work1, ub1, ua1, 0)
    dims1 = (24, WIDE)
    odd1 = odd_cells(dims1, 1)
    bit0 = lane_bit(dims1, 0)
    for m in range(PAIRS):
        x0, x1 = ua1[m], ub1[m]
        low, high = jnp.where(odd1, x1, x0), jnp.where(odd1, x0, x1)
        for work, pick in (
            (work0a, lambda x: jnp.where(bit0, near_prev(x, 1), x)),
            (work0b, lambda x: jnp.where(bit0, x, near_next(x, 1))),
        ):
            spread_rows(0, pick(low), pick(high), work, m)

    rows = 48
    odd = odd_cells((rows, WIDE), 0)
    coeffs = (east0, north0, inner0, outer0)
    for m in range(PAIRS):
        work0a[m] = work0a[m] + first0[m]
    for m in range(PAIRS):
        va[m] = (source0[1, m] + beside(1, work0a, coeffs, m, odd, 1)) * inv0[1, m]
        vb[m] = beside(1, work0b, coeffs, m, odd, 1) * inv0[1, m]
    for m in range(PAIRS):
        wa[m] = first0[m] + beside(0, va, coeffs, m, odd, 1) * inv0[0, m]
        wb[m] = beside(0, vb, coeffs, m, odd, 1) * inv0[0, m]
    for m in range(PAIRS):
        work0a[m] = work0a[m] - wa[m]
        work0b[m] = work0b[m] - wb[m]
    acc = [jnp.zeros((ROWS, LANES), f32)] * 11

    def own(x):
        return x[8 : 8 + ROWS, :LANES]

    for m in range(PAIRS):
        change_a = own(beside(1, work0a, coeffs, m, odd, 1))
        img_b = own(beside(1, work0b, coeffs, m, odd, 1))
        r0, r1 = own(source0[0, m]), own(source0[1, m])
        p0, p1, q0, q1 = own(wa[m]), own(va[m]), own(wb[m]), own(vb[m])
        img_a = r1 + change_a
        d = -change_a
        terms = (
            r0 * p0 + r1 * p1, r0 * q0 + r1 * q1,
            r0 * p0 + img_a * p1, r0 * q0 + img_a * q1 + img_b * p1, img_b * q1,
            d * d, d * img_a, img_a * img_a + r0 * r0, d * img_b, img_a * img_b, img_b * img_b,
        )
        acc = [x + y for x, y in zip(acc, terms, strict=True)]
        for t, x in enumerate((p0, p1, q0, q1, r0, r1, img_a, img_b)):
            fields[t, m] = x
    lane = iota((1, LANES), 1)
    line = jnp.zeros((1, LANES), f32)
    for q, x in enumerate(acc):
        line = jnp.where(lane == q, jnp.sum(x, keepdims=True), line)
    line = jnp.where(lane == 11, own_f, line)
    line = jnp.where(lane == 12, own_s, line)
    line = jnp.where(lane == 13, guess, line)
    sums[...] = jnp.broadcast_to(line, sums.shape)


def last_kernel(sums, line, fields, solution_out, residual_out, norm_ref, solution_ref, residual_ref, sems, *, cells):
    wide = jnp.concatenate([sums[...], jnp.zeros((sums.shape[0], LANES - sums.shape[1]), jnp.float32)], axis=1).T
    x = jnp.concatenate([wide[:16], wide[16:32]], axis=1)

    def column(q):
        return x[q : q + 1]

    def total(v):
        return jnp.sum(v, axis=1, keepdims=True)

    rp, rq, pa, pb, qb, dd, da, aa, db, ab, bb = [column(q) for q in range(11)]
    mean = total(column(11)) / total(column(12))
    shift = mean - column(13)
    step = total(rp + shift * rq) / total(pa + shift * (pb + shift * qb))
    s, t = step - 1.0, step * shift
    squares = total(dd - 2.0 * s * da + s * s * aa - 2.0 * t * db + 2.0 * s * t * ab + t * t * bb)
    norm_ref[...] = jnp.sqrt(jnp.maximum(squares, 0.0) / cells)
    here = mean - line[0:1, 13:14]
    odd = odd_cells((ROWS, LANES), 0)
    copies = []
    for m in range(PAIRS):
        p0, p1, q0, q1, r0, r1, img_a, img_b = [fields[t, m] for t in range(8)]
        s0, s1 = step * (p0 + here * q0), step * (p1 + here * q1)
        n0, n1 = r0 - step * r0, r1 - step * (img_a + here * img_b)
        solution_ref[2 * m] = jnp.where(odd, s1, s0)
        solution_ref[2 * m + 1] = jnp.where(odd, s0, s1)
        residual_ref[2 * m] = jnp.where(odd, n1, n0)
        residual_ref[2 * m + 1] = jnp.where(odd, n0, n1)
        layers = pl.ds(2 * m, 2)
        for q, (ref, out) in enumerate(((solution_ref, solution_out), (residual_ref, residual_out))):
            copies.append(pltpu.make_async_copy(ref.at[layers], out.at[layers], sems.at[q, m]))
            copies[-1].start()
    for copy in copies:
        copy.wait()


def level_dims(rows):
    two, one, four = [(*lead, 2, rows, LANES) for lead in ((2, PAIRS), (PAIRS,), (PAIRS - 1,))]
    return two, one, four


def level_shapes(rows):
    two, one, four = [shape(*dims) for dims in level_dims(rows)]
    return two, two, one, two, two, one, four


def scratch(*dims):
    return pltpu.VMEM(dims, jnp.float32)


def pairs_of(count, first):
    return [(i, i + 1) for i in range(first, count - 1, 2)] + [(i + 1, i) for i in range(first, count - 1, 2)]


def pair_exchange(x, axis):
    count = lax.axis_size(axis)
    return [lax.ppermute(x_i, axis, pairs_of(count, first)) for first, x_i in enumerate(x)]


def shards(pressure, soil, vg_alpha, vg_n, sat_cond, storage, right_side):
    count_x, count_y = lax.axis_size("gx"), lax.axis_size("gy")
    block = scratch(2 * PAIRS, ROWS, LANES)
    side = shape(6, ROWS, LANES)
    arguments = (pressure, soil, storage, right_side, *[v.reshape(1, NSOIL) for v in (vg_alpha, vg_n, sat_cond)])
    packed, *sides = pl.pallas_call(
        first_kernel, out_shape=(shape(6 * PAIRS, ROWS, LANES), side, side),
        in_specs=[HBM] * 7, out_specs=(VM,) * 3,
        scratch_shapes=[
            block, pltpu.VMEM((2 * PAIRS, ROWS, LANES), jnp.int32), block, block, scratch(3, 1, NSOIL), pltpu.SemaphoreType.DMA((7,)),
        ],
        compiler_params=params(4), name="conductivity",
    )(*[pltpu.with_memory_space_constraint(v, pltpu.MemorySpace.HBM) for v in arguments])
    beside_y = pair_exchange(sides, "gy")
    slab = shape(6 * PAIRS + 12, HALO, LANES)
    slabs = pl.pallas_call(
        edge_kernel, out_shape=(slab, slab), in_specs=[VM] * 3, out_specs=(VM, VM), compiler_params=params(2), name="edges",
    )(packed, *beside_y[::-1])
    halos = pair_exchange(slabs, "gx") + beside_y[::-1]

    def sized(rows):
        return [scratch(*dims) for dims in level_dims(rows)]

    two, one, four = sized(EXT)
    two1, one1, four1 = sized(ROWS1)
    two2, one2, _ = sized(ROWS2)
    two3, one3, four3 = sized(16)
    out = pl.pallas_call(
        third_kernel,
        out_shape=(*level_shapes(48), *level_shapes(24), *level_shapes(ROWS2), shape(4 * TILES, LANES), shape(8, LANES)),
        in_specs=[VM] * 5, out_specs=(VM,) * 23,
        scratch_shapes=[
            two, two, two, two, two, one, four, two, one, one, one,
            two1, two1, two1, two1, one1, four1, two1, one1, one1, one1,
            two2, one2, one2,
            two3, two3, two3, two3, one3, four3,
        ],
        compiler_params=params(12), name="descent",
    )(packed, *halos)
    levels, tiles, sums = out[:21], out[21], out[22]

    tile_pair, tile_next = pair_exchange((tiles, tiles), "gy")
    window = pl.pallas_call(
        window_kernel, out_shape=shape(4 * TILES, WIDE), in_specs=[VM] * 3, out_specs=VM, compiler_params=params(2), name="window",
    )(tiles, tile_pair, tile_next)
    sibling = lax.ppermute(window, "gx", pairs_of(count_x, 0))
    both = pl.pallas_call(
        join_kernel, out_shape=shape(8 * TILES, WIDE), in_specs=[VM] * 2, out_specs=VM, compiler_params=params(2), name="join",
    )(window, sibling)
    received = lax.ppermute(both, "gx", pairs_of(count_x, 1))
    passed_on = lax.ppermute(received, "gx", pairs_of(count_x, 0))
    blocks = (window, sibling, received, passed_on)

    devices = count_x * count_y
    fields, line = pl.pallas_call(
        fourth_kernel,
        out_shape=(shape(8, PAIRS, ROWS, LANES), shape(8, LANES)),
        in_specs=[VM] * 26, out_specs=(VM, VM),
        scratch_shapes=[
            scratch(TILES, 24, WIDE), sized(ROWS2)[1], sized(24)[1],
            *[sized(48)[1]] * 6, *[sized(24)[1]] * 4,
        ],
        compiler_params=params(8), name="ascent",
    )(*blocks, sums, *levels)
    both = jnp.concatenate([line[:1, :16], lax.ppermute(line, "gx", pairs_of(count_x, 0))[:1, :16]], axis=1)
    kinds = [[x * count_y + y for y in range(count_y) for x in range(c, count_x, 2)][::-1] for c in range(2)]
    both = jnp.broadcast_to(both, (devices // 2, 32))
    every = lax.all_to_all(both, ("gx", "gy"), 0, 0, axis_index_groups=kinds, tiled=True)

    layers = 2 * PAIRS
    out = shape(layers, ROWS, LANES)
    solution_out, residual_out, norm = pl.pallas_call(
        functools.partial(last_kernel, cells=float(layers * ROWS * LANES * devices)),
        out_shape=(out, out, shape(1, 1)), in_specs=[VM, VM, VM], out_specs=(HBM, HBM, VM),
        scratch_shapes=[scratch(*out.shape), scratch(*out.shape), pltpu.SemaphoreType.DMA((2, PAIRS))],
        compiler_params=params(4), name="outputs",
    )(every, line, fields)
    return solution_out, residual_out, norm.reshape(1)


def solution(mesh):
    split, whole = P(None, "gx", "gy"), P()
    return jax.shard_map(
        shards, mesh=mesh, in_specs=(split, split, whole, whole, whole, split, split),
        out_specs=(split, split, whole), check_vma=False,
    )
```
